256 devices in a mesh: azim: 16 (over y_lo, z), block: 16 (over x, y_hi, core).
Axes of the slice: x: 4, y: 4 (y_hi: 2, y_lo: 2; y = y_hi * 2 + y_lo), z: 8, core: 2. Of those that a mesh axis runs over, the one named last changes fastest.
Arguments:
- flow_state: float32 [16, 5, 64, 16, 2048], P('block', None, None, None, 'azim'), may hold values from -6 to 6
- jacobians: float32 [2, 3, 5, 5], replicated, may hold values from -2.5 to 2.5
- interp_weights: float32 [2, 2, 16, 16], replicated, may hold values from -1.5 to 1.5
- offsets: int32 [2], replicated, may hold values from 0 to 2047
- live_rows: int32 [16], P('block'), may hold values from 8 to 16
Outputs:
- advanced: float32 [16, 5, 64, 16, 2048], P('block', None, None, None, 'azim')
The draws below stay inside these ranges and needn't reach their ends.
All inputs are finite; a program needn't handle non-finite values.
Results may differ from the reference program's by a relative error of at most 0.0003.
Values sent between devices are 32-bit elements; how exact they have to be, the bound alone decides.
No kernel may reach another device: no remote copies, remote signals or barrier semaphores. Data moves between devices by JAX's collectives and lax.ppermute only.
A program may use at most 128 MiB of HBM per device.

```python
import jax
import jax.numpy as jnp
import numpy as np
from jax import lax

VARS = 5
NODES = 64
FACE_NODES = 16
SECTIONS = 2
SPAN_ROWS = 16
BLOCKS = 16
CYCLE = 2048


def place_ends(entries, key, low, largest):
    place = [jax.random.randint(jax.random.fold_in(key, axis), (), 0, length) for axis, length in enumerate(entries.shape)]
    longest = entries.shape.index(max(entries.shape))
    next_to = place[:longest] + [(place[longest] + 1) % entries.shape[longest]] + place[longest + 1:]
    return entries.at[tuple(place)].set(low).at[tuple(next_to)].set(largest)


def levels(stream_key, extent, split, smallest, largest):
    level = 1.0
    for dim, blocks in split:
        steps = jax.random.uniform(jax.random.fold_in(jax.random.fold_in(stream_key, 6), dim), (blocks,), jnp.float32, smallest / len(split), largest / len(split))
        level = level * jnp.repeat(jnp.exp(steps), extent[dim] // blocks).reshape((-1,) + (1,) * (len(extent) - 1 - dim))
    return level


def scatter_about(stream_key, dims, deviation, reach, shards=(), held_as=jnp.bfloat16):
    values = jax.random.normal(stream_key, dims, jnp.float32) * deviation
    if len(shards) > 0:
        values = levels(stream_key, dims, shards, -0.22, 0.18) * values
    return jnp.clip(values, min=-reach, max=reach).astype(held_as)


def setup_inputs(seed: int = 0) -> dict:
    key_list = jax.random.split(jax.random.key(seed), 6)
    return {
        "flow_state": scatter_about(key_list[0], (BLOCKS, VARS, NODES, SPAN_ROWS, CYCLE), 1.0, 6.0, ((0, 16), (4, 16)), jnp.float32),
        "jacobians": scatter_about(key_list[1], (2, 3, VARS, VARS), VARS ** -0.5, 2.5, (), jnp.float32),
        "interp_weights": scatter_about(key_list[2], (SECTIONS, 2, FACE_NODES, FACE_NODES), FACE_NODES ** -0.5, 1.5, (), jnp.float32),
        "offsets": jax.random.randint(key_list[3], (SECTIONS,), 0, CYCLE).astype(jnp.int32),
        "live_rows": place_ends(jax.random.randint(key_list[4], (BLOCKS,), SPAN_ROWS // 2, SPAN_ROWS + 1), jax.random.fold_in(key_list[4], 1), SPAN_ROWS // 2, SPAN_ROWS).astype(jnp.int32),
    }


step_size = 0.04
highest = lax.Precision.HIGHEST

def derivative_matrix():
    points = np.array([-1.0, -1.0 / np.sqrt(5.0), 1.0 / np.sqrt(5.0), 1.0])
    differ = points[:, None] - points[None, :]
    filled = differ + np.eye(4)
    weights = 1.0 / np.prod(filled, axis=1)
    matrix = weights[None, :] / weights[:, None] / filled
    matrix = matrix * (1.0 - np.eye(4))
    matrix = matrix - np.eye(4) * matrix.sum(axis=1)[:, None]
    return jnp.asarray(matrix, jnp.float32)

def mix_vars(matrix, field):
    return jnp.einsum('wv,v...->w...', matrix, field, precision=highest)

def mix_nodes(matrix, field):
    return jnp.einsum('nm,vm...->vn...', matrix, field, precision=highest)

def element_rate(nodal_grid, jacobian, ext_west, ext_east, ext_front, ext_back, live_count):
    derivative = derivative_matrix()
    along_theta = jnp.einsum('ab,vbjkse->vajkse', derivative, nodal_grid, precision=highest)
    along_span = jnp.einsum('ab,vibkse->viakse', derivative, nodal_grid, precision=highest)
    along_axis = jnp.einsum('ab,vijbse->vijase', derivative, nodal_grid, precision=highest)
    tendency = -(mix_vars(jacobian[0], along_theta) + mix_vars(jacobian[1], along_span) + mix_vars(jacobian[2], along_axis))
    bounds = lax.optimization_barrier(jnp.max(lax.optimization_barrier(jnp.sum(jnp.abs(jacobian), axis=2)), axis=1))
    identity = jnp.eye(jacobian.shape[1], dtype=jnp.float32)

    def penalty(direction, orientation):
        return 3.0 * (orientation * jacobian[direction] - bounds[direction] * identity)
    west_face = nodal_grid[:, 0]
    east_face = nodal_grid[:, 3]
    tendency = tendency.at[:, 0].add(mix_vars(penalty(0, -1.0), west_face - ext_west))
    tendency = tendency.at[:, 3].add(mix_vars(penalty(0, 1.0), east_face - ext_east))
    lower_face = nodal_grid[:, :, 0]
    upper_face = nodal_grid[:, :, 3]
    below_face = jnp.concatenate([lower_face[:, :, :, :1], upper_face[:, :, :, :-1]], axis=3)
    above_face = jnp.concatenate([lower_face[:, :, :, 1:], upper_face[:, :, :, -1:]], axis=3)
    tendency = tendency.at[:, :, 0].add(mix_vars(penalty(1, -1.0), lower_face - below_face))
    tendency = tendency.at[:, :, 3].add(mix_vars(penalty(1, 1.0), upper_face - above_face))
    front_face = nodal_grid[:, :, :, 0]
    back_face = nodal_grid[:, :, :, 3]
    tendency = tendency.at[:, :, :, 0].add(mix_vars(penalty(2, -1.0), front_face - ext_front))
    tendency = tendency.at[:, :, :, 3].add(mix_vars(penalty(2, 1.0), back_face - ext_back))
    span_index = jnp.arange(nodal_grid.shape[4], dtype=jnp.int32)
    live_mask = (span_index < live_count).astype(jnp.float32)
    return tendency * live_mask[:, None]

def section_rate(flow_state, jacobians, interp_pair, offset, live_rows):
    block_count = flow_state.shape[0]
    half_point = block_count // 2
    span_rows = flow_state.shape[3]
    cycle_cells = flow_state.shape[4]
    vars_count = flow_state.shape[1]
    nodal_grid = flow_state.reshape(block_count, vars_count, 4, 4, 4, span_rows, cycle_cells)
    west_face = nodal_grid[:, :, 0]
    east_face = nodal_grid[:, :, 3]
    ext_west = jnp.roll(east_face, 1, axis=-1)
    ext_east = jnp.roll(west_face, -1, axis=-1)
    front_face = nodal_grid[:, :, :, :, 0]
    back_face = nodal_grid[:, :, :, :, 3]
    zero_face = jnp.zeros_like(back_face[:1])
    ext_front = jnp.concatenate([zero_face, back_face[:-1]], axis=0)
    ext_back = jnp.concatenate([front_face[1:], zero_face], axis=0)
    rotor_panel = back_face[half_point - 1].reshape(vars_count, 16, span_rows, cycle_cells)
    stator_panel = front_face[half_point].reshape(vars_count, 16, span_rows, cycle_cells)
    rotor_near = jnp.roll(rotor_panel, offset, axis=-1)
    rotor_far = jnp.roll(rotor_panel, offset + 1, axis=-1)
    into_stator = mix_nodes(interp_pair[0], rotor_near) + mix_nodes(interp_pair[1], rotor_far)
    stator_near = jnp.roll(stator_panel, -offset, axis=-1)
    stator_far = jnp.roll(stator_panel, -(offset + 1), axis=-1)
    into_rotor = mix_nodes(interp_pair[0].T, stator_near) + mix_nodes(interp_pair[1].T, stator_far)
    ext_front = ext_front.at[half_point].set(into_stator.reshape(vars_count, 4, 4, span_rows, cycle_cells))
    ext_back = ext_back.at[half_point - 1].set(into_rotor.reshape(vars_count, 4, 4, span_rows, cycle_cells))
    layer_index = jnp.arange(block_count, dtype=jnp.int32)

    def one_block(block_items):
        grid_one, west_one, east_one, front_one, back_one, live_one, index_one = block_items
        jacobian = jnp.where(index_one < half_point, jacobians[0], jacobians[1])
        return element_rate(grid_one, jacobian, west_one, east_one, front_one, back_one, live_one)
    tendencies = lax.map(one_block, (nodal_grid, ext_west, ext_east, ext_front, ext_back, live_rows, layer_index))
    return tendencies.reshape(flow_state.shape)

def reference(flow_state, jacobians, interp_weights, offsets, live_rows):
    first_section = flow_state + step_size * section_rate(flow_state, jacobians, interp_weights[0], offsets[0], live_rows)
    second_section = first_section + step_size * section_rate(first_section, jacobians, interp_weights[1], offsets[1], live_rows)
    return 0.5 * flow_state + 0.5 * second_section
```

```python
import functools

import jax
import jax.numpy as jnp
import numpy as np
from jax import lax
from jax.experimental import pallas as pl
from jax.experimental.pallas import tpu as pltpu
from jax.sharding import PartitionSpec as P

STEP = 0.04
GROUPS = 4
WIDTH = 128 // GROUPS
VARS = 5
TILE = (8, 128)
AXES = ("azim", "block")
VMEM = pl.BlockSpec(memory_space=pltpu.VMEM)
ANY = pl.BlockSpec(memory_space=pl.ANY)
SMEM = pl.BlockSpec(memory_space=pltpu.SMEM)
PARAMS = pltpu.CompilerParams(vmem_limit_bytes=40 * 1024 * 1024)


def derivative_matrix():
    points = np.array([-1.0, -1.0 / np.sqrt(5.0), 1.0 / np.sqrt(5.0), 1.0])
    differ = points[:, None] - points[None, :]
    filled = differ + np.eye(4)
    weights = 1.0 / np.prod(filled, axis=1)
    matrix = weights[None, :] / weights[:, None] / filled
    matrix = matrix * (1.0 - np.eye(4))
    return matrix - np.eye(4) * matrix.sum(axis=1)[:, None]


DM = derivative_matrix()


def lanes():
    return lax.broadcasted_iota(jnp.int32, TILE, 1)


def rows():
    return lax.broadcasted_iota(jnp.int32, TILE, 0)


def splat_matrix(jac_ref, side, k):
    return [[jnp.full(TILE, jac_ref[side, k, w, v], jnp.float32) for v in range(VARS)] for w in range(VARS)]


def bound_of(matrix):
    sums = [functools.reduce(jnp.add, [jnp.abs(e) for e in row]) for row in matrix]
    return functools.reduce(jnp.maximum, sums)


def face_matrix(jac_ref, side, k, orient, scale):
    matrix = splat_matrix(jac_ref, side, k)
    lam = bound_of(matrix)
    factor = jnp.full(TILE, orient, jnp.float32) * (3.0 * scale)
    return [
        [factor * matrix[w][v] + (3.0 * scale) * lam if w == v else factor * matrix[w][v] for v in range(VARS)]
        for w in range(VARS)
    ]


def mix(matrix, z):
    return [functools.reduce(jnp.add, [matrix[w][v] * z[v] for v in range(VARS)]) for w in range(VARS)]


def live_masks(live_ref):
    live = live_ref[0]
    return [(rows() + 8 * h < live).astype(jnp.float32) for h in range(2)]


def put_columns(lane, j, west_tile, east_tile, west, east):
    return (
        jnp.where(lane == j, pltpu.roll(west_tile, j, 1), west),
        jnp.where(lane == j, pltpu.roll(east_tile, j + 1, 1), east),
    )


def pack_groups(ctl_ref, face_ref, out_ref):
    lane_block = lanes() // WIDTH
    reverse = ctl_ref[0] >= 8

    def body(s, carry):
        tiles = [face_ref[2 * s + i // 2, i % 2] for i in range(4)]
        for j in range(GROUPS):
            out = tiles[0] if j == 0 else pltpu.roll(tiles[0], (-j * WIDTH) % 128, 1)
            for i in range(1, 4):
                rolled = tiles[i] if i == j else pltpu.roll(tiles[i], ((i - j) * WIDTH) % 128, 1)
                out = jnp.where(lane_block == i, rolled, out)
            out_ref[jnp.where(reverse, GROUPS - 1 - j, j), s] = out
        return carry

    lax.fori_loop(0, 40, body, 0, unroll=8)


def split_bf16(x):
    high = x.astype(jnp.bfloat16)
    return high, (x - high.astype(jnp.float32)).astype(jnp.bfloat16)


def interface_exterior(ctl_ref, offset_ref, section, window_ref, weight_ref, near_ref, out_ref):
    rotor = ctl_ref[0] < 8
    within = offset_ref[section] % WIDTH
    lane = lanes()
    lane_block = lane // WIDTH
    z_block = jnp.where(rotor, 0, 3)

    def pick(x, z, amount):
        start = jnp.where(rotor, 0, 128 - amount)
        sent = (lane >= start) & (lane < start + amount)
        return pltpu.roll(jnp.where(sent, z, x), jnp.where(rotor, (128 - amount) % 128, amount), 1)

    def body(s, carry):
        groups = [window_ref[jnp.where(rotor, 4 - b, 1 + b), s] for b in range(4)]
        extra = window_ref[0, s]
        for i in range(4):
            x = groups[0] if i == 0 else pltpu.roll(groups[0], (-i * WIDTH) % 128, 1)
            for b in range(1, 4):
                rolled = groups[b] if i == b else pltpu.roll(groups[b], ((b - i) * WIDTH) % 128, 1)
                x = jnp.where(lane_block == b, rolled, x)
            z = pltpu.roll(extra, ((z_block - i + 4) % 4) * WIDTH, 1)
            index = 2 * (s // 8) + i % 2
            place = pl.multiple_of(8 * (2 * (s % 8) + i // 2), 8)
            near_ref[index, pl.ds(place, 8), :] = pick(x, z, within)
            near_ref[index, pl.ds(place + 128, 8), :] = pick(x, z, within + 1)
        return carry

    lax.fori_loop(0, 40, body, 0, unroll=4)
    w_high, w_low = split_bf16(weight_ref[section])
    w_both = jnp.concatenate([w_high, w_low], axis=0)
    for v in range(VARS):
        both = jnp.concatenate([near_ref[2 * v], near_ref[2 * v + 1]], axis=1)
        high, low = split_bf16(both)
        first = jnp.dot(w_both, high, preferred_element_type=jnp.float32)
        total = first[:128] + first[128:] + jnp.dot(w_high, low, preferred_element_type=jnp.float32)
        out_ref[2 * v] = total[:, :128]
        out_ref[2 * v + 1] = total[:, 128:]


def extract_kernel(ctl_ref, live_ref, u_ref, off_ref, on_ref, west_ref, east_ref, groups_ref, sides_ref, sems):
    block = ctl_ref[0]
    x_off = 3 * (block % 2)
    copies = [[], [], []]
    for v in range(VARS):
        face = pl.ds(v * 16, 16)
        copies[0].append(pltpu.make_async_copy(u_ref.at[v, :, x_off], off_ref.at[face], sems.at[v]))
        copies[1].append(pltpu.make_async_copy(u_ref.at[v, :, 3 - x_off], on_ref.at[face], sems.at[5 + v]))
        for e in range(2):
            copies[2].append(
                pltpu.make_async_copy(
                    u_ref.at[v, pl.ds(12 * e, 4), pl.ds(1, 2)], sides_ref.at[v, e], sems.at[10 + 2 * v + e]
                )
            )
    for group in copies:
        for copy in group:
            copy.start()
    masks = live_masks(live_ref)
    for h in range(2):
        off_ref[80, h] = masks[h]
        on_ref[80, h] = masks[h]
    for copy in copies[0]:
        copy.wait()

    @pl.when((block == 7) | (block == 8))
    def _():
        pack_groups(ctl_ref, off_ref, groups_ref)

    for group in copies[1:]:
        for copy in group:
            copy.wait()
    lane = lanes()
    for h in range(2):
        west = jnp.zeros(TILE, jnp.float32)
        east = jnp.zeros(TILE, jnp.float32)
        for v in range(VARS):
            for p in range(4):
                for x in (1, 2):
                    j = 16 * v + 4 * p + x
                    west, east = put_columns(
                        lane, j, sides_ref[v, 0, p, x - 1, h], sides_ref[v, 1, p, x - 1, h], west, east
                    )
        west_ref[h] = west
        east_ref[h] = east
    face_columns(ctl_ref, off_ref, on_ref, west_ref, east_ref)


def face_columns(ctl_ref, off_ref, on_ref, west_ref, east_ref):
    x_off = 3 * (ctl_ref[0] % 2)
    lane = lanes()
    for h in range(2):
        west, east = west_ref[h], east_ref[h]
        for x, ref in ((x_off, off_ref), (3 - x_off, on_ref)):
            for v in range(VARS):
                for p in range(4):
                    j = 16 * v + 4 * p + x
                    west, east = put_columns(lane, j, ref[v * 16 + p, h], ref[v * 16 + 12 + p, h], west, east)
        west_ref[h] = west
        east_ref[h] = east


def derivative_terms(u0, u1, u2, u3):
    even = (u0 + u3) - (u1 + u2)
    o, g = u0 - u3, u1 - u2
    a = float(0.5 * (DM[0, 0] + DM[3, 0]))
    b = float(0.5 * (DM[0, 1] + DM[3, 1]))
    c = float(0.5 * (DM[1, 0] + DM[2, 0]))
    d = float(0.5 * (DM[1, 1] + DM[2, 1]))
    outer = (-a) * o - b * g
    inner = (-c) * o - d * g
    outer_even = float(-0.5 * (DM[0, 0] - DM[3, 0])) * even
    inner_even = float(-0.5 * (DM[1, 0] - DM[2, 0])) * even
    return outer + outer_even, inner + inner_even, inner - inner_even, outer - outer_even


def interior(ctl_ref, live_ref, jac_ref, u_ref, west_ref, east_ref, acc_ref, scale, finish):
    side = jnp.where(ctl_ref[0] < 8, 0, 1)
    lane, row = lanes(), rows()
    masks = live_masks(live_ref)

    def terms(matrix, lam3, z, jumps):
        outs = []
        for node in range(4):
            mixed = mix(matrix, [z[v][node] for v in range(VARS)])
            if node in jumps:
                mixed = [mixed[v] - lam3 * jumps[node][v] for v in range(VARS)]
            outs.append(mixed)
        return outs

    def coefficients(k):
        matrix = splat_matrix(jac_ref, side, k)
        lam3 = bound_of(matrix) * (3.0 * scale)
        return [[scale * e for e in r] for r in matrix], lam3

    def along_a(matrix, lam3):
        def body(i, carry):
            h, n = i % 2, i // 2
            p, x = n // 4, n % 4
            halo_w, halo_e = west_ref[h], east_ref[h]
            z, jump_w, jump_e = [], [], []
            for v in range(VARS):
                u = [u_ref[v, 4 * a + p, x, h] for a in range(4)]
                d = derivative_terms(*u)
                from_w = pltpu.roll(halo_w, (128 - 16 * v - n) % 128, 1)
                from_e = pltpu.roll(halo_e, 127 - 16 * v - n, 1)
                west = u[0] - jnp.where(lane == 0, from_w, pltpu.roll(u[3], 1, 1))
                east = u[3] - jnp.where(lane == 127, from_e, pltpu.roll(u[0], 127, 1))
                z.append([d[0] - 3.0 * west, d[1], d[2], d[3] + 3.0 * east])
                jump_w.append(west)
                jump_e.append(east)
            outs = terms(matrix, lam3, z, {0: jump_w, 3: jump_e})
            for a in range(4):
                for v in range(VARS):
                    acc_ref[v, 4 * a + p, x, h] = outs[a][v]
            return carry

        lax.fori_loop(0, 32, body, 0)

    def along_x(matrix, lam3):
        def body(i, carry):
            h, ap = i % 2, i // 2
            z, first, last = [], [], []
            for v in range(VARS):
                u = [u_ref[v, ap, x, h] for x in range(4)]
                d = derivative_terms(*u)
                z.append([d[0] - 3.0 * u[0], d[1], d[2], d[3] + 3.0 * u[3]])
                first.append(u[0])
                last.append(u[3])
            outs = terms(matrix, lam3, z, {0: first, 3: last})
            for x in range(4):
                for v in range(VARS):
                    acc_ref[v, ap, x, h] += outs[x][v]
            return carry

        lax.fori_loop(0, 32, body, 0)

    def along_p(matrix, lam3):
        def body(i, carry):
            a, x = i // 4, i % 4
            for h in range(2):
                z, jump_l, jump_u = [], [], []
                for v in range(VARS):
                    u = [u_ref[v, 4 * a + p, x, h] for p in range(4)]
                    d = derivative_terms(*u)
                    if h == 0:
                        below = jnp.where(row == 0, u[0], pltpu.roll(u[3], 1, 0))
                        other = u_ref[v, 4 * a, x, 1]
                        above = pltpu.roll(jnp.where(row == 0, other, u[0]), 7, 0)
                    else:
                        other = u_ref[v, 4 * a + 3, x, 0]
                        below = pltpu.roll(jnp.where(row == 7, other, u[3]), 1, 0)
                        above = jnp.where(row == 7, u[3], pltpu.roll(u[0], 7, 0))
                    lower, upper = u[0] - below, u[3] - above
                    z.append([d[0] - 3.0 * lower, d[1], d[2], d[3] + 3.0 * upper])
                    jump_l.append(lower)
                    jump_u.append(upper)
                outs = terms(matrix, lam3, z, {0: jump_l, 3: jump_u})
                for p in range(4):
                    for v in range(VARS):
                        total = acc_ref[v, 4 * a + p, x, h] + outs[p][v]
                        acc_ref[v, 4 * a + p, x, h] = finish(v, 4 * a + p, x, h, masks[h] * total)
            return carry

        lax.fori_loop(0, 16, body, 0)

    along_a(*coefficients(0))
    along_x(*coefficients(2))
    along_p(*coefficients(1))


def expanded_weights(rotor, pair):
    row = lax.broadcasted_iota(jnp.int32, (128, 16), 0) // 8
    spread = (row == lax.broadcasted_iota(jnp.int32, (128, 16), 1)).astype(jnp.float32)
    same = (
        lax.broadcasted_iota(jnp.int32, (128, 128), 0) % 8 == lax.broadcasted_iota(jnp.int32, (128, 128), 1) % 8
    )
    dot = functools.partial(
        lax.dot_general, precision=lax.Precision.HIGHEST, preferred_element_type=jnp.float32
    )
    out = []
    for matrix in pair:
        plain = dot(spread, matrix, (((1,), (0,)), ((), ())))
        turned = dot(spread, matrix, (((1,), (1,)), ((), ())))
        picked = jnp.where(rotor, turned, plain)
        out.append(jnp.where(same, dot(picked, spread, (((1,), (1,)), ((), ()))), 0.0))
    return jnp.concatenate(out, axis=1)


def first_interior_kernel(ctl_ref, live_ref, jac_ref, u_ref, west_ref, east_ref, weight_ref,
                          out_ref, off_ref, on_ref, new_west_ref, new_east_ref, expanded_ref):
    block = ctl_ref[0]
    interior(
        ctl_ref, live_ref, jac_ref, u_ref, west_ref, east_ref, out_ref, STEP,
        lambda v, ap, x, h, total: u_ref[v, ap, x, h] + total,
    )
    x_off = 3 * (block % 2)

    def body(ap, carry):
        for v in range(VARS):
            off_ref[v * 16 + ap] = out_ref[v, ap, x_off]
            on_ref[v * 16 + ap] = out_ref[v, ap, 3 - x_off]
        return carry

    lax.fori_loop(0, 16, body, 0)
    lane = lanes()
    for h in range(2):
        west = jnp.zeros(TILE, jnp.float32)
        east = jnp.zeros(TILE, jnp.float32)
        for v in range(VARS):
            for p in range(4):
                for x in (1, 2):
                    j = 16 * v + 4 * p + x
                    west, east = put_columns(lane, j, out_ref[v, p, x, h], out_ref[v, 12 + p, x, h], west, east)
        new_west_ref[h] = west
        new_east_ref[h] = east

    @pl.when((block == 7) | (block == 8))
    def _():
        for section in range(2):
            expanded_ref[section] = expanded_weights(block < 8, [weight_ref[section, i] for i in range(2)])


def second_interior_kernel(ctl_ref, live_ref, jac_ref, u_ref, west_ref, east_ref, first_ref, off_mask_ref,
                           on_mask_ref, out_ref):
    interior(
        ctl_ref, live_ref, jac_ref, first_ref, west_ref, east_ref, out_ref, 0.5 * STEP,
        lambda v, ap, x, h, total: 0.5 * u_ref[v, ap, x, h] + 0.5 * first_ref[v, ap, x, h] + total,
    )
    block = ctl_ref[0]
    side = jnp.where(block < 8, 0, 1)
    x_off = 3 * (block % 2)
    masks = live_masks(live_ref)
    jac = splat_matrix(jac_ref, side, 2)
    lam = bound_of(jac)
    factor = 0.5 * (3.0 * STEP) ** 2
    matrix = []
    for w in range(VARS):
        line = []
        for v in range(VARS):
            square = functools.reduce(jnp.add, [jac[w][k] * jac[k][v] for k in range(VARS)])
            line.append(factor * (lam * lam - square) if w == v else -factor * square)
        matrix.append(line)
    for x, mask_ref in ((x_off, off_mask_ref), (3 - x_off, on_mask_ref)):
        both = [masks[h] * mask_ref[80, h] for h in range(2)]

        def body(ap, carry, x=x, both=both):
            for h in range(2):
                mixed = mix(matrix, [u_ref[v, ap, x, h] for v in range(VARS)])
                for v in range(VARS):
                    out_ref[v, ap, x, h] += both[h] * mixed[v]
            return carry

        lax.fori_loop(0, 16, body, 0)


def apply_exterior(ctl_ref, live_ref, offset_ref, jac_ref, base_ref, off_ref, on_ref, window_ref, weight_ref,
                   out_ref, near_ref, ext_ref, faces_ref, sems, section, scale, between):
    block = ctl_ref[0]
    side = jnp.where(block < 8, 0, 1)
    odd = block % 2
    x_off = 3 * odd
    masks = live_masks(live_ref)
    interface = (block == 7) | (block == 8)
    xs = (x_off, 3 - x_off)
    loads = [
        [
            pltpu.make_async_copy(base_ref.at[v, :, xs[f]], faces_ref.at[f, pl.ds(16 * v, 16)], sems.at[f, v])
            for v in range(VARS)
        ]
        for f in range(2)
    ]
    stores = [
        [
            pltpu.make_async_copy(faces_ref.at[f, pl.ds(16 * v, 16)], out_ref.at[v, :, xs[f]], sems.at[f, v])
            for v in range(VARS)
        ]
        for f in range(2)
    ]
    for group in loads:
        for copy in group:
            copy.start()

    @pl.when(interface)
    def _():
        interface_exterior(ctl_ref, offset_ref, section, window_ref, weight_ref, near_ref, ext_ref)

    @pl.when(jnp.logical_not(interface))
    def _():
        def body(ap, carry):
            place = pl.multiple_of(8 * ap, 8)
            for v in range(VARS):
                for h in range(2):
                    ext_ref[2 * v + h, pl.ds(place, 8), :] = off_ref[v * 16 + ap, h]
            return carry

        lax.fori_loop(0, 16, body, 0)

    orient = jnp.where(odd == 0, 1.0, -1.0)
    for f in range(2):
        for copy in loads[f]:
            copy.wait()
        matrix = face_matrix(jac_ref, side, 2, orient if f == 0 else -orient, scale)

        def body(ap, carry, f=f, matrix=matrix):
            place = pl.multiple_of(8 * ap, 8)
            for h in range(2):
                if f == 0:
                    ext = [ext_ref[2 * v + h, pl.ds(place, 8), :] for v in range(VARS)]
                else:
                    ext = [on_ref[v * 16 + ap, h] for v in range(VARS)]
                mixed = mix(matrix, ext)
                for v in range(VARS):
                    faces_ref[f, v * 16 + ap, h] += masks[h] * mixed[v]
            return carry

        lax.fori_loop(0, 16, body, 0, unroll=2)
        for copy in stores[f]:
            copy.start()
        between(f)
    for group in stores:
        for copy in group:
            copy.wait()


def first_exterior_kernel(ctl_ref, live_ref, offset_ref, jac_ref, base_ref, off_ref, on_ref, window_ref, weight_ref,
                          west_ref, east_ref, out_ref, new_west_ref, new_east_ref, groups_ref,
                          near_ref, ext_ref, faces_ref, sems):
    block = ctl_ref[0]

    def between(f):
        if f == 0:
            @pl.when((block == 7) | (block == 8))
            def _():
                pack_groups(ctl_ref, faces_ref.at[0], groups_ref)
        else:
            new_west_ref[...] = west_ref[...]
            new_east_ref[...] = east_ref[...]
            face_columns(ctl_ref, faces_ref.at[0], faces_ref.at[1], new_west_ref, new_east_ref)

    apply_exterior(ctl_ref, live_ref, offset_ref, jac_ref, base_ref, off_ref, on_ref, window_ref, weight_ref,
                   out_ref, near_ref, ext_ref, faces_ref, sems, 0, STEP, between)


def second_exterior_kernel(ctl_ref, live_ref, offset_ref, jac_ref, base_ref, off_ref, on_ref, window_ref, weight_ref,
                           out_ref, near_ref, ext_ref, faces_ref, sems):
    apply_exterior(ctl_ref, live_ref, offset_ref, jac_ref, base_ref, off_ref, on_ref, window_ref, weight_ref,
                   out_ref, near_ref, ext_ref, faces_ref, sems, 1, 0.5 * STEP, lambda f: None)


def shape(*dims):
    return jax.ShapeDtypeStruct(dims, jnp.float32)


STATE = shape(VARS, 16, 4, 2, 8, 128)
FACE = shape(80, 2, 8, 128)
FACE_AND_MASK = shape(81, 2, 8, 128)
COLUMNS = shape(2, 8, 128)
PANEL = shape(GROUPS, 40, 8, 128)
EXPANDED = shape(2, 128, 256)
EXTERIOR_SCRATCH = [
    pltpu.VMEM((10, 256, 128), jnp.float32),
    pltpu.VMEM((10, 128, 128), jnp.float32),
    pltpu.VMEM((2, 80, 2, 8, 128), jnp.float32),
    pltpu.SemaphoreType.DMA((2, VARS)),
]
EXTRACT_SCRATCH = [pltpu.VMEM((VARS, 2, 4, 2, 2, 8, 128), jnp.float32), pltpu.SemaphoreType.DMA((20,))]


def call(kernel, smem, vmem, outs, scratch=(), flops=10**7, first_any=False, in_place=False):
    moved = sum(4 * a.size for a in vmem) + sum(4 * np.prod(o.shape) for o in outs)
    head = [ANY] if first_any else [VMEM]
    return pl.pallas_call(
        kernel,
        in_specs=[SMEM] * len(smem) + head + [VMEM] * (len(vmem) - 1),
        out_specs=([ANY] if in_place else [VMEM]) + [VMEM] * (len(outs) - 1),
        out_shape=list(outs),
        scratch_shapes=list(scratch),
        input_output_aliases={len(smem): 0} if in_place else {},
        compiler_params=PARAMS,
        cost_estimate=pl.CostEstimate(flops=flops, bytes_accessed=int(moved), transcendentals=0),
    )(*smem, *vmem)


def send(array, route):
    sectors, layers = lax.axis_size("azim"), lax.axis_size("block")
    pairs = []
    for s in range(sectors):
        for b in range(layers):
            to = route(s, b)
            if to is not None:
                pairs.append((s * layers + b, to[0] * layers + to[1]))
    return lax.ppermute(array, AXES, pairs)


def off_chip(s, b):
    if b in (0, 7, 8, 15):
        return None
    return (s, b + 1 if b % 2 else b - 1)


def on_chip(s, b):
    return (s, b ^ 1)


def eastward(s, b):
    return ((s + 1) % 16, b)


def westward(s, b):
    return ((s - 1) % 16, b)


def across(turns):
    def route(s, b):
        if b == 7:
            return ((s + turns) % 16, 8)
        if b == 8:
            return ((s - turns) % 16, 7)
        return None

    return route


def exchange(panel, west, east, offset, compute, operands):
    def branch(index):
        turns, steps = index // GROUPS, index % GROUPS

        def run(panel, west, east, operands):
            aligned = send(panel[: GROUPS - steps], across(turns))
            lagging = send(panel[GROUPS - 1 - steps :], across(turns + 1))
            from_west = send(east, eastward)
            from_east = send(west, westward)
            results = compute(from_west, from_east, *operands)
            return (jnp.concatenate([lagging, aligned], axis=0), *results)

        return run

    def tree(first, count, shift):
        if count == 1:
            return branch(first)
        part = count // 4
        branches = [tree(first + i * part, part, shift - 2) for i in range(4)]

        def run(panel, west, east, operands):
            index = lax.shift_right_logical(offset, jnp.int32(shift)) & 3
            return lax.switch(index, branches, panel, west, east, operands)

        return run

    return tree(0, 16 * GROUPS, 9)(panel, west, east, operands)


def shards(flow_state, jacobians, interp_weights, offsets, live_rows):
    ctl = lax.axis_index("block").astype(jnp.int32).reshape(1)
    u = flow_state.reshape(VARS, 16, 4, 2, 8, 128)
    off, on, west, east, panel = call(
        extract_kernel,
        [ctl, live_rows],
        [u],
        [FACE_AND_MASK, FACE_AND_MASK, COLUMNS, COLUMNS, PANEL],
        EXTRACT_SCRATCH,
        first_any=True,
    )
    off_1 = send(off, off_chip)
    on_1 = send(on, on_chip)

    def first_part(from_west, from_east, ctl, live, jac, u, weights):
        return call(
            first_interior_kernel,
            [ctl, live, jac],
            [u, from_west, from_east, weights],
            [STATE, FACE, FACE, COLUMNS, COLUMNS, EXPANDED],
            flops=10**8,
        )

    window_1, base_1, off, on, west, east, expanded = exchange(
        panel, west, east, offsets[0], first_part, (ctl, live_rows, jacobians, u, interp_weights)
    )
    off_2 = send(off, off_chip)
    on_2 = send(on, on_chip)
    smem = [ctl, live_rows, offsets, jacobians]
    first, west, east, panel = call(
        first_exterior_kernel,
        smem,
        [base_1, off_1, on_1, window_1, expanded, west, east],
        [STATE, COLUMNS, COLUMNS, PANEL],
        EXTERIOR_SCRATCH,
        first_any=True,
        in_place=True,
    )

    def second_part(from_west, from_east, ctl, live, jac, u, first, off_1, on_1):
        return call(
            second_interior_kernel,
            [ctl, live, jac],
            [u, from_west, from_east, first, off_1, on_1],
            [STATE],
            flops=10**8,
        )

    window_2, base_2 = exchange(
        panel, west, east, offsets[1], second_part, (ctl, live_rows, jacobians, u, first, off_1, on_1)
    )
    out = call(
        second_exterior_kernel,
        smem,
        [base_2, off_2, on_2, window_2, expanded],
        [STATE],
        EXTERIOR_SCRATCH,
        first_any=True,
        in_place=True,
    )[0]
    return out.reshape(flow_state.shape)


def solution(mesh):
    placed = (P("block", None, None, None, "azim"), P(), P(), P(), P("block"))
    return jax.shard_map(
        shards,
        mesh=mesh,
        in_specs=placed,
        out_specs=P("block", None, None, None, "azim"),
        check_vma=False,
    )
```

```python
import functools

import jax
import jax.numpy as jnp
import numpy as np
from jax import lax
from jax.experimental import pallas as pl
from jax.experimental.pallas import tpu as pltpu
from jax.sharding import PartitionSpec as P

STEP = 0.04
VARS = 5
TILE = (8, 128)
AXES = ("azim", "block")
VMEM = pl.BlockSpec(memory_space=pltpu.VMEM)
ANY = pl.BlockSpec(memory_space=pl.ANY)
SMEM = pl.BlockSpec(memory_space=pltpu.SMEM)
PARAMS = pltpu.CompilerParams(vmem_limit_bytes=40 * 1024 * 1024)


def derivative_matrix():
    points = np.array([-1.0, -1.0 / np.sqrt(5.0), 1.0 / np.sqrt(5.0), 1.0])
    differ = points[:, None] - points[None, :]
    filled = differ + np.eye(4)
    weights = 1.0 / np.prod(filled, axis=1)
    matrix = weights[None, :] / weights[:, None] / filled
    matrix = matrix * (1.0 - np.eye(4))
    return matrix - np.eye(4) * matrix.sum(axis=1)[:, None]


DM = derivative_matrix()


def lanes():
    return lax.broadcasted_iota(jnp.int32, TILE, 1)


def rows():
    return lax.broadcasted_iota(jnp.int32, TILE, 0)


def splat_matrix(jac_ref, side, k):
    return [[jnp.full(TILE, jac_ref[side, k, w, v], jnp.float32) for v in range(VARS)] for w in range(VARS)]


def bound_of(matrix):
    sums = [functools.reduce(jnp.add, [jnp.abs(e) for e in row]) for row in matrix]
    return functools.reduce(jnp.maximum, sums)


def face_matrix(jac_ref, side, k, orient, scale):
    matrix = splat_matrix(jac_ref, side, k)
    lam = bound_of(matrix)
    factor = jnp.full(TILE, orient, jnp.float32) * (3.0 * scale)
    return [
        [factor * matrix[w][v] + (3.0 * scale) * lam if w == v else factor * matrix[w][v] for v in range(VARS)]
        for w in range(VARS)
    ]


def mix(matrix, z):
    return [functools.reduce(jnp.add, [matrix[w][v] * z[v] for v in range(VARS)]) for w in range(VARS)]


def live_masks(live_ref):
    live = live_ref[0]
    return [(rows() + 8 * h < live).astype(jnp.float32) for h in range(2)]


def put_columns(lane, j, west_tile, east_tile, west, east):
    return (
        jnp.where(lane == j, pltpu.roll(west_tile, j, 1), west),
        jnp.where(lane == j, pltpu.roll(east_tile, j + 1, 1), east),
    )


def split_bf16(x):
    high = x.astype(jnp.bfloat16)
    return high, (x - high.astype(jnp.float32)).astype(jnp.bfloat16)


def extract_kernel(ctl_ref, live_ref, u_ref, off_ref, on_ref, west_ref, east_ref, sides_ref, sems):
    block = ctl_ref[0]
    x_off = 3 * (block % 2)
    copies = [[], [], []]
    for v in range(VARS):
        face = pl.ds(v * 16, 16)
        copies[0].append(pltpu.make_async_copy(u_ref.at[v, :, x_off], off_ref.at[face], sems.at[v]))
        copies[1].append(pltpu.make_async_copy(u_ref.at[v, :, 3 - x_off], on_ref.at[face], sems.at[5 + v]))
        for e in range(2):
            copies[2].append(
                pltpu.make_async_copy(
                    u_ref.at[v, pl.ds(12 * e, 4), pl.ds(1, 2)], sides_ref.at[v, e], sems.at[10 + 2 * v + e]
                )
            )
    for group in copies:
        for copy in group:
            copy.start()
    masks = live_masks(live_ref)
    for h in range(2):
        off_ref[80, h] = masks[h]
        on_ref[80, h] = masks[h]
    for group in copies:
        for copy in group:
            copy.wait()
    lane = lanes()
    for h in range(2):
        west = jnp.zeros(TILE, jnp.float32)
        east = jnp.zeros(TILE, jnp.float32)
        for v in range(VARS):
            for p in range(4):
                for x in (1, 2):
                    j = 16 * v + 4 * p + x
                    west, east = put_columns(
                        lane, j, sides_ref[v, 0, p, x - 1, h], sides_ref[v, 1, p, x - 1, h], west, east
                    )
        west_ref[h] = west
        east_ref[h] = east
    face_columns(ctl_ref, off_ref, on_ref, west_ref, east_ref)


def face_columns(ctl_ref, off_ref, on_ref, west_ref, east_ref):
    x_off = 3 * (ctl_ref[0] % 2)
    lane = lanes()
    for h in range(2):
        west, east = west_ref[h], east_ref[h]
        for x, ref in ((x_off, off_ref), (3 - x_off, on_ref)):
            for v in range(VARS):
                for p in range(4):
                    j = 16 * v + 4 * p + x
                    west, east = put_columns(lane, j, ref[v * 16 + p, h], ref[v * 16 + 12 + p, h], west, east)
        west_ref[h] = west
        east_ref[h] = east


def derivative_terms(u0, u1, u2, u3):
    even = (u0 + u3) - (u1 + u2)
    o, g = u0 - u3, u1 - u2
    a = float(0.5 * (DM[0, 0] + DM[3, 0]))
    b = float(0.5 * (DM[0, 1] + DM[3, 1]))
    c = float(0.5 * (DM[1, 0] + DM[2, 0]))
    d = float(0.5 * (DM[1, 1] + DM[2, 1]))
    outer = (-a) * o - b * g
    inner = (-c) * o - d * g
    outer_even = float(-0.5 * (DM[0, 0] - DM[3, 0])) * even
    inner_even = float(-0.5 * (DM[1, 0] - DM[2, 0])) * even
    return outer + outer_even, inner + inner_even, inner - inner_even, outer - outer_even


def interior(ctl_ref, live_ref, jac_ref, u_ref, west_ref, east_ref, acc_ref, scale, finish):
    side = jnp.where(ctl_ref[0] < 8, 0, 1)
    lane, row = lanes(), rows()
    masks = live_masks(live_ref)

    def terms(matrix, lam3, z, jumps):
        outs = []
        for node in range(4):
            mixed = mix(matrix, [z[v][node] for v in range(VARS)])
            if node in jumps:
                mixed = [mixed[v] - lam3 * jumps[node][v] for v in range(VARS)]
            outs.append(mixed)
        return outs

    def coefficients(k):
        matrix = splat_matrix(jac_ref, side, k)
        lam3 = bound_of(matrix) * (3.0 * scale)
        return [[scale * e for e in r] for r in matrix], lam3

    def along_a(matrix, lam3):
        def body(i, carry):
            h, n = i % 2, i // 2
            p, x = n // 4, n % 4
            halo_w, halo_e = west_ref[h], east_ref[h]
            z, jump_w, jump_e = [], [], []
            for v in range(VARS):
                u = [u_ref[v, 4 * a + p, x, h] for a in range(4)]
                d = derivative_terms(*u)
                from_w = pltpu.roll(halo_w, (128 - 16 * v - n) % 128, 1)
                from_e = pltpu.roll(halo_e, 127 - 16 * v - n, 1)
                west = u[0] - jnp.where(lane == 0, from_w, pltpu.roll(u[3], 1, 1))
                east = u[3] - jnp.where(lane == 127, from_e, pltpu.roll(u[0], 127, 1))
                z.append([d[0] - 3.0 * west, d[1], d[2], d[3] + 3.0 * east])
                jump_w.append(west)
                jump_e.append(east)
            outs = terms(matrix, lam3, z, {0: jump_w, 3: jump_e})
            for a in range(4):
                for v in range(VARS):
                    acc_ref[v, 4 * a + p, x, h] = outs[a][v]
            return carry

        lax.fori_loop(0, 32, body, 0)

    def along_x(matrix, lam3):
        def body(i, carry):
            h, ap = i % 2, i // 2
            z, first, last = [], [], []
            for v in range(VARS):
                u = [u_ref[v, ap, x, h] for x in range(4)]
                d = derivative_terms(*u)
                z.append([d[0] - 3.0 * u[0], d[1], d[2], d[3] + 3.0 * u[3]])
                first.append(u[0])
                last.append(u[3])
            outs = terms(matrix, lam3, z, {0: first, 3: last})
            for x in range(4):
                for v in range(VARS):
                    acc_ref[v, ap, x, h] += outs[x][v]
            return carry

        lax.fori_loop(0, 32, body, 0)

    def along_p(matrix, lam3):
        def body(i, carry):
            a, x = i // 4, i % 4
            for h in range(2):
                z, jump_l, jump_u = [], [], []
                for v in range(VARS):
                    u = [u_ref[v, 4 * a + p, x, h] for p in range(4)]
                    d = derivative_terms(*u)
                    if h == 0:
                        below = jnp.where(row == 0, u[0], pltpu.roll(u[3], 1, 0))
                        other = u_ref[v, 4 * a, x, 1]
                        above = pltpu.roll(jnp.where(row == 0, other, u[0]), 7, 0)
                    else:
                        other = u_ref[v, 4 * a + 3, x, 0]
                        below = pltpu.roll(jnp.where(row == 7, other, u[3]), 1, 0)
                        above = jnp.where(row == 7, u[3], pltpu.roll(u[0], 7, 0))
                    lower, upper = u[0] - below, u[3] - above
                    z.append([d[0] - 3.0 * lower, d[1], d[2], d[3] + 3.0 * upper])
                    jump_l.append(lower)
                    jump_u.append(upper)
                outs = terms(matrix, lam3, z, {0: jump_l, 3: jump_u})
                for p in range(4):
                    for v in range(VARS):
                        total = acc_ref[v, 4 * a + p, x, h] + outs[p][v]
                        acc_ref[v, 4 * a + p, x, h] = finish(v, 4 * a + p, x, h, masks[h] * total)
            return carry

        lax.fori_loop(0, 16, body, 0)

    along_a(*coefficients(0))
    along_x(*coefficients(2))
    along_p(*coefficients(1))


def expanded_weights(turn, pair):
    row = lax.broadcasted_iota(jnp.int32, (128, 16), 0) // 8
    spread = (row == lax.broadcasted_iota(jnp.int32, (128, 16), 1)).astype(jnp.float32)
    same = (
        lax.broadcasted_iota(jnp.int32, (128, 128), 0) % 8 == lax.broadcasted_iota(jnp.int32, (128, 128), 1) % 8
    )
    dot = functools.partial(
        lax.dot_general, precision=lax.Precision.HIGHEST, preferred_element_type=jnp.float32
    )
    out = []
    for matrix in pair:
        plain = dot(spread, matrix, (((1,), (0,)), ((), ())))
        turned = dot(spread, matrix, (((1,), (1,)), ((), ())))
        picked = jnp.where(turn, turned, plain)
        out.append(jnp.where(same, dot(picked, spread, (((1,), (1,)), ((), ()))), 0.0))
    return jnp.concatenate(out, axis=1)


def first_interior_kernel(ctl_ref, live_ref, jac_ref, u_ref, west_ref, east_ref, weight_ref,
                          out_ref, off_ref, on_ref, new_west_ref, new_east_ref, expanded_ref):
    block = ctl_ref[0]
    interior(
        ctl_ref, live_ref, jac_ref, u_ref, west_ref, east_ref, out_ref, STEP,
        lambda v, ap, x, h, total: u_ref[v, ap, x, h] + total,
    )
    x_off = 3 * (block % 2)

    def body(ap, carry):
        for v in range(VARS):
            off_ref[v * 16 + ap] = out_ref[v, ap, x_off]
            on_ref[v * 16 + ap] = out_ref[v, ap, 3 - x_off]
        return carry

    lax.fori_loop(0, 16, body, 0)
    lane = lanes()
    for h in range(2):
        west = jnp.zeros(TILE, jnp.float32)
        east = jnp.zeros(TILE, jnp.float32)
        for v in range(VARS):
            for p in range(4):
                for x in (1, 2):
                    j = 16 * v + 4 * p + x
                    west, east = put_columns(lane, j, out_ref[v, p, x, h], out_ref[v, 12 + p, x, h], west, east)
        new_west_ref[h] = west
        new_east_ref[h] = east

    @pl.when((block == 7) | (block == 8))
    def _():
        for section in range(2):
            expanded_ref[section] = expanded_weights(block >= 8, [weight_ref[section, i] for i in range(2)])


def second_interior_kernel(ctl_ref, live_ref, jac_ref, u_ref, west_ref, east_ref, first_ref, off_mask_ref,
                           on_mask_ref, out_ref, off_ref, on_ref):
    interior(
        ctl_ref, live_ref, jac_ref, first_ref, west_ref, east_ref, out_ref, 0.5 * STEP,
        lambda v, ap, x, h, total: 0.5 * u_ref[v, ap, x, h] + 0.5 * first_ref[v, ap, x, h] + total,
    )
    block = ctl_ref[0]
    side = jnp.where(block < 8, 0, 1)
    x_off = 3 * (block % 2)
    masks = live_masks(live_ref)
    jac = splat_matrix(jac_ref, side, 2)
    lam = bound_of(jac)
    factor = 0.5 * (3.0 * STEP) ** 2
    matrix = []
    for w in range(VARS):
        line = []
        for v in range(VARS):
            square = functools.reduce(jnp.add, [jac[w][k] * jac[k][v] for k in range(VARS)])
            line.append(factor * (lam * lam - square) if w == v else -factor * square)
        matrix.append(line)
    for x, mask_ref, face_ref in ((x_off, off_mask_ref, off_ref), (3 - x_off, on_mask_ref, on_ref)):
        both = [masks[h] * mask_ref[80, h] for h in range(2)]

        def body(ap, carry, x=x, both=both, face_ref=face_ref):
            for h in range(2):
                mixed = mix(matrix, [u_ref[v, ap, x, h] for v in range(VARS)])
                for v in range(VARS):
                    face_ref[v * 16 + ap, h] = out_ref[v, ap, x, h] + both[h] * mixed[v]
            return carry

        lax.fori_loop(0, 16, body, 0)


def interface_kernel(section, ctl_ref, offset_ref, own_ref, next_ref, weight_ref, out_ref, near_ref):
    block = ctl_ref[0]

    @pl.when((block == 7) | (block == 8))
    def _():
        rotor = block < 8
        within = lax.rem(offset_ref[section], 128)
        lane = lanes()

        def pick(own, other, amount):
            start = jnp.where(rotor, 128 - amount, 0)
            sent = (lane >= start) & (lane < start + amount)
            turn = lax.rem(jnp.where(rotor, amount, 128 - amount), 128)
            return pltpu.roll(jnp.where(sent, other, own), turn, 1)

        def body(ap, carry):
            place = pl.multiple_of(8 * ap, 8)
            for v in range(VARS):
                for h in range(2):
                    own, other = own_ref[v * 16 + ap, h], next_ref[v * 16 + ap, h]
                    near_ref[2 * v + h, pl.ds(place, 8), :] = pick(own, other, within)
                    near_ref[2 * v + h, pl.ds(place + 128, 8), :] = pick(own, other, within + 1)
            return carry

        lax.fori_loop(0, 16, body, 0, unroll=2)
        w_high, w_low = split_bf16(weight_ref[section])
        w_both = jnp.concatenate([w_high, w_low], axis=0)
        for v in range(VARS):
            both = jnp.concatenate([near_ref[2 * v], near_ref[2 * v + 1]], axis=1)
            high, low = split_bf16(both)
            first = jnp.dot(w_both, high, preferred_element_type=jnp.float32)
            total = first[:128] + first[128:] + jnp.dot(w_high, low, preferred_element_type=jnp.float32)
            out_ref[2 * v] = total[:, :128]
            out_ref[2 * v + 1] = total[:, 128:]


def off_face(ctl_ref, live_ref, jac_ref, base_ref, ext_ref, window_ref, out_ref, scale):
    block = ctl_ref[0]
    odd = block % 2
    masks = live_masks(live_ref)
    matrix = face_matrix(
        jac_ref, jnp.where(block < 8, 0, 1), 2, jnp.where(odd == 0, 1.0, -1.0), scale
    )
    interface = (block == 7) | (block == 8)

    def run(load):
        def body(ap, carry):
            for h in range(2):
                mixed = mix(matrix, [load(v, ap, h) for v in range(VARS)])
                for v in range(VARS):
                    out_ref[v * 16 + ap, h] = base_ref[v * 16 + ap, h] + masks[h] * mixed[v]
            return carry

        lax.fori_loop(0, 16, body, 0, unroll=2)

    @pl.when(interface)
    def _():
        run(lambda v, ap, h: window_ref[2 * v + h, pl.ds(pl.multiple_of(8 * ap, 8), 8), :])

    @pl.when(jnp.logical_not(interface))
    def _():
        run(lambda v, ap, h: ext_ref[v * 16 + ap, h])


def on_face(ctl_ref, live_ref, jac_ref, base_ref, ext_ref, out_ref, scale):
    block = ctl_ref[0]
    masks = live_masks(live_ref)
    matrix = face_matrix(
        jac_ref, jnp.where(block < 8, 0, 1), 2, jnp.where(block % 2 == 0, -1.0, 1.0), scale
    )

    def body(ap, carry):
        for h in range(2):
            mixed = mix(matrix, [ext_ref[v * 16 + ap, h] for v in range(VARS)])
            for v in range(VARS):
                out_ref[v * 16 + ap, h] = base_ref[v * 16 + ap, h] + masks[h] * mixed[v]
        return carry

    lax.fori_loop(0, 16, body, 0, unroll=2)


def face_stores(face_ref, out_ref, x, sems):
    return [
        pltpu.make_async_copy(face_ref.at[pl.ds(16 * v, 16)], out_ref.at[v, :, x], sems.at[v])
        for v in range(VARS)
    ]


def first_off_kernel(ctl_ref, live_ref, jac_ref, base_ref, ext_ref, window_ref, out_ref):
    off_face(ctl_ref, live_ref, jac_ref, base_ref, ext_ref, window_ref, out_ref, STEP)


def first_on_kernel(ctl_ref, live_ref, jac_ref, state_ref, off_ref, base_ref, ext_ref, west_ref, east_ref,
                    out_ref, new_west_ref, new_east_ref, on_ref, sems):
    x_off = 3 * (ctl_ref[0] % 2)
    stores = face_stores(off_ref, out_ref, x_off, sems.at[0])
    for copy in stores:
        copy.start()
    on_face(ctl_ref, live_ref, jac_ref, base_ref, ext_ref, on_ref, STEP)
    more = face_stores(on_ref, out_ref, 3 - x_off, sems.at[1])
    for copy in more:
        copy.start()
    new_west_ref[...] = west_ref[...]
    new_east_ref[...] = east_ref[...]
    face_columns(ctl_ref, off_ref, on_ref, new_west_ref, new_east_ref)
    for copy in stores + more:
        copy.wait()


def second_exterior_kernel(ctl_ref, live_ref, jac_ref, state_ref, off_base_ref, off_ext_ref, window_ref, on_base_ref,
                           on_ext_ref, out_ref, off_ref, on_ref, sems):
    x_off = 3 * (ctl_ref[0] % 2)
    on_face(ctl_ref, live_ref, jac_ref, on_base_ref, on_ext_ref, on_ref, 0.5 * STEP)
    stores = face_stores(on_ref, out_ref, 3 - x_off, sems.at[0])
    for copy in stores:
        copy.start()
    off_face(ctl_ref, live_ref, jac_ref, off_base_ref, off_ext_ref, window_ref, off_ref, 0.5 * STEP)
    more = face_stores(off_ref, out_ref, x_off, sems.at[1])
    for copy in more:
        copy.start()
    for copy in stores + more:
        copy.wait()


def shape(*dims):
    return jax.ShapeDtypeStruct(dims, jnp.float32)


STATE = shape(VARS, 16, 4, 2, 8, 128)
FACE = shape(80, 2, 8, 128)
FACE_AND_MASK = shape(81, 2, 8, 128)
COLUMNS = shape(2, 8, 128)
EXPANDED = shape(2, 128, 256)
WINDOW = shape(10, 128, 128)
FACE_SCRATCH = pltpu.VMEM((80, 2, 8, 128), jnp.float32)
STORE_SEMS = pltpu.SemaphoreType.DMA((2, VARS))
EXTRACT_SCRATCH = [pltpu.VMEM((VARS, 2, 4, 2, 2, 8, 128), jnp.float32), pltpu.SemaphoreType.DMA((20,))]


def call(kernel, smem, vmem, outs, scratch=(), flops=10**7, first_any=False, in_place=False):
    moved = sum(4 * a.size for a in vmem) + sum(4 * np.prod(o.shape) for o in outs)
    head = [ANY] if first_any else [VMEM]
    return pl.pallas_call(
        kernel,
        in_specs=[SMEM] * len(smem) + head + [VMEM] * (len(vmem) - 1),
        out_specs=([ANY] if in_place else [VMEM]) + [VMEM] * (len(outs) - 1),
        out_shape=list(outs),
        scratch_shapes=list(scratch),
        input_output_aliases={len(smem): 0} if in_place else {},
        compiler_params=PARAMS,
        cost_estimate=pl.CostEstimate(flops=flops, bytes_accessed=int(moved), transcendentals=0),
    )(*smem, *vmem)


def send(array, route):
    sectors, layers = lax.axis_size("azim"), lax.axis_size("block")
    pairs = []
    for s in range(sectors):
        for b in range(layers):
            to = route(s, b)
            if to is not None:
                pairs.append((s * layers + b, to[0] * layers + to[1]))
    return lax.ppermute(array, AXES, pairs)


def off_chip(s, b):
    if b in (0, 7, 8, 15):
        return None
    return (s, b + 1 if b % 2 else b - 1)


def on_chip(s, b):
    return (s, b ^ 1)


def eastward(s, b):
    return ((s + 1) % 16, b)


def westward(s, b):
    return ((s - 1) % 16, b)


def across(turns):
    def route(s, b):
        if b == 7:
            return ((s + turns) % 16, 8)
        if b == 8:
            return ((s - turns) % 16, 7)
        return None

    return route


def beside(s, b):
    return {7: ((s + 1) % 16, 7), 8: ((s - 1) % 16, 8)}.get(b)


def cross_interface(panel, offset):
    branches = [lambda panel, turns=turns: send(panel, across(turns)) for turns in range(16)]
    return lax.switch(lax.shift_right_logical(offset, jnp.int32(7)), branches, panel)


def interpolated(section, ctl, offsets, own, other, expanded):
    return call(
        functools.partial(interface_kernel, section),
        [ctl, offsets],
        [own, other, expanded],
        [WINDOW],
        [pltpu.VMEM((10, 256, 128), jnp.float32)],
    )[0]


def shards(flow_state, jacobians, interp_weights, offsets, live_rows):
    ctl = lax.axis_index("block").astype(jnp.int32).reshape(1)
    smem = [ctl, live_rows, jacobians]
    u = flow_state.reshape(VARS, 16, 4, 2, 8, 128)
    off, on, west, east = call(
        extract_kernel,
        [ctl, live_rows],
        [u],
        [FACE_AND_MASK, FACE_AND_MASK, COLUMNS, COLUMNS],
        EXTRACT_SCRATCH,
        first_any=True,
    )
    other = send(off, beside)
    from_west, from_east = send(east, eastward), send(west, westward)
    off_1 = send(off, off_chip)
    on_1 = send(on, on_chip)
    base_1, off_v, on_v, west, east, expanded = call(
        first_interior_kernel,
        smem,
        [u, from_west, from_east, interp_weights],
        [STATE, FACE, FACE, COLUMNS, COLUMNS, EXPANDED],
        flops=10**8,
    )
    off_2 = send(off_v, off_chip)
    on_2 = send(on_v, on_chip)
    window_1 = cross_interface(interpolated(0, ctl, offsets, off, other, expanded), offsets[0])
    off = call(first_off_kernel, smem, [off_v, off_1, window_1], [FACE])[0]
    other = send(off, beside)
    first, west, east = call(
        first_on_kernel,
        smem,
        [base_1, off, on_v, on_1, west, east],
        [STATE, COLUMNS, COLUMNS],
        [FACE_SCRATCH, STORE_SEMS],
        first_any=True,
        in_place=True,
    )
    from_west, from_east = send(east, eastward), send(west, westward)
    base_2, off_base, on_base = call(
        second_interior_kernel,
        smem,
        [u, from_west, from_east, first, off_1, on_1],
        [STATE, FACE, FACE],
        flops=10**8,
    )
    window_2 = cross_interface(interpolated(1, ctl, offsets, off, other, expanded), offsets[1])
    out = call(
        second_exterior_kernel,
        smem,
        [base_2, off_base, off_2, window_2, on_base, on_2],
        [STATE],
        [FACE_SCRATCH, FACE_SCRATCH, STORE_SEMS],
        first_any=True,
        in_place=True,
    )[0]
    return out.reshape(flow_state.shape)


def solution(mesh):
    placed = (P("block", None, None, None, "azim"), P(), P(), P(), P("block"))
    return jax.shard_map(
        shards,
        mesh=mesh,
        in_specs=placed,
        out_specs=P("block", None, None, None, "azim"),
        check_vma=False,
    )
```

```python
import functools

import jax
import jax.numpy as jnp
import numpy as np
from jax import lax
from jax.experimental import pallas as pl
from jax.experimental.pallas import tpu as pltpu
from jax.sharding import PartitionSpec as P

STEP = 0.04
VARS = 5
TILE = (8, 128)
AXES = ("azim", "block")
VMEM = pl.BlockSpec(memory_space=pltpu.VMEM)
ANY = pl.BlockSpec(memory_space=pl.ANY)
SMEM = pl.BlockSpec(memory_space=pltpu.SMEM)
PARAMS = pltpu.CompilerParams(vmem_limit_bytes=20 * 1024 * 1024)


def derivative_matrix():
    points = np.array([-1.0, -1.0 / np.sqrt(5.0), 1.0 / np.sqrt(5.0), 1.0])
    differ = points[:, None] - points[None, :]
    filled = differ + np.eye(4)
    weights = 1.0 / np.prod(filled, axis=1)
    matrix = weights[None, :] / weights[:, None] / filled
    matrix = matrix * (1.0 - np.eye(4))
    return matrix - np.eye(4) * matrix.sum(axis=1)[:, None]


DM = derivative_matrix()


def lanes():
    return lax.broadcasted_iota(jnp.int32, TILE, 1)


def rows():
    return lax.broadcasted_iota(jnp.int32, TILE, 0)


def splat_matrix(jac_ref, side, k):
    return [[jnp.full(TILE, jac_ref[side, k, w, v], jnp.float32) for v in range(VARS)] for w in range(VARS)]


def bound_of(matrix):
    sums = [functools.reduce(jnp.add, [jnp.abs(e) for e in row]) for row in matrix]
    return functools.reduce(jnp.maximum, sums)


def face_matrix(jac_ref, side, k, orient, scale):
    matrix = splat_matrix(jac_ref, side, k)
    lam = bound_of(matrix)
    factor = jnp.full(TILE, orient, jnp.float32) * (3.0 * scale)
    return [
        [factor * matrix[w][v] + (3.0 * scale) * lam if w == v else factor * matrix[w][v] for v in range(VARS)]
        for w in range(VARS)
    ]


def mix(matrix, z):
    return [functools.reduce(jnp.add, [matrix[w][v] * z[v] for v in range(VARS)]) for w in range(VARS)]


def live_masks(live_ref):
    live = live_ref[0]
    return [(rows() + 8 * h < live).astype(jnp.float32) for h in range(2)]


def put_columns(lane, j, west_tile, east_tile, west, east):
    return (
        jnp.where(lane == j, pltpu.roll(west_tile, j, 1), west),
        jnp.where(lane == j, pltpu.roll(east_tile, j + 1, 1), east),
    )


def split_bf16(x):
    high = x.astype(jnp.bfloat16)
    return high, (x - high.astype(jnp.float32)).astype(jnp.bfloat16)


def extract_kernel(ctl_ref, live_ref, u_ref, off_ref, on_ref, west_ref, east_ref, sides_ref, sems):
    block = ctl_ref[0]
    x_off = 3 * (block % 2)
    copies = [[], [], []]
    for v in range(VARS):
        face = pl.ds(v * 16, 16)
        copies[0].append(pltpu.make_async_copy(u_ref.at[v, :, x_off], off_ref.at[face], sems.at[v]))
        copies[1].append(pltpu.make_async_copy(u_ref.at[v, :, 3 - x_off], on_ref.at[face], sems.at[5 + v]))
        for e in range(2):
            copies[2].append(
                pltpu.make_async_copy(
                    u_ref.at[v, pl.ds(12 * e, 4), pl.ds(1, 2)], sides_ref.at[v, e], sems.at[10 + 2 * v + e]
                )
            )
    for group in copies:
        for copy in group:
            copy.start()
    masks = live_masks(live_ref)
    for h in range(2):
        off_ref[80, h] = masks[h]
        on_ref[80, h] = masks[h]
    for group in copies:
        for copy in group:
            copy.wait()
    lane = lanes()
    for h in range(2):
        west = jnp.zeros(TILE, jnp.float32)
        east = jnp.zeros(TILE, jnp.float32)
        for v in range(VARS):
            for p in range(4):
                for x in (1, 2):
                    j = 16 * v + 4 * p + x
                    west, east = put_columns(
                        lane, j, sides_ref[v, 0, p, x - 1, h], sides_ref[v, 1, p, x - 1, h], west, east
                    )
        west_ref[h] = west
        east_ref[h] = east
    face_columns(ctl_ref, off_ref, on_ref, west_ref, east_ref)


def face_columns(ctl_ref, off_ref, on_ref, west_ref, east_ref):
    x_off = 3 * (ctl_ref[0] % 2)
    lane = lanes()
    for h in range(2):
        west, east = west_ref[h], east_ref[h]
        for x, ref in ((x_off, off_ref), (3 - x_off, on_ref)):
            for v in range(VARS):
                for p in range(4):
                    j = 16 * v + 4 * p + x
                    west, east = put_columns(lane, j, ref[v * 16 + p, h], ref[v * 16 + 12 + p, h], west, east)
        west_ref[h] = west
        east_ref[h] = east


def derivative_terms(u0, u1, u2, u3):
    even = (u0 + u3) - (u1 + u2)
    o, g = u0 - u3, u1 - u2
    a = float(0.5 * (DM[0, 0] + DM[3, 0]))
    b = float(0.5 * (DM[0, 1] + DM[3, 1]))
    c = float(0.5 * (DM[1, 0] + DM[2, 0]))
    d = float(0.5 * (DM[1, 1] + DM[2, 1]))
    outer = (-a) * o - b * g
    inner = (-c) * o - d * g
    outer_even = float(-0.5 * (DM[0, 0] - DM[3, 0])) * even
    inner_even = float(-0.5 * (DM[1, 0] - DM[2, 0])) * even
    return outer + outer_even, inner + inner_even, inner - inner_even, outer - outer_even


def terms(matrix, lam3, z, jumps):
    outs = []
    for node in range(4):
        mixed = mix(matrix, [z[v][node] for v in range(VARS)])
        if node in jumps:
            mixed = [mixed[v] - lam3 * jumps[node][v] for v in range(VARS)]
        outs.append(mixed)
    return outs


def coefficients(ctl_ref, jac_ref, k, scale):
    matrix = splat_matrix(jac_ref, jnp.where(ctl_ref[0] < 8, 0, 1), k)
    lam3 = bound_of(matrix) * (3.0 * scale)
    return [[scale * e for e in r] for r in matrix], lam3


def interior_axis_span(ctl_ref, jac_ref, u_ref, acc_ref, scale):
    row = rows()

    def along_x(matrix, lam3):
        def body(i, carry):
            h, ap = i % 2, i // 2
            z, first, last = [], [], []
            for v in range(VARS):
                u = [u_ref[v, ap, x, h] for x in range(4)]
                d = derivative_terms(*u)
                z.append([d[0] - 3.0 * u[0], d[1], d[2], d[3] + 3.0 * u[3]])
                first.append(u[0])
                last.append(u[3])
            outs = terms(matrix, lam3, z, {0: first, 3: last})
            for x in range(4):
                for v in range(VARS):
                    acc_ref[v, ap, x, h] = outs[x][v]
            return carry

        lax.fori_loop(0, 32, body, 0, unroll=4)

    def along_p(matrix, lam3):
        def body(i, carry):
            a, x = i // 4, i % 4
            for h in range(2):
                z, jump_l, jump_u = [], [], []
                for v in range(VARS):
                    u = [u_ref[v, 4 * a + p, x, h] for p in range(4)]
                    d = derivative_terms(*u)
                    if h == 0:
                        below = jnp.where(row == 0, u[0], pltpu.roll(u[3], 1, 0))
                        other = u_ref[v, 4 * a, x, 1]
                        above = pltpu.roll(jnp.where(row == 0, other, u[0]), 7, 0)
                    else:
                        other = u_ref[v, 4 * a + 3, x, 0]
                        below = pltpu.roll(jnp.where(row == 7, other, u[3]), 1, 0)
                        above = jnp.where(row == 7, u[3], pltpu.roll(u[0], 7, 0))
                    lower, upper = u[0] - below, u[3] - above
                    z.append([d[0] - 3.0 * lower, d[1], d[2], d[3] + 3.0 * upper])
                    jump_l.append(lower)
                    jump_u.append(upper)
                outs = terms(matrix, lam3, z, {0: jump_l, 3: jump_u})
                for p in range(4):
                    for v in range(VARS):
                        acc_ref[v, 4 * a + p, x, h] += outs[p][v]
            return carry

        lax.fori_loop(0, 16, body, 0, unroll=2)

    along_x(*coefficients(ctl_ref, jac_ref, 2, scale))
    along_p(*coefficients(ctl_ref, jac_ref, 1, scale))


def interior_azimuth(ctl_ref, live_ref, jac_ref, u_ref, acc_ref, west_ref, east_ref, out_ref, scale, base, done):
    lane = lanes()
    matrix, lam3 = coefficients(ctl_ref, jac_ref, 0, scale)
    live = live_ref[0]

    def one_p(p, carry):
        def body(i, carry):
            h, x = i % 2, i // 2
            n = 4 * p + x
            mask = (rows() + 8 * h < live).astype(jnp.float32)
            halo_w, halo_e = west_ref[h], east_ref[h]
            z, jump_w, jump_e = [], [], []
            for v in range(VARS):
                u = [u_ref[v, 4 * a + p, x, h] for a in range(4)]
                d = derivative_terms(*u)
                from_w = pltpu.roll(halo_w, (128 - 16 * v - n) % 128, 1)
                from_e = pltpu.roll(halo_e, 127 - 16 * v - n, 1)
                west = u[0] - jnp.where(lane == 0, from_w, pltpu.roll(u[3], 1, 1))
                east = u[3] - jnp.where(lane == 127, from_e, pltpu.roll(u[0], 127, 1))
                z.append([d[0] - 3.0 * west, d[1], d[2], d[3] + 3.0 * east])
                jump_w.append(west)
                jump_e.append(east)
            outs = terms(matrix, lam3, z, {0: jump_w, 3: jump_e})
            for a in range(4):
                for v in range(VARS):
                    ap = 4 * a + p
                    out_ref[v, ap, x, h] = base(v, ap, x, h) + mask * (acc_ref[v, ap, x, h] + outs[a][v])
            return carry

        lax.fori_loop(0, 8, body, 0, unroll=4)
        done(p)
        return carry

    lax.fori_loop(0, 4, one_p, 0)


def axis_span_kernel(scale, ctl_ref, jac_ref, u_ref, acc_ref):
    interior_axis_span(ctl_ref, jac_ref, u_ref, acc_ref, scale)


def expanded_weights(turn, weight_ref, out_ref):
    parts = []
    for section in range(2):
        for i in range(2):
            high, low = split_bf16(weight_ref[section, i])
            parts += [high.astype(jnp.float32), low.astype(jnp.float32)]
    spread = lax.broadcasted_iota(jnp.int32, (128, 16), 0) // 8 == lax.broadcasted_iota(jnp.int32, (128, 16), 1)
    spread = spread.astype(jnp.bfloat16)

    def dot(a, b, dims):
        return lax.dot_general(
            a.astype(jnp.bfloat16), b.astype(jnp.bfloat16), (dims, ((), ())), preferred_element_type=jnp.float32
        )

    plain = dot(spread, jnp.concatenate(parts, axis=1), ((1,), (0,)))
    turned = dot(spread, jnp.concatenate(parts, axis=0), ((1,), (1,)))
    picked = jnp.where(turn, turned, plain)
    row = lax.broadcasted_iota(jnp.int32, (128, 1024), 0)
    col = lax.broadcasted_iota(jnp.int32, (128, 1024), 1)
    widen = (row == 16 * (col // 128) + (col % 128) // 8).astype(jnp.bfloat16)
    wide = dot(picked, widen, ((1,), (0,)))
    wide = jnp.where(row % 8 == col % 8, wide, 0.0).astype(jnp.bfloat16)
    for section in range(2):
        near_high, near_low, far_high, far_low = [
            wide[:, 128 * (4 * section + k) : 128 * (4 * section + k + 1)] for k in range(4)
        ]
        high = jnp.concatenate([near_high, far_high], axis=1)
        low = jnp.concatenate([near_low, far_low], axis=1)
        out_ref[section] = jnp.concatenate([high, low], axis=0)


def first_azimuth_kernel(ctl_ref, live_ref, jac_ref, u_ref, acc_ref, west_ref, east_ref, weight_ref,
                         out_ref, off_ref, on_ref, new_west_ref, new_east_ref, expanded_ref):
    block = ctl_ref[0]
    interior_azimuth(
        ctl_ref, live_ref, jac_ref, u_ref, acc_ref, west_ref, east_ref, out_ref, STEP,
        lambda v, ap, x, h: u_ref[v, ap, x, h], lambda p: None,
    )
    x_off = 3 * (block % 2)

    def body(ap, carry):
        for v in range(VARS):
            off_ref[v * 16 + ap] = out_ref[v, ap, x_off]
            on_ref[v * 16 + ap] = out_ref[v, ap, 3 - x_off]
        return carry

    lax.fori_loop(0, 16, body, 0)
    lane = lanes()
    for h in range(2):
        west = jnp.zeros(TILE, jnp.float32)
        east = jnp.zeros(TILE, jnp.float32)
        for v in range(VARS):
            for p in range(4):
                for x in (1, 2):
                    j = 16 * v + 4 * p + x
                    west, east = put_columns(lane, j, out_ref[v, p, x, h], out_ref[v, 12 + p, x, h], west, east)
        new_west_ref[h] = west
        new_east_ref[h] = east

    @pl.when((block == 7) | (block == 8))
    def _():
        expanded_weights(block >= 8, weight_ref, expanded_ref)


def second_azimuth_kernel(ctl_ref, live_ref, jac_ref, first_ref, acc_ref, west_ref, east_ref, u_ref, off_mask_ref,
                          on_mask_ref, state_ref, off_ref, on_ref, out_ref, sems):
    def store(p):
        return [
            pltpu.make_async_copy(out_ref.at[:, 4 * a + p], state_ref.at[:, 4 * a + p], sems.at[p, a])
            for a in range(4)
        ]

    def done(p):
        for copy in store(p):
            copy.start()

    interior_azimuth(
        ctl_ref, live_ref, jac_ref, first_ref, acc_ref, west_ref, east_ref, out_ref, 0.5 * STEP,
        lambda v, ap, x, h: 0.5 * u_ref[v, ap, x, h] + 0.5 * first_ref[v, ap, x, h], done,
    )
    block = ctl_ref[0]
    side = jnp.where(block < 8, 0, 1)
    x_off = 3 * (block % 2)
    masks = live_masks(live_ref)
    jac = splat_matrix(jac_ref, side, 2)
    lam = bound_of(jac)
    factor = 0.5 * (3.0 * STEP) ** 2
    matrix = []
    for w in range(VARS):
        line = []
        for v in range(VARS):
            square = functools.reduce(jnp.add, [jac[w][k] * jac[k][v] for k in range(VARS)])
            line.append(factor * (lam * lam - square) if w == v else -factor * square)
        matrix.append(line)
    for x, mask_ref, face_ref in ((x_off, off_mask_ref, off_ref), (3 - x_off, on_mask_ref, on_ref)):
        both = [masks[h] * mask_ref[80, h] for h in range(2)]
        if mask_ref is off_mask_ref:
            early = jnp.where((block == 7) | (block == 8), 0.0, 1.0)
            both = [early * b for b in both]

        def body(ap, carry, x=x, both=both, face_ref=face_ref):
            for h in range(2):
                mixed = mix(matrix, [u_ref[v, ap, x, h] for v in range(VARS)])
                for v in range(VARS):
                    face_ref[v * 16 + ap, h] = out_ref[v, ap, x, h] + both[h] * mixed[v]
            return carry

        lax.fori_loop(0, 16, body, 0, unroll=2)
    for p in range(4):
        for copy in store(p):
            copy.wait()


def interface_kernel(section, ctl_ref, offset_ref, own_ref, next_ref, weight_ref, out_ref, near_ref):
    block = ctl_ref[0]

    @pl.when((block == 7) | (block == 8))
    def _():
        rotor = block < 8
        within = lax.rem(offset_ref[section], 128)
        lane = lanes()

        def pick(own, other, amount):
            start = jnp.where(rotor, 128 - amount, 0)
            sent = (lane >= start) & (lane < start + amount)
            turn = lax.rem(jnp.where(rotor, amount, 128 - amount), 128)
            return pltpu.roll(jnp.where(sent, other, own), turn, 1)

        def body(ap, carry):
            place = pl.multiple_of(8 * ap, 8)
            for v in range(VARS):
                for h in range(2):
                    own, other = own_ref[v * 16 + ap, h], next_ref[v * 16 + ap, h]
                    near_ref[2 * v + h, pl.ds(place, 8), :] = pick(own, other, within)
                    near_ref[2 * v + h, pl.ds(place + 128, 8), :] = pick(own, other, within + 1)
            return carry

        lax.fori_loop(0, 16, body, 0, unroll=2)
        w_both = weight_ref[section]
        for v in range(VARS):
            both = jnp.concatenate([near_ref[2 * v], near_ref[2 * v + 1]], axis=1)
            high, low = split_bf16(both)
            first = jnp.dot(w_both, high, preferred_element_type=jnp.float32)
            total = first[:128] + first[128:] + jnp.dot(w_both[:128], low, preferred_element_type=jnp.float32)
            out_ref[2 * v] = total[:, :128]
            out_ref[2 * v + 1] = total[:, 128:]


def off_face(ctl_ref, live_ref, jac_ref, base_ref, ext_ref, window_ref, out_ref, scale):
    block = ctl_ref[0]
    odd = block % 2
    masks = live_masks(live_ref)
    matrix = face_matrix(
        jac_ref, jnp.where(block < 8, 0, 1), 2, jnp.where(odd == 0, 1.0, -1.0), scale
    )
    interface = (block == 7) | (block == 8)

    def run(load):
        def body(ap, carry):
            for h in range(2):
                mixed = mix(matrix, [load(v, ap, h) for v in range(VARS)])
                for v in range(VARS):
                    out_ref[v * 16 + ap, h] = base_ref[v * 16 + ap, h] + masks[h] * mixed[v]
            return carry

        lax.fori_loop(0, 16, body, 0, unroll=2)

    @pl.when(interface)
    def _():
        run(lambda v, ap, h: window_ref[2 * v + h, pl.ds(pl.multiple_of(8 * ap, 8), 8), :])

    @pl.when(jnp.logical_not(interface))
    def _():
        run(lambda v, ap, h: ext_ref[v * 16 + ap, h])


def on_face(ctl_ref, live_ref, jac_ref, base_ref, ext_ref, out_ref, scale):
    block = ctl_ref[0]
    masks = live_masks(live_ref)
    matrix = face_matrix(
        jac_ref, jnp.where(block < 8, 0, 1), 2, jnp.where(block % 2 == 0, -1.0, 1.0), scale
    )

    def body(ap, carry):
        for h in range(2):
            mixed = mix(matrix, [ext_ref[v * 16 + ap, h] for v in range(VARS)])
            for v in range(VARS):
                out_ref[v * 16 + ap, h] = base_ref[v * 16 + ap, h] + masks[h] * mixed[v]
        return carry

    lax.fori_loop(0, 16, body, 0, unroll=2)


def face_stores(face_ref, out_ref, x, sems):
    return [
        pltpu.make_async_copy(face_ref.at[pl.ds(16 * v, 16)], out_ref.at[v, :, x], sems.at[v])
        for v in range(VARS)
    ]


def first_off_kernel(ctl_ref, live_ref, jac_ref, base_ref, ext_ref, window_ref, out_ref):
    off_face(ctl_ref, live_ref, jac_ref, base_ref, ext_ref, window_ref, out_ref, STEP)


def first_on_kernel(ctl_ref, live_ref, jac_ref, state_ref, off_ref, base_ref, ext_ref, west_ref, east_ref,
                    out_ref, new_west_ref, new_east_ref, on_ref, sems):
    x_off = 3 * (ctl_ref[0] % 2)
    stores = face_stores(off_ref, out_ref, x_off, sems.at[0])
    for copy in stores:
        copy.start()
    on_face(ctl_ref, live_ref, jac_ref, base_ref, ext_ref, on_ref, STEP)
    more = face_stores(on_ref, out_ref, 3 - x_off, sems.at[1])
    for copy in more:
        copy.start()
    new_west_ref[...] = west_ref[...]
    new_east_ref[...] = east_ref[...]
    face_columns(ctl_ref, off_ref, on_ref, new_west_ref, new_east_ref)
    for copy in stores + more:
        copy.wait()


def second_exterior_kernel(ctl_ref, live_ref, jac_ref, state_ref, off_base_ref, off_ext_ref, window_ref, on_base_ref,
                           on_ext_ref, out_ref, off_ref, on_ref, sems):
    x_off = 3 * (ctl_ref[0] % 2)
    on_face(ctl_ref, live_ref, jac_ref, on_base_ref, on_ext_ref, on_ref, 0.5 * STEP)
    stores = face_stores(on_ref, out_ref, 3 - x_off, sems.at[0])
    for copy in stores:
        copy.start()
    off_face(ctl_ref, live_ref, jac_ref, off_base_ref, off_ext_ref, window_ref, off_ref, 0.5 * STEP)
    more = face_stores(off_ref, out_ref, x_off, sems.at[1])
    for copy in more:
        copy.start()
    for copy in stores + more:
        copy.wait()


def shape(*dims):
    return jax.ShapeDtypeStruct(dims, jnp.float32)


STATE = shape(VARS, 16, 4, 2, 8, 128)
FACE = shape(80, 2, 8, 128)
FACE_AND_MASK = shape(81, 2, 8, 128)
COLUMNS = shape(2, 8, 128)
EXPANDED = jax.ShapeDtypeStruct((2, 256, 256), jnp.bfloat16)
WINDOW = shape(10, 128, 128)
FACE_SCRATCH = pltpu.VMEM((80, 2, 8, 128), jnp.float32)
STATE_SCRATCH = pltpu.VMEM((VARS, 16, 4, 2, 8, 128), jnp.float32)
STORE_SEMS = pltpu.SemaphoreType.DMA((2, VARS))
EXTRACT_SCRATCH = [pltpu.VMEM((VARS, 2, 4, 2, 2, 8, 128), jnp.float32), pltpu.SemaphoreType.DMA((20,))]


def call(kernel, smem, vmem, outs, scratch=(), flops=10**7, first_any=False, out_any=False, in_place=False):
    moved = sum(4 * a.size for a in vmem) + sum(4 * np.prod(o.shape) for o in outs)
    return pl.pallas_call(
        kernel,
        in_specs=[SMEM] * len(smem) + [ANY if first_any else VMEM] + [VMEM] * (len(vmem) - 1),
        out_specs=[ANY if in_place or out_any else VMEM] + [VMEM] * (len(outs) - 1),
        out_shape=list(outs),
        scratch_shapes=list(scratch),
        input_output_aliases={len(smem): 0} if in_place else {},
        compiler_params=PARAMS,
        cost_estimate=pl.CostEstimate(flops=flops, bytes_accessed=int(moved), transcendentals=0),
    )(*smem, *vmem)


def send(array, route):
    sectors, layers = lax.axis_size("azim"), lax.axis_size("block")
    pairs = []
    for s in range(sectors):
        for b in range(layers):
            to = route(s, b)
            if to is not None:
                pairs.append((s * layers + b, to[0] * layers + to[1]))
    return lax.ppermute(array, AXES, pairs)


def off_chip(s, b):
    if b in (0, 7, 8, 15):
        return None
    return (s, b + 1 if b % 2 else b - 1)


def off_chip_or_beside(s, b):
    return beside(s, b) or off_chip(s, b)


def on_chip(s, b):
    return (s, b ^ 1)


def eastward(s, b):
    return ((s + 1) % 16, b)


def westward(s, b):
    return ((s - 1) % 16, b)


def across(turns):
    def route(s, b):
        if b == 7:
            return ((s + turns) % 16, 8)
        if b == 8:
            return ((s - turns) % 16, 7)
        return None

    return route


def beside(s, b):
    return {7: ((s + 1) % 16, 7), 8: ((s - 1) % 16, 8)}.get(b)


def cross_interface(panel, offset):
    branches = [lambda panel, turns=turns: send(panel, across(turns)) for turns in range(16)]
    return lax.switch(lax.shift_right_logical(offset, jnp.int32(7)), branches, panel)


def interpolated(section, ctl, offsets, own, other, expanded):
    return call(
        functools.partial(interface_kernel, section),
        [ctl, offsets],
        [own, other, expanded],
        [WINDOW],
        [pltpu.VMEM((10, 256, 128), jnp.float32)],
    )[0]


def shards(flow_state, jacobians, interp_weights, offsets, live_rows):
    ctl = lax.axis_index("block").astype(jnp.int32).reshape(1)
    smem = [ctl, live_rows, jacobians]
    u = flow_state.reshape(VARS, 16, 4, 2, 8, 128)
    off, on, west, east = call(
        extract_kernel,
        [ctl, live_rows],
        [u],
        [FACE_AND_MASK, FACE_AND_MASK, COLUMNS, COLUMNS],
        EXTRACT_SCRATCH,
        first_any=True,
    )
    off_1 = send(off, off_chip_or_beside)
    from_west, from_east = send(east, eastward), send(west, westward)
    on_1 = send(on, on_chip)
    acc = call(functools.partial(axis_span_kernel, STEP), [ctl, jacobians], [u], [STATE], flops=10**8)[0]
    base_1, off_v, on_v, west, east, expanded = call(
        first_azimuth_kernel,
        smem,
        [u, acc, from_west, from_east, interp_weights],
        [STATE, FACE, FACE, COLUMNS, COLUMNS, EXPANDED],
        flops=10**8,
    )
    off_2 = send(off_v, off_chip)
    on_2 = send(on_v, on_chip)
    window_1 = cross_interface(interpolated(0, ctl, offsets, off, off_1, expanded), offsets[0])
    off = call(first_off_kernel, smem, [off_v, off_1, window_1], [FACE])[0]
    other = send(off, beside)
    first, west, east = call(
        first_on_kernel,
        smem,
        [base_1, off, on_v, on_1, west, east],
        [STATE, COLUMNS, COLUMNS],
        [FACE_SCRATCH, STORE_SEMS],
        first_any=True,
        in_place=True,
    )
    from_west, from_east = send(east, eastward), send(west, westward)
    acc = call(functools.partial(axis_span_kernel, 0.5 * STEP), [ctl, jacobians], [first], [STATE], flops=10**8)[0]
    base_2, off_base, on_base = call(
        second_azimuth_kernel,
        smem,
        [first, acc, from_west, from_east, u, off_1, on_1],
        [STATE, FACE, FACE],
        [STATE_SCRATCH, pltpu.SemaphoreType.DMA((4, 4))],
        flops=10**8,
        out_any=True,
    )
    window_2 = cross_interface(interpolated(1, ctl, offsets, off, other, expanded), offsets[1])
    out = call(
        second_exterior_kernel,
        smem,
        [base_2, off_base, off_2, window_2, on_base, on_2],
        [STATE],
        [FACE_SCRATCH, FACE_SCRATCH, STORE_SEMS],
        first_any=True,
        in_place=True,
    )[0]
    return out.reshape(flow_state.shape)


def solution(mesh):
    placed = (P("block", None, None, None, "azim"), P(), P(), P(), P("block"))
    return jax.shard_map(
        shards,
        mesh=mesh,
        in_specs=placed,
        out_specs=P("block", None, None, None, "azim"),
        check_vma=False,
    )
```

```python
import functools

import jax
import jax.numpy as jnp
import numpy as np
from jax import lax
from jax.experimental import pallas as pl
from jax.experimental.pallas import tpu as pltpu
from jax.sharding import PartitionSpec as P

STEP = 0.04
VARS = 5
TILE = (8, 128)
AXES = ("azim", "block")
VMEM = pl.BlockSpec(memory_space=pltpu.VMEM)
HBM = pl.BlockSpec(memory_space=pltpu.HBM)
SMEM = pl.BlockSpec(memory_space=pltpu.SMEM)
PARAMS = pltpu.CompilerParams(vmem_limit_bytes=20 * 1024 * 1024)


def derivative_matrix():
    points = np.array([-1.0, -1.0 / np.sqrt(5.0), 1.0 / np.sqrt(5.0), 1.0])
    differ = points[:, None] - points[None, :]
    filled = differ + np.eye(4)
    weights = 1.0 / np.prod(filled, axis=1)
    matrix = weights[None, :] / weights[:, None] / filled
    matrix = matrix * (1.0 - np.eye(4))
    return matrix - np.eye(4) * matrix.sum(axis=1)[:, None]


DM = derivative_matrix()


def lanes():
    return lax.broadcasted_iota(jnp.int32, TILE, 1)


def rows():
    return lax.broadcasted_iota(jnp.int32, TILE, 0)


def splat_matrix(jac_ref, side, k):
    return [[jnp.full(TILE, jac_ref[k, w, side, v], jnp.float32) for v in range(VARS)] for w in range(VARS)]


def bound_of(matrix):
    sums = [functools.reduce(jnp.add, [jnp.abs(e) for e in row]) for row in matrix]
    return functools.reduce(jnp.maximum, sums)


def face_matrix(jac_ref, side, k, orient, scale):
    matrix = splat_matrix(jac_ref, side, k)
    lam = bound_of(matrix)
    factor = jnp.full(TILE, orient, jnp.float32) * (3.0 * scale)
    return [
        [factor * matrix[w][v] + (3.0 * scale) * lam if w == v else factor * matrix[w][v] for v in range(VARS)]
        for w in range(VARS)
    ]


def mix(matrix, z):
    return [functools.reduce(jnp.add, [matrix[w][v] * z[v] for v in range(VARS)]) for w in range(VARS)]


def live_masks(live_ref):
    live = live_ref[0]
    return [(rows() + 8 * h < live).astype(jnp.float32) for h in range(2)]


def put_columns(lane, j, west_tile, east_tile, west, east):
    return (
        jnp.where(lane == j, pltpu.roll(west_tile, j, 1), west),
        jnp.where(lane == j, pltpu.roll(east_tile, j + 1, 1), east),
    )


def split_bf16(x):
    high = x.astype(jnp.bfloat16)
    return high, (x - high.astype(jnp.float32)).astype(jnp.bfloat16)


def extract_kernel(ctl_ref, offset_ref, u_ref, off_ref, on_ref, west_ref, east_ref, turn_0_ref, turn_1_ref,
                   sides_ref, sems):
    x_off = 3 * (ctl_ref[0] % 2)
    copies = []
    for v in range(VARS):
        face = pl.ds(v * 16, 16)
        copies.append(pltpu.make_async_copy(u_ref.at[v, :, x_off], off_ref.at[face], sems.at[v]))
        copies.append(pltpu.make_async_copy(u_ref.at[v, :, 3 - x_off], on_ref.at[face], sems.at[5 + v]))
        for e in range(2):
            copies.append(
                pltpu.make_async_copy(
                    u_ref.at[v, pl.ds(12 * e, 4), pl.ds(1, 2)], sides_ref.at[v, e], sems.at[10 + 2 * v + e]
                )
            )
    for copy in copies:
        copy.start()
    turn_0_ref[0] = lax.shift_right_logical(offset_ref[0], 7)
    turn_1_ref[0] = lax.shift_right_logical(offset_ref[1], 7)
    for copy in copies:
        copy.wait()
    middle_columns(lambda v, e, p, x, h: sides_ref[v, e, p, x - 1, h], west_ref, east_ref)
    face_columns(off_ref, x_off, west_ref, east_ref)
    face_columns(on_ref, 3 - x_off, west_ref, east_ref)


def middle_columns(tile, west_ref, east_ref):
    lane = lanes()
    for h in range(2):
        west = jnp.zeros(TILE, jnp.float32)
        east = jnp.zeros(TILE, jnp.float32)
        for v in range(VARS):
            for p in range(4):
                for x in (1, 2):
                    west, east = put_columns(
                        lane, 16 * v + 4 * p + x, tile(v, 0, p, x, h), tile(v, 1, p, x, h), west, east
                    )
        west_ref[h] = west
        east_ref[h] = east


def face_columns(face_ref, x, west_ref, east_ref):
    lane = lanes()
    for h in range(2):
        west, east = west_ref[h], east_ref[h]
        for v in range(VARS):
            for p in range(4):
                west, east = put_columns(
                    lane, 16 * v + 4 * p + x, face_ref[v * 16 + p, h], face_ref[v * 16 + 12 + p, h], west, east
                )
        west_ref[h] = west
        east_ref[h] = east


def derivative_terms(u0, u1, u2, u3):
    even = (u0 + u3) - (u1 + u2)
    o, g = u0 - u3, u1 - u2
    a = float(0.5 * (DM[0, 0] + DM[3, 0]))
    b = float(0.5 * (DM[0, 1] + DM[3, 1]))
    c = float(0.5 * (DM[1, 0] + DM[2, 0]))
    d = float(0.5 * (DM[1, 1] + DM[2, 1]))
    outer = (-a) * o - b * g
    inner = (-c) * o - d * g
    outer_even = float(-0.5 * (DM[0, 0] - DM[3, 0])) * even
    inner_even = float(-0.5 * (DM[1, 0] - DM[2, 0])) * even
    return outer + outer_even, inner + inner_even, inner - inner_even, outer - outer_even


def terms(matrix, lam3, z, jumps):
    outs = []
    for node in range(4):
        mixed = mix(matrix, [z[v][node] for v in range(VARS)])
        if node in jumps:
            mixed = [mixed[v] - lam3 * jumps[node][v] for v in range(VARS)]
        outs.append(mixed)
    return outs


def coefficients(ctl_ref, jac_ref, k, scale):
    matrix = splat_matrix(jac_ref, jnp.where(ctl_ref[0] < 8, 0, 1), k)
    lam3 = bound_of(matrix) * (3.0 * scale)
    return [[scale * e for e in r] for r in matrix], lam3


def interior_axis_span(ctl_ref, jac_ref, u_ref, acc_ref, scale, before):
    row = rows()

    def along_x(matrix, lam3):
        def one_a(a, carry):
            before(a)

            def body(i, carry):
                h, ap = i % 2, 4 * a + i // 2
                z, first, last = [], [], []
                for v in range(VARS):
                    u = [u_ref[v, ap, x, h] for x in range(4)]
                    d = derivative_terms(*u)
                    z.append([d[0] - 3.0 * u[0], d[1], d[2], d[3] + 3.0 * u[3]])
                    first.append(u[0])
                    last.append(u[3])
                outs = terms(matrix, lam3, z, {0: first, 3: last})
                for x in range(4):
                    for v in range(VARS):
                        acc_ref[v, ap, x, h] = outs[x][v]
                return carry

            lax.fori_loop(0, 8, body, 0, unroll=2)
            return carry

        lax.fori_loop(0, 4, one_a, 0)

    def along_p(matrix, lam3):
        def body(i, carry):
            a, x = i // 4, i % 4
            for h in range(2):
                z, jump_l, jump_u = [], [], []
                for v in range(VARS):
                    u = [u_ref[v, 4 * a + p, x, h] for p in range(4)]
                    d = derivative_terms(*u)
                    if h == 0:
                        below = jnp.where(row == 0, u[0], pltpu.roll(u[3], 1, 0))
                        other = u_ref[v, 4 * a, x, 1]
                        above = pltpu.roll(jnp.where(row == 0, other, u[0]), 7, 0)
                    else:
                        other = u_ref[v, 4 * a + 3, x, 0]
                        below = pltpu.roll(jnp.where(row == 7, other, u[3]), 1, 0)
                        above = jnp.where(row == 7, u[3], pltpu.roll(u[0], 7, 0))
                    lower, upper = u[0] - below, u[3] - above
                    z.append([d[0] - 3.0 * lower, d[1], d[2], d[3] + 3.0 * upper])
                    jump_l.append(lower)
                    jump_u.append(upper)
                outs = terms(matrix, lam3, z, {0: jump_l, 3: jump_u})
                for p in range(4):
                    for v in range(VARS):
                        acc_ref[v, 4 * a + p, x, h] += outs[p][v]
            return carry

        lax.fori_loop(0, 16, body, 0, unroll=2)

    along_x(*coefficients(ctl_ref, jac_ref, 2, scale))
    along_p(*coefficients(ctl_ref, jac_ref, 1, scale))


def interior_azimuth(ctl_ref, live_ref, jac_ref, u_ref, acc_ref, west_ref, east_ref, out_ref, scale, base, done):
    lane = lanes()
    matrix, lam3 = coefficients(ctl_ref, jac_ref, 0, scale)
    live = live_ref[0]
    x_off = 3 * (ctl_ref[0] % 2)

    def one_x(step, carry):
        x = jnp.where(step == 0, x_off, jnp.where(step == 3, 3 - x_off, step))

        def body(i, carry):
            h, p = i % 2, i // 2
            n = 4 * p + x
            mask = (rows() + 8 * h < live).astype(jnp.float32)
            halo_w, halo_e = west_ref[h], east_ref[h]
            z, jump_w, jump_e = [], [], []
            for v in range(VARS):
                u = [u_ref[v, 4 * a + p, x, h] for a in range(4)]
                d = derivative_terms(*u)
                from_w = pltpu.roll(halo_w, (128 - 16 * v - n) % 128, 1)
                from_e = pltpu.roll(halo_e, 127 - 16 * v - n, 1)
                west = u[0] - jnp.where(lane == 0, from_w, pltpu.roll(u[3], 1, 1))
                east = u[3] - jnp.where(lane == 127, from_e, pltpu.roll(u[0], 127, 1))
                z.append([d[0] - 3.0 * west, d[1], d[2], d[3] + 3.0 * east])
                jump_w.append(west)
                jump_e.append(east)
            outs = terms(matrix, lam3, z, {0: jump_w, 3: jump_e})
            for a in range(4):
                for v in range(VARS):
                    ap = 4 * a + p
                    out_ref[v, ap, x, h] = base(v, ap, x, h) + mask * (acc_ref[v, ap, x, h] + outs[a][v])
            return carry

        lax.fori_loop(0, 8, body, 0, unroll=4)
        done(step, x)
        return carry

    lax.fori_loop(0, 4, one_x, 0)


def plane_copies(source, target, x, sems):
    return [pltpu.make_async_copy(source.at[v, :, x], target.at[v, :, x], sems.at[v]) for v in range(VARS)]


def azimuth_and_on_face(ctl_ref, live_ref, jac_ref, u_ref, acc_ref, west_ref, east_ref, on_ext_ref, state_ref,
                        out_ref, ext_ref, sems, ext_sem, scale, base, on_ref=None):
    block = ctl_ref[0]
    x_on = 3 - 3 * (block % 2)
    load = pltpu.make_async_copy(on_ext_ref, ext_ref, ext_sem)
    load.start()

    def done(step, x):
        @pl.when(step == 3)
        def _():
            load.wait()
            masks = live_masks(live_ref)
            orient = jnp.where(block % 2 == 0, -1.0, 1.0)
            matrix = face_matrix(jac_ref, jnp.where(block < 8, 0, 1), 2, orient, scale)

            def body(ap, carry):
                for h in range(2):
                    mixed = mix(matrix, [ext_ref[v * 16 + ap, h] for v in range(VARS)])
                    for v in range(VARS):
                        total = out_ref[v, ap, x, h] + masks[h] * mixed[v]
                        out_ref[v, ap, x, h] = total
                        if on_ref is not None:
                            on_ref[v * 16 + ap, h] = total
                return carry

            lax.fori_loop(0, 16, body, 0, unroll=2)

        for copy in plane_copies(out_ref, state_ref, x, sems.at[step]):
            copy.start()

    interior_azimuth(
        ctl_ref, live_ref, jac_ref, u_ref, acc_ref, west_ref, east_ref, out_ref, scale, base, done
    )

    def finish():
        for step, x in enumerate((3 - x_on, 1, 2, x_on)):
            for copy in plane_copies(out_ref, state_ref, x, sems.at[step]):
                copy.wait()

    return finish


def axis_span_kernel(ctl_ref, jac_ref, u_ref, acc_ref):
    interior_axis_span(ctl_ref, jac_ref, u_ref, acc_ref, STEP, lambda a: None)


def second_axis_span_kernel(ctl_ref, jac_ref, state_ref, off_ref, first_ref, acc_ref, sems):
    x_off = 3 * (ctl_ref[0] % 2)

    def load(a):
        part = pl.ds(4 * a, 4)
        return pltpu.make_async_copy(state_ref.at[:, part], first_ref.at[:, part], sems.at[a])

    for a in range(4):
        load(a).start()

    def before(a):
        load(a).wait()
        for v in range(VARS):
            for p in range(4):
                ap = 4 * a + p
                first_ref[v, ap, x_off] = off_ref[v * 16 + ap]

    interior_axis_span(ctl_ref, jac_ref, first_ref, acc_ref, 0.5 * STEP, before)


def expanded_weights(turn, weight_ref, out_ref):
    parts = []
    for section in range(2):
        for i in range(2):
            high, low = split_bf16(weight_ref[section, i])
            parts += [high.astype(jnp.float32), low.astype(jnp.float32)]
    spread = lax.broadcasted_iota(jnp.int32, (128, 16), 0) // 8 == lax.broadcasted_iota(jnp.int32, (128, 16), 1)
    spread = spread.astype(jnp.bfloat16)

    def dot(a, b, dims):
        return lax.dot_general(
            a.astype(jnp.bfloat16), b.astype(jnp.bfloat16), (dims, ((), ())), preferred_element_type=jnp.float32
        )

    plain = dot(spread, jnp.concatenate(parts, axis=1), ((1,), (0,)))
    turned = dot(spread, jnp.concatenate(parts, axis=0), ((1,), (1,)))
    picked = jnp.where(turn, turned, plain)
    row = lax.broadcasted_iota(jnp.int32, (128, 1024), 0)
    col = lax.broadcasted_iota(jnp.int32, (128, 1024), 1)
    widen = (row == 16 * (col // 128) + (col % 128) // 8).astype(jnp.bfloat16)
    wide = dot(picked, widen, ((1,), (0,)))
    wide = jnp.where(row % 8 == col % 8, wide, 0.0).astype(jnp.bfloat16)
    for section in range(2):
        near_high, near_low, far_high, far_low = [
            wide[:, 128 * (4 * section + k) : 128 * (4 * section + k + 1)] for k in range(4)
        ]
        high = jnp.concatenate([near_high, far_high], axis=1)
        low = jnp.concatenate([near_low, far_low], axis=1)
        out_ref[section] = jnp.concatenate([high, low], axis=0)


def first_azimuth_kernel(ctl_ref, live_ref, jac_ref, u_ref, acc_ref, west_ref, east_ref, weight_ref, on_ext_ref,
                         state_ref, on_ref, new_west_ref, new_east_ref, near_ref, later_ref,
                         out_ref, ext_ref, expanded_ref, sems, ext_sems):
    block = ctl_ref[0]
    finish = azimuth_and_on_face(
        ctl_ref, live_ref, jac_ref, u_ref, acc_ref, west_ref, east_ref, on_ext_ref, state_ref,
        out_ref, ext_ref, sems, ext_sems.at[0], STEP, lambda v, ap, x, h: u_ref[v, ap, x, h], on_ref,
    )
    middle_columns(lambda v, e, p, x, h: out_ref[v, 12 * e + p, x, h], new_west_ref, new_east_ref)
    face_columns(on_ref, 3 - 3 * (block % 2), new_west_ref, new_east_ref)

    @pl.when((block == 7) | (block == 8))
    def _():
        expanded_weights(block >= 8, weight_ref, expanded_ref)
        stores = [
            pltpu.make_async_copy(expanded_ref.at[i], ref, ext_sems.at[1 + i])
            for i, ref in enumerate((near_ref, later_ref))
        ]
        for copy in stores:
            copy.start()
        for copy in stores:
            copy.wait()

    finish()


def second_azimuth_kernel(ctl_ref, live_ref, jac_ref, first_ref, acc_ref, west_ref, east_ref, u_ref, on_ext_ref,
                          state_ref, out_ref, ext_ref, sems, ext_sems):
    finish = azimuth_and_on_face(
        ctl_ref, live_ref, jac_ref, first_ref, acc_ref, west_ref, east_ref, on_ext_ref, state_ref,
        out_ref, ext_ref, sems, ext_sems.at[0], 0.5 * STEP,
        lambda v, ap, x, h: 0.5 * u_ref[v, ap, x, h] + 0.5 * first_ref[v, ap, x, h],
    )
    finish()


def interface_kernel(section, ctl_ref, offset_ref, own_ref, next_hbm_ref, weight_hbm_ref, out_ref,
                     next_ref, weight_ref, near_ref, sems):
    block = ctl_ref[0]

    @pl.when((block == 7) | (block == 8))
    def _():
        loads = [
            pltpu.make_async_copy(
                next_hbm_ref.at[pl.ds(16 * v, 16)], next_ref.at[pl.ds(16 * v, 16)], sems.at[v]
            )
            for v in range(VARS)
        ]
        loads.append(pltpu.make_async_copy(weight_hbm_ref, weight_ref, sems.at[VARS]))
        for copy in loads:
            copy.start()
        rotor = block < 8
        within = lax.rem(offset_ref[section], 128)
        lane = lanes()

        def pick(own, other, amount):
            start = jnp.where(rotor, 128 - amount, 0)
            sent = (lane >= start) & (lane < start + amount)
            turn = lax.rem(jnp.where(rotor, amount, 128 - amount), 128)
            return pltpu.roll(jnp.where(sent, other, own), turn, 1)

        for copy in loads:
            copy.wait()

        def body(ap, carry):
            place = pl.multiple_of(8 * ap, 8)
            for v in range(VARS):
                for h in range(2):
                    own, other = own_ref[v * 16 + ap, h], next_ref[v * 16 + ap, h]
                    near_ref[2 * v + h, pl.ds(place, 8), :] = pick(own, other, within)
                    near_ref[2 * v + h, pl.ds(place + 128, 8), :] = pick(own, other, within + 1)
            return carry

        lax.fori_loop(0, 16, body, 0, unroll=2)
        w_both = weight_ref[...]
        for v in range(VARS):
            both = jnp.concatenate([near_ref[2 * v], near_ref[2 * v + 1]], axis=1)
            high, low = split_bf16(both)
            first = jnp.dot(w_both, high, preferred_element_type=jnp.float32)
            total = first[:128] + first[128:] + jnp.dot(w_both[:128], low, preferred_element_type=jnp.float32)
            out_ref[2 * v] = total[:, :128]
            out_ref[2 * v + 1] = total[:, 128:]


def off_face(ctl_ref, live_ref, jac_ref, state_ref, off_ext_ref, window_ref, out_ref, ext_ref, cross_ref, sems, scale):
    block = ctl_ref[0]
    odd = block % 2
    x_off = 3 * odd
    masks = live_masks(live_ref)
    interface = (block == 7) | (block == 8)
    loads = [
        pltpu.make_async_copy(state_ref.at[v, :, x_off], out_ref.at[pl.ds(16 * v, 16)], sems.at[v])
        for v in range(VARS)
    ]
    for copy in loads:
        copy.start()
    matrix = face_matrix(jac_ref, jnp.where(block < 8, 0, 1), 2, jnp.where(odd == 0, 1.0, -1.0), scale)

    def run(copies, load):
        for copy in copies:
            copy.start()
        for copy in loads + copies:
            copy.wait()

        def body(ap, carry):
            for h in range(2):
                mixed = mix(matrix, [load(v, ap, h) for v in range(VARS)])
                for v in range(VARS):
                    out_ref[v * 16 + ap, h] += masks[h] * mixed[v]
            return carry

        lax.fori_loop(0, 16, body, 0, unroll=2)

    @pl.when(interface)
    def _():
        run(
            [
                pltpu.make_async_copy(
                    window_ref.at[pl.ds(2 * v, 2)], cross_ref.at[pl.ds(2 * v, 2)], sems.at[VARS + v]
                )
                for v in range(VARS)
            ],
            lambda v, ap, h: cross_ref[2 * v + h, pl.ds(pl.multiple_of(8 * ap, 8), 8), :],
        )

    @pl.when(jnp.logical_not(interface))
    def _():
        run(
            [
                pltpu.make_async_copy(
                    off_ext_ref.at[pl.ds(16 * v, 16)], ext_ref.at[pl.ds(16 * v, 16)], sems.at[VARS + v]
                )
                for v in range(VARS)
            ],
            lambda v, ap, h: ext_ref[v * 16 + ap, h],
        )


def first_off_kernel(ctl_ref, live_ref, jac_ref, west_ref, east_ref, state_ref, off_ext_ref, window_ref,
                     out_ref, new_west_ref, new_east_ref, ext_ref, cross_ref, sems):
    off_face(ctl_ref, live_ref, jac_ref, state_ref, off_ext_ref, window_ref, out_ref, ext_ref, cross_ref, sems, STEP)
    new_west_ref[...] = west_ref[...]
    new_east_ref[...] = east_ref[...]
    face_columns(out_ref, 3 * (ctl_ref[0] % 2), new_west_ref, new_east_ref)


def second_off_kernel(ctl_ref, live_ref, jac_ref, state_ref, off_ext_ref, window_ref, out_ref,
                      face_ref, ext_ref, cross_ref, sems):
    off_face(
        ctl_ref, live_ref, jac_ref, state_ref, off_ext_ref, window_ref, face_ref, ext_ref, cross_ref, sems, 0.5 * STEP
    )
    x_off = 3 * (ctl_ref[0] % 2)
    stores = [
        pltpu.make_async_copy(face_ref.at[pl.ds(16 * v, 16)], out_ref.at[v, :, x_off], sems.at[v])
        for v in range(VARS)
    ]
    for copy in stores:
        copy.start()
    for copy in stores:
        copy.wait()


def shape(*dims, dtype=jnp.float32):
    return jax.ShapeDtypeStruct(dims, dtype)


def vmem(like):
    return pltpu.VMEM(like.shape, like.dtype)


STATE = shape(VARS, 16, 4, 2, 8, 128)
FACE = shape(80, 2, 8, 128)
COLUMNS = shape(2, 8, 128)
EXPANDED = shape(256, 256, dtype=jnp.bfloat16)
WINDOW = shape(10, 128, 128)
TURN = shape(1, dtype=jnp.int32)
DMA = pltpu.SemaphoreType.DMA


def call(kernel, operands, outs, scratch=(), flops=10**7, aliases=None):
    moved = sum(a.size * a.dtype.itemsize for _, a in operands)
    moved += sum(int(np.prod(o.shape)) * o.dtype.itemsize for _, o in outs)
    return pl.pallas_call(
        kernel,
        in_specs=[m for m, _ in operands],
        out_specs=[m for m, _ in outs],
        out_shape=[o for _, o in outs],
        scratch_shapes=list(scratch),
        input_output_aliases=aliases or {},
        compiler_params=PARAMS,
        cost_estimate=pl.CostEstimate(flops=flops, bytes_accessed=moved, transcendentals=0),
    )(*[a for _, a in operands])


def send(array, route):
    sectors, layers = lax.axis_size("azim"), lax.axis_size("block")
    pairs = []
    for s in range(sectors):
        for b in range(layers):
            to = route(s, b)
            if to is not None:
                pairs.append((s * layers + b, to[0] * layers + to[1]))
    return lax.ppermute(array, AXES, pairs)


def off_chip(s, b):
    if b in (0, 7, 8, 15):
        return None
    return (s, b + 1 if b % 2 else b - 1)


def off_chip_or_beside(s, b):
    return beside(s, b) or off_chip(s, b)


def on_chip(s, b):
    return (s, b ^ 1)


def eastward(s, b):
    return ((s + 1) % 16, b)


def westward(s, b):
    return ((s - 1) % 16, b)


def across(turns):
    def route(s, b):
        if b == 7:
            return ((s + turns) % 16, 8)
        if b == 8:
            return ((s - turns) % 16, 7)
        return None

    return route


def beside(s, b):
    return {7: ((s + 1) % 16, 7), 8: ((s - 1) % 16, 8)}.get(b)


def cross_interface(panel, turn):
    branches = [lambda panel, turns=turns: send(panel, across(turns)) for turns in range(16)]
    return lax.switch(turn[0], branches, panel)


def extract(ctl, offsets, u):
    return call(
        extract_kernel,
        [(SMEM, ctl), (SMEM, offsets), (HBM, u)],
        [(VMEM, FACE), (VMEM, FACE), (VMEM, COLUMNS), (VMEM, COLUMNS), (SMEM, TURN), (SMEM, TURN)],
        [pltpu.VMEM((VARS, 2, 4, 2, 2, 8, 128), jnp.float32), DMA((20,))],
    )


def first_axis_span(ctl, jac, u):
    return call(axis_span_kernel, [(SMEM, ctl), (SMEM, jac), (VMEM, u)], [(VMEM, STATE)], flops=10**8)[0]


def second_axis_span(ctl, jac, state, off):
    return call(
        second_axis_span_kernel,
        [(SMEM, ctl), (SMEM, jac), (HBM, state), (VMEM, off)],
        [(VMEM, STATE), (VMEM, STATE)],
        [DMA((4,))],
        flops=10**8,
    )


def first_azimuth(ctl, live, jac, u, acc, west, east, weights, on_ext):
    return call(
        first_azimuth_kernel,
        [(SMEM, ctl), (SMEM, live), (SMEM, jac)]
        + [(VMEM, a) for a in (u, acc, west, east, weights)]
        + [(HBM, on_ext)],
        [(HBM, STATE), (VMEM, FACE), (VMEM, COLUMNS), (VMEM, COLUMNS), (HBM, EXPANDED), (HBM, EXPANDED)],
        [vmem(STATE), vmem(FACE), pltpu.VMEM((2, 256, 256), jnp.bfloat16), DMA((4, VARS)), DMA((3,))],
        flops=10**8,
    )


def second_azimuth(ctl, live, jac, first, acc, west, east, u, on_ext):
    return call(
        second_azimuth_kernel,
        [(SMEM, ctl), (SMEM, live), (SMEM, jac)]
        + [(VMEM, a) for a in (first, acc, west, east, u)]
        + [(HBM, on_ext)],
        [(HBM, STATE)],
        [vmem(STATE), vmem(FACE), DMA((4, VARS)), DMA((1,))],
        flops=10**8,
    )[0]


def interpolated(section, ctl, offsets, own, other, expanded):
    return call(
        functools.partial(interface_kernel, section),
        [(SMEM, ctl), (SMEM, offsets), (VMEM, own), (HBM, other), (HBM, expanded)],
        [(VMEM, WINDOW)],
        [vmem(FACE), vmem(EXPANDED), pltpu.VMEM((10, 256, 128), jnp.float32), DMA((VARS + 1,))],
    )[0]


def first_off(ctl, live, jac, west, east, state, off_ext, window):
    return call(
        first_off_kernel,
        [(SMEM, ctl), (SMEM, live), (SMEM, jac), (VMEM, west), (VMEM, east)]
        + [(HBM, a) for a in (state, off_ext, window)],
        [(VMEM, FACE), (VMEM, COLUMNS), (VMEM, COLUMNS)],
        [vmem(FACE), vmem(WINDOW), DMA((2 * VARS,))],
    )


def second_off(ctl, live, jac, state, off_ext, window):
    return call(
        second_off_kernel,
        [(SMEM, ctl), (SMEM, live), (SMEM, jac)] + [(HBM, a) for a in (state, off_ext, window)],
        [(HBM, STATE)],
        [vmem(FACE), vmem(FACE), vmem(WINDOW), DMA((2 * VARS,))],
        aliases={3: 0},
    )[0]


def shards(flow_state, jacobians, interp_weights, offsets, live_rows):
    ctl = lax.axis_index("block").astype(jnp.int32).reshape(1)
    jac = jnp.transpose(jacobians, (1, 2, 0, 3))
    u = flow_state.reshape(VARS, 16, 4, 2, 8, 128)
    off, on, west, east, turn_0, turn_1 = extract(ctl, offsets, u)
    off_ext = send(off, off_chip_or_beside)
    from_west, from_east = send(east, eastward), send(west, westward)
    on_ext = send(on, on_chip)
    acc = first_axis_span(ctl, jac, u)
    state, on, west, east, near, later = first_azimuth(
        ctl, live_rows, jac, u, acc, from_west, from_east, interp_weights, on_ext
    )
    on_ext = send(on, on_chip)
    window = cross_interface(interpolated(0, ctl, offsets, off, off_ext, near), turn_0)
    off, west, east = first_off(ctl, live_rows, jac, west, east, state, off_ext, window)
    off_ext = send(off, off_chip_or_beside)
    from_west, from_east = send(east, eastward), send(west, westward)
    first, acc = second_axis_span(ctl, jac, state, off)
    state = second_azimuth(ctl, live_rows, jac, first, acc, from_west, from_east, u, on_ext)
    window = cross_interface(interpolated(1, ctl, offsets, off, off_ext, later), turn_1)
    out = second_off(ctl, live_rows, jac, state, off_ext, window)
    return out.reshape(flow_state.shape)


def solution(mesh):
    placed = (P("block", None, None, None, "azim"), P(), P(), P(), P("block"))
    return jax.shard_map(
        shards,
        mesh=mesh,
        in_specs=placed,
        out_specs=P("block", None, None, None, "azim"),
        check_vma=False,
    )
```

```python
import functools

import jax
import jax.numpy as jnp
import numpy as np
from jax import lax
from jax.experimental import pallas as pl
from jax.experimental.pallas import tpu as pltpu
from jax.sharding import PartitionSpec as P

STEP = 0.04
VARS = 5
TILE = (8, 128)
AXES = ("azim", "block")
VMEM = pl.BlockSpec(memory_space=pltpu.VMEM)
HBM = pl.BlockSpec(memory_space=pltpu.HBM)
SMEM = pl.BlockSpec(memory_space=pltpu.SMEM)


def derivative_matrix():
    points = np.array([-1.0, -1.0 / np.sqrt(5.0), 1.0 / np.sqrt(5.0), 1.0])
    differ = points[:, None] - points[None, :]
    filled = differ + np.eye(4)
    weights = 1.0 / np.prod(filled, axis=1)
    matrix = weights[None, :] / weights[:, None] / filled
    matrix = matrix * (1.0 - np.eye(4))
    return matrix - np.eye(4) * matrix.sum(axis=1)[:, None]


DM = derivative_matrix()


def lanes():
    return lax.broadcasted_iota(jnp.int32, TILE, 1)


def rows():
    return lax.broadcasted_iota(jnp.int32, TILE, 0)


def splat_matrix(jac_ref, side, k):
    return [[jnp.full(TILE, jac_ref[k, w, side, v], jnp.float32) for v in range(VARS)] for w in range(VARS)]


def bound_of(matrix):
    sums = [functools.reduce(jnp.add, [jnp.abs(e) for e in row]) for row in matrix]
    return functools.reduce(jnp.maximum, sums)


def face_matrix(jac_ref, side, k, orient, scale):
    matrix = splat_matrix(jac_ref, side, k)
    lam = bound_of(matrix)
    factor = jnp.full(TILE, orient, jnp.float32) * (3.0 * scale)
    return [
        [factor * matrix[w][v] + (3.0 * scale) * lam if w == v else factor * matrix[w][v] for v in range(VARS)]
        for w in range(VARS)
    ]


def mix(matrix, z):
    return [functools.reduce(jnp.add, [matrix[w][v] * z[v] for v in range(VARS)]) for w in range(VARS)]


def live_masks(live_ref):
    live = live_ref[0]
    return [(rows() + 8 * h < live).astype(jnp.float32) for h in range(2)]


def put_columns(lane, j, west_tile, east_tile, west, east):
    return (
        jnp.where(lane == j, pltpu.roll(west_tile, j, 1), west),
        jnp.where(lane == j, pltpu.roll(east_tile, j + 1, 1), east),
    )


def split_bf16(x):
    high = x.astype(jnp.bfloat16)
    return high, (x - high.astype(jnp.float32)).astype(jnp.bfloat16)


def extract_kernel(ctl_ref, u_ref, off_ref, on_ref, west_ref, east_ref, sides_ref, sems):
    x_off = 3 * (ctl_ref[0] % 2)
    copies = []
    for v in range(VARS):
        face = pl.ds(v * 16, 16)
        copies.append(pltpu.make_async_copy(u_ref.at[v, :, x_off], off_ref.at[face], sems.at[v]))
        copies.append(pltpu.make_async_copy(u_ref.at[v, :, 3 - x_off], on_ref.at[face], sems.at[5 + v]))
        for e in range(2):
            copies.append(
                pltpu.make_async_copy(
                    u_ref.at[v, pl.ds(12 * e, 4), pl.ds(1, 2)], sides_ref.at[v, e], sems.at[10 + 2 * v + e]
                )
            )
    for copy in copies:
        copy.start()
    for copy in copies:
        copy.wait()
    middle_columns(lambda v, e, p, x, h: sides_ref[v, e, p, x - 1, h], west_ref, east_ref)
    face_columns(off_ref, x_off, west_ref, east_ref)
    face_columns(on_ref, 3 - x_off, west_ref, east_ref)


def middle_columns(tile, west_ref, east_ref):
    lane = lanes()
    for h in range(2):
        west = jnp.zeros(TILE, jnp.float32)
        east = jnp.zeros(TILE, jnp.float32)
        for v in range(VARS):
            for p in range(4):
                for x in (1, 2):
                    west, east = put_columns(
                        lane, 16 * v + 4 * p + x, tile(v, 0, p, x, h), tile(v, 1, p, x, h), west, east
                    )
        west_ref[h] = west
        east_ref[h] = east


def face_columns(face_ref, x, west_ref, east_ref):
    lane = lanes()
    for h in range(2):
        west, east = west_ref[h], east_ref[h]
        for v in range(VARS):
            for p in range(4):
                west, east = put_columns(
                    lane, 16 * v + 4 * p + x, face_ref[v * 16 + p, h], face_ref[v * 16 + 12 + p, h], west, east
                )
        west_ref[h] = west
        east_ref[h] = east


def derivative_terms(u0, u1, u2, u3):
    even = (u0 + u3) - (u1 + u2)
    o, g = u0 - u3, u1 - u2
    a = float(0.5 * (DM[0, 0] + DM[3, 0]))
    b = float(0.5 * (DM[0, 1] + DM[3, 1]))
    c = float(0.5 * (DM[1, 0] + DM[2, 0]))
    d = float(0.5 * (DM[1, 1] + DM[2, 1]))
    outer = (-a) * o - b * g
    inner = (-c) * o - d * g
    outer_even = float(-0.5 * (DM[0, 0] - DM[3, 0])) * even
    inner_even = float(-0.5 * (DM[1, 0] - DM[2, 0])) * even
    return outer + outer_even, inner + inner_even, inner - inner_even, outer - outer_even


def terms(matrix, lam3, z, jumps):
    outs = []
    for node in range(4):
        mixed = mix(matrix, [z[v][node] for v in range(VARS)])
        if node in jumps:
            mixed = [mixed[v] - lam3 * jumps[node][v] for v in range(VARS)]
        outs.append(mixed)
    return outs


def coefficients(ctl_ref, jac_ref, k, scale):
    matrix = splat_matrix(jac_ref, jnp.where(ctl_ref[0] < 8, 0, 1), k)
    lam3 = bound_of(matrix) * (3.0 * scale)
    return [[scale * e for e in r] for r in matrix], lam3


def interior_axis_span(ctl_ref, jac_ref, u_ref, acc_ref, scale, before):
    row = rows()

    def along_x(matrix, lam3):
        def one_a(a, carry):
            before(a)

            def body(i, carry):
                h, ap = i % 2, 4 * a + i // 2
                z, first, last = [], [], []
                for v in range(VARS):
                    u = [u_ref[v, ap, x, h] for x in range(4)]
                    d = derivative_terms(*u)
                    z.append([d[0] - 3.0 * u[0], d[1], d[2], d[3] + 3.0 * u[3]])
                    first.append(u[0])
                    last.append(u[3])
                outs = terms(matrix, lam3, z, {0: first, 3: last})
                for x in range(4):
                    for v in range(VARS):
                        acc_ref[v, ap, x, h] = outs[x][v]
                return carry

            lax.fori_loop(0, 8, body, 0, unroll=2)
            return carry

        lax.fori_loop(0, 4, one_a, 0)

    def along_p(matrix, lam3):
        def body(i, carry):
            a, x = i // 4, i % 4
            for h in range(2):
                z, jump_l, jump_u = [], [], []
                for v in range(VARS):
                    u = [u_ref[v, 4 * a + p, x, h] for p in range(4)]
                    d = derivative_terms(*u)
                    if h == 0:
                        below = jnp.where(row == 0, u[0], pltpu.roll(u[3], 1, 0))
                        other = u_ref[v, 4 * a, x, 1]
                        above = pltpu.roll(jnp.where(row == 0, other, u[0]), 7, 0)
                    else:
                        other = u_ref[v, 4 * a + 3, x, 0]
                        below = pltpu.roll(jnp.where(row == 7, other, u[3]), 1, 0)
                        above = jnp.where(row == 7, u[3], pltpu.roll(u[0], 7, 0))
                    lower, upper = u[0] - below, u[3] - above
                    z.append([d[0] - 3.0 * lower, d[1], d[2], d[3] + 3.0 * upper])
                    jump_l.append(lower)
                    jump_u.append(upper)
                outs = terms(matrix, lam3, z, {0: jump_l, 3: jump_u})
                for p in range(4):
                    for v in range(VARS):
                        acc_ref[v, 4 * a + p, x, h] += outs[p][v]
            return carry

        lax.fori_loop(0, 16, body, 0, unroll=2)

    along_x(*coefficients(ctl_ref, jac_ref, 2, scale))
    along_p(*coefficients(ctl_ref, jac_ref, 1, scale))


def interior_azimuth(ctl_ref, live_ref, jac_ref, u_ref, acc_ref, west_ref, east_ref, out_ref, scale, base, before, done):
    lane = lanes()
    matrix, lam3 = coefficients(ctl_ref, jac_ref, 0, scale)
    live = live_ref[0]
    x_off = 3 * (ctl_ref[0] % 2)

    def one_x(step, carry):
        x = jnp.where(step == 0, x_off, jnp.where(step == 3, 3 - x_off, step))
        before(step, x)

        def body(i, carry):
            h, p = i % 2, i // 2
            n = 4 * p + x
            mask = (rows() + 8 * h < live).astype(jnp.float32)
            halo_w, halo_e = west_ref[h], east_ref[h]
            z, jump_w, jump_e = [], [], []
            for v in range(VARS):
                u = [u_ref[v, 4 * a + p, x, h] for a in range(4)]
                d = derivative_terms(*u)
                from_w = pltpu.roll(halo_w, (128 - 16 * v - n) % 128, 1)
                from_e = pltpu.roll(halo_e, 127 - 16 * v - n, 1)
                west = u[0] - jnp.where(lane == 0, from_w, pltpu.roll(u[3], 1, 1))
                east = u[3] - jnp.where(lane == 127, from_e, pltpu.roll(u[0], 127, 1))
                z.append([d[0] - 3.0 * west, d[1], d[2], d[3] + 3.0 * east])
                jump_w.append(west)
                jump_e.append(east)
            outs = terms(matrix, lam3, z, {0: jump_w, 3: jump_e})
            for a in range(4):
                for v in range(VARS):
                    ap = 4 * a + p
                    out_ref[v, ap, x, h] = base(v, ap, x, h) + mask * (acc_ref[v, ap, x, h] + outs[a][v])
            return carry

        lax.fori_loop(0, 8, body, 0, unroll=4)
        done(step, x)
        return carry

    lax.fori_loop(0, 4, one_x, 0)


def plane_copies(source, target, x, sems):
    return [pltpu.make_async_copy(source.at[v, :, x], target.at[v, :, x], sems.at[v]) for v in range(VARS)]


def azimuth_and_on_face(ctl_ref, live_ref, jac_ref, u_ref, acc_ref, west_ref, east_ref, on_ext_ref, state_ref,
                        out_ref, ext_ref, sems, ext_sem, scale, base, on_ref=None, before=lambda step, x: None):
    block = ctl_ref[0]
    x_on = 3 - 3 * (block % 2)
    load = pltpu.make_async_copy(on_ext_ref, ext_ref, ext_sem)
    load.start()

    def done(step, x):
        @pl.when(step == 3)
        def _():
            load.wait()
            masks = live_masks(live_ref)
            orient = jnp.where(block % 2 == 0, -1.0, 1.0)
            matrix = face_matrix(jac_ref, jnp.where(block < 8, 0, 1), 2, orient, scale)

            def body(ap, carry):
                for h in range(2):
                    mixed = mix(matrix, [ext_ref[v * 16 + ap, h] for v in range(VARS)])
                    for v in range(VARS):
                        total = out_ref[v, ap, x, h] + masks[h] * mixed[v]
                        out_ref[v, ap, x, h] = total
                        if on_ref is not None:
                            on_ref[v * 16 + ap, h] = total
                return carry

            lax.fori_loop(0, 16, body, 0, unroll=2)

        for copy in plane_copies(out_ref, state_ref, x, sems.at[step]):
            copy.start()

    interior_azimuth(
        ctl_ref, live_ref, jac_ref, u_ref, acc_ref, west_ref, east_ref, out_ref, scale, base, before, done
    )

    def finish():
        for step, x in enumerate((3 - x_on, 1, 2, x_on)):
            for copy in plane_copies(out_ref, state_ref, x, sems.at[step]):
                copy.wait()

    return finish


def load_parts(source, target, sems):
    def load(a):
        part = pl.ds(4 * a, 4)
        return pltpu.make_async_copy(source.at[:, part], target.at[:, part], sems.at[a])

    for a in range(4):
        load(a).start()
    return load


def first_axis_span_kernel(ctl_ref, jac_ref, offset_ref, state_ref, u_ref, acc_ref, turn_0_ref, turn_1_ref, sems):
    load = load_parts(state_ref, u_ref, sems)
    turn_0_ref[0] = lax.shift_right_logical(offset_ref[0], 7)
    turn_1_ref[0] = lax.shift_right_logical(offset_ref[1], 7)
    interior_axis_span(ctl_ref, jac_ref, u_ref, acc_ref, STEP, lambda a: load(a).wait())


def second_axis_span_kernel(ctl_ref, jac_ref, state_ref, off_ref, first_ref, acc_ref, sems):
    x_off = 3 * (ctl_ref[0] % 2)
    load = load_parts(state_ref, first_ref, sems)

    def before(a):
        load(a).wait()
        for v in range(VARS):
            for p in range(4):
                ap = 4 * a + p
                first_ref[v, ap, x_off] = off_ref[v * 16 + ap]

    interior_axis_span(ctl_ref, jac_ref, first_ref, acc_ref, 0.5 * STEP, before)


def expanded_weights(turn, weight_ref, out_refs):
    parts = []
    for section in range(2):
        for i in range(2):
            high, low = split_bf16(weight_ref[section, i])
            parts += [high.astype(jnp.float32), low.astype(jnp.float32)]
    spread = lax.broadcasted_iota(jnp.int32, (128, 16), 0) // 8 == lax.broadcasted_iota(jnp.int32, (128, 16), 1)
    spread = spread.astype(jnp.bfloat16)

    def dot(a, b, dims):
        return lax.dot_general(
            a.astype(jnp.bfloat16), b.astype(jnp.bfloat16), (dims, ((), ())), preferred_element_type=jnp.float32
        )

    plain = dot(spread, jnp.concatenate(parts, axis=1), ((1,), (0,)))
    turned = dot(spread, jnp.concatenate(parts, axis=0), ((1,), (1,)))
    picked = jnp.where(turn, turned, plain)
    row = lax.broadcasted_iota(jnp.int32, (128, 1024), 0)
    col = lax.broadcasted_iota(jnp.int32, (128, 1024), 1)
    widen = (row == 16 * (col // 128) + (col % 128) // 8).astype(jnp.bfloat16)
    wide = dot(picked, widen, ((1,), (0,)))
    wide = jnp.where(row % 8 == col % 8, wide, 0.0).astype(jnp.bfloat16)
    for section in range(2):
        near_high, near_low, far_high, far_low = [
            wide[:, 128 * (4 * section + k) : 128 * (4 * section + k + 1)] for k in range(4)
        ]
        high = jnp.concatenate([near_high, far_high], axis=1)
        low = jnp.concatenate([near_low, far_low], axis=1)
        out_refs[section][...] = jnp.concatenate([high, low], axis=0)


def first_azimuth_kernel(ctl_ref, live_ref, jac_ref, u_ref, acc_ref, west_ref, east_ref, weight_ref, on_ext_ref,
                         state_ref, on_ref, new_west_ref, new_east_ref, near_ref, later_ref,
                         out_ref, ext_ref, sems, ext_sems):
    block = ctl_ref[0]
    finish = azimuth_and_on_face(
        ctl_ref, live_ref, jac_ref, u_ref, acc_ref, west_ref, east_ref, on_ext_ref, state_ref,
        out_ref, ext_ref, sems, ext_sems.at[0], STEP, lambda v, ap, x, h: u_ref[v, ap, x, h], on_ref,
    )
    middle_columns(lambda v, e, p, x, h: out_ref[v, 12 * e + p, x, h], new_west_ref, new_east_ref)
    face_columns(on_ref, 3 - 3 * (block % 2), new_west_ref, new_east_ref)

    @pl.when((block == 7) | (block == 8))
    def _():
        expanded_weights(block >= 8, weight_ref, (near_ref, later_ref))

    finish()


def second_azimuth_kernel(ctl_ref, live_ref, jac_ref, first_ref, acc_ref, west_ref, east_ref, u_ref, on_ext_ref,
                          old_ref, state_ref, out_ref, ext_ref, near_ref, sems, ext_sems, near_sems):
    def loads(step, x):
        return plane_copies(u_ref, near_ref, x, near_sems.at[step])

    x_off = 3 * (ctl_ref[0] % 2)
    for step, x in enumerate((x_off, 1, 2, 3 - x_off)):
        for copy in loads(step, x):
            copy.start()

    def before(step, x):
        for copy in loads(step, x):
            copy.wait()

    finish = azimuth_and_on_face(
        ctl_ref, live_ref, jac_ref, first_ref, acc_ref, west_ref, east_ref, on_ext_ref, state_ref,
        out_ref, ext_ref, sems, ext_sems.at[0], 0.5 * STEP,
        lambda v, ap, x, h: 0.5 * near_ref[v, ap, x, h] + 0.5 * first_ref[v, ap, x, h], before=before,
    )
    finish()


def interface_kernel(section, ctl_ref, offset_ref, own_ref, next_ref, weight_ref, *rest):
    out_ref, near_ref = rest[-2:]
    block = ctl_ref[0]

    @pl.when((block == 7) | (block == 8))
    def _():
        rotor = block < 8
        within = lax.rem(offset_ref[section], 128)
        lane = lanes()

        def pick(own, other, amount):
            start = jnp.where(rotor, 128 - amount, 0)
            sent = (lane >= start) & (lane < start + amount)
            turn = lax.rem(jnp.where(rotor, amount, 128 - amount), 128)
            return pltpu.roll(jnp.where(sent, other, own), turn, 1)

        def body(ap, carry):
            place = pl.multiple_of(8 * ap, 8)
            for v in range(VARS):
                for h in range(2):
                    own, other = own_ref[v * 16 + ap, h], next_ref[v * 16 + ap, h]
                    near_ref[2 * v + h, pl.ds(place, 8), :] = pick(own, other, within)
                    near_ref[2 * v + h, pl.ds(place + 128, 8), :] = pick(own, other, within + 1)
            return carry

        lax.fori_loop(0, 16, body, 0, unroll=2)
        w_both = weight_ref[...]
        for v in range(VARS):
            both = jnp.concatenate([near_ref[2 * v], near_ref[2 * v + 1]], axis=1)
            high, low = split_bf16(both)
            first = jnp.dot(w_both, high, preferred_element_type=jnp.float32)
            total = first[:128] + first[128:] + jnp.dot(w_both[:128], low, preferred_element_type=jnp.float32)
            out_ref[2 * v] = total[:, :128]
            out_ref[2 * v + 1] = total[:, 128:]


def off_face(ctl_ref, live_ref, jac_ref, off_ext_ref, state_ref, window_ref, out_ref, cross_ref, sems, scale):
    block = ctl_ref[0]
    odd = block % 2
    masks = live_masks(live_ref)
    interface = (block == 7) | (block == 8)
    loads = [
        pltpu.make_async_copy(state_ref.at[v, :, 3 * odd], out_ref.at[pl.ds(16 * v, 16)], sems.at[v])
        for v in range(VARS)
    ]
    for copy in loads:
        copy.start()
    matrix = face_matrix(jac_ref, jnp.where(block < 8, 0, 1), 2, jnp.where(odd == 0, 1.0, -1.0), scale)

    def run(copies, load):
        for copy in copies:
            copy.start()
        for copy in loads + copies:
            copy.wait()

        def body(ap, carry):
            for h in range(2):
                mixed = mix(matrix, [load(v, ap, h) for v in range(VARS)])
                for v in range(VARS):
                    out_ref[v * 16 + ap, h] += masks[h] * mixed[v]
            return carry

        lax.fori_loop(0, 16, body, 0, unroll=2)

    @pl.when(interface)
    def _():
        run(
            [
                pltpu.make_async_copy(
                    window_ref.at[pl.ds(2 * v, 2)], cross_ref.at[pl.ds(2 * v, 2)], sems.at[VARS + v]
                )
                for v in range(VARS)
            ],
            lambda v, ap, h: cross_ref[2 * v + h, pl.ds(pl.multiple_of(8 * ap, 8), 8), :],
        )

    @pl.when(jnp.logical_not(interface))
    def _():
        run([], lambda v, ap, h: off_ext_ref[v * 16 + ap, h])


def first_off_kernel(ctl_ref, live_ref, jac_ref, west_ref, east_ref, off_ext_ref, state_ref, window_ref,
                     out_ref, new_west_ref, new_east_ref, cross_ref, sems):
    off_face(ctl_ref, live_ref, jac_ref, off_ext_ref, state_ref, window_ref, out_ref, cross_ref, sems, STEP)
    new_west_ref[...] = west_ref[...]
    new_east_ref[...] = east_ref[...]
    face_columns(out_ref, 3 * (ctl_ref[0] % 2), new_west_ref, new_east_ref)


def second_off_kernel(ctl_ref, live_ref, jac_ref, off_ext_ref, state_ref, window_ref, out_ref,
                      face_ref, cross_ref, sems):
    x_off = 3 * (ctl_ref[0] % 2)
    off_face(ctl_ref, live_ref, jac_ref, off_ext_ref, state_ref, window_ref, face_ref, cross_ref, sems, 0.5 * STEP)
    stores = [
        pltpu.make_async_copy(face_ref.at[pl.ds(16 * v, 16)], out_ref.at[v, :, x_off], sems.at[v])
        for v in range(VARS)
    ]
    for copy in stores:
        copy.start()
    for copy in stores:
        copy.wait()


def shape(*dims, dtype=jnp.float32):
    return jax.ShapeDtypeStruct(dims, dtype)


def vmem(like):
    return pltpu.VMEM(like.shape, like.dtype)


STATE = shape(VARS, 16, 4, 2, 8, 128)
FACE = shape(80, 2, 8, 128)
COLUMNS = shape(2, 8, 128)
EXPANDED = shape(256, 256, dtype=jnp.bfloat16)
WINDOW = shape(10, 128, 128)
TURN = shape(1, dtype=jnp.int32)
DMA = pltpu.SemaphoreType.DMA


def call(kernel, operands, outs, scratch=(), flops=10**7, aliases=None, moved=None, limit=20):
    if moved is None:
        moved = sum(a.size * a.dtype.itemsize for _, a in operands)
        moved += sum(int(np.prod(o.shape)) * o.dtype.itemsize for _, o in outs)
    return pl.pallas_call(
        kernel,
        in_specs=[m for m, _ in operands],
        out_specs=[m for m, _ in outs],
        out_shape=[o for _, o in outs],
        scratch_shapes=list(scratch),
        input_output_aliases=aliases or {},
        compiler_params=pltpu.CompilerParams(vmem_limit_bytes=limit * 2**20),
        cost_estimate=pl.CostEstimate(flops=flops, bytes_accessed=moved, transcendentals=0),
    )(*[a for _, a in operands])


def send(array, route):
    sectors, layers = lax.axis_size("azim"), lax.axis_size("block")
    pairs = []
    for s in range(sectors):
        for b in range(layers):
            to = route(s, b)
            if to is not None:
                pairs.append((s * layers + b, to[0] * layers + to[1]))
    return lax.ppermute(array, AXES, pairs)


def off_chip(s, b):
    if b in (0, 7, 8, 15):
        return None
    return (s, b + 1 if b % 2 else b - 1)


def off_chip_or_beside(s, b):
    return beside(s, b) or off_chip(s, b)


def on_chip(s, b):
    return (s, b ^ 1)


def eastward(s, b):
    return ((s + 1) % 16, b)


def westward(s, b):
    return ((s - 1) % 16, b)


def across(turns):
    def route(s, b):
        if b == 7:
            return ((s + turns) % 16, 8)
        if b == 8:
            return ((s - turns) % 16, 7)
        return None

    return route


def beside(s, b):
    return {7: ((s + 1) % 16, 7), 8: ((s - 1) % 16, 8)}.get(b)


def cross_interface(panel, turn):
    branches = [lambda panel, turns=turns: send(panel, across(turns)) for turns in range(16)]
    return lax.switch(turn[0], branches, panel)


def extract(ctl, u):
    return call(
        extract_kernel,
        [(SMEM, ctl), (HBM, u)],
        [(VMEM, FACE), (VMEM, FACE), (VMEM, COLUMNS), (VMEM, COLUMNS)],
        [pltpu.VMEM((VARS, 2, 4, 2, 2, 8, 128), jnp.float32), DMA((20,))],
        limit=53,
    )


def first_axis_span(ctl, jac, offsets, u):
    return call(
        first_axis_span_kernel,
        [(SMEM, ctl), (SMEM, jac), (SMEM, offsets), (HBM, u)],
        [(VMEM, STATE), (VMEM, STATE), (SMEM, TURN), (SMEM, TURN)],
        [DMA((4,))],
        flops=10**8,
        limit=48,
    )


def second_axis_span(ctl, jac, state, off):
    return call(
        second_axis_span_kernel,
        [(SMEM, ctl), (SMEM, jac), (HBM, state), (VMEM, off)],
        [(VMEM, STATE), (VMEM, STATE)],
        [DMA((4,))],
        flops=10**8,
    )


def first_azimuth(ctl, live, jac, u, acc, west, east, weights, on_ext):
    return call(
        first_azimuth_kernel,
        [(SMEM, ctl), (SMEM, live), (SMEM, jac)]
        + [(VMEM, a) for a in (u, acc, west, east, weights)]
        + [(HBM, on_ext)],
        [(HBM, STATE), (VMEM, FACE)]
        + [(VMEM, COLUMNS), (VMEM, COLUMNS), (VMEM, EXPANDED), (VMEM, EXPANDED)],
        [vmem(STATE), vmem(FACE), DMA((4, VARS)), DMA((1,))],
        flops=10**8,
    )


def second_azimuth(ctl, live, jac, first, acc, west, east, u, on_ext, state):
    return call(
        second_azimuth_kernel,
        [(SMEM, ctl), (SMEM, live), (SMEM, jac)]
        + [(VMEM, a) for a in (first, acc, west, east)]
        + [(HBM, u), (HBM, on_ext), (HBM, state)],
        [(HBM, STATE)],
        [vmem(STATE), vmem(FACE), vmem(STATE), DMA((4, VARS)), DMA((1,)), DMA((4, VARS))],
        flops=10**8,
        aliases={9: 0},
        limit=48,
    )[0]


def interpolated(section, ctl, offsets, own, other, expanded, later=()):
    return call(
        functools.partial(interface_kernel, section),
        [(SMEM, ctl), (SMEM, offsets), (VMEM, own), (VMEM, other), (VMEM, expanded)]
        + [(HBM, a) for a in later],
        [(VMEM, WINDOW)],
        [pltpu.VMEM((10, 256, 128), jnp.float32)],
    )[0]


def first_off(ctl, live, jac, west, east, off_ext, state, window):
    return call(
        first_off_kernel,
        [(SMEM, ctl), (SMEM, live), (SMEM, jac), (VMEM, west), (VMEM, east)]
        + [(VMEM, off_ext), (HBM, state), (HBM, window)],
        [(VMEM, FACE), (VMEM, COLUMNS), (VMEM, COLUMNS)],
        [vmem(WINDOW), DMA((2 * VARS,))],
    )


def second_off(ctl, live, jac, state, off_ext, window):
    return call(
        second_off_kernel,
        [(SMEM, ctl), (SMEM, live), (SMEM, jac), (VMEM, off_ext), (HBM, state), (HBM, window)],
        [(HBM, STATE)],
        [vmem(FACE), vmem(WINDOW), DMA((2 * VARS,))],
        aliases={4: 0},
    )[0]


def shards(flow_state, jacobians, interp_weights, offsets, live_rows):
    ctl = lax.axis_index("block").astype(jnp.int32).reshape(1)
    jac = jnp.transpose(jacobians, (1, 2, 0, 3))
    u = flow_state.reshape(VARS, 16, 4, 2, 8, 128)
    off, on, west, east = extract(ctl, u)
    off_ext = send(off, off_chip_or_beside)
    from_west, from_east = send(east, eastward), send(west, westward)
    on_ext = send(on, on_chip)
    u_near, acc, turn_0, turn_1 = first_axis_span(ctl, jac, offsets, u)
    state, on, west, east, near, later = first_azimuth(
        ctl, live_rows, jac, u_near, acc, from_west, from_east, interp_weights, on_ext
    )
    window = cross_interface(interpolated(0, ctl, offsets, off, off_ext, near, [on]), turn_0)
    off, west, east = first_off(ctl, live_rows, jac, west, east, off_ext, state, window)
    off_ext = send(off, off_chip_or_beside)
    on_ext = send(on, on_chip)
    from_west, from_east = send(east, eastward), send(west, westward)
    first, acc = second_axis_span(ctl, jac, state, off)
    state = second_azimuth(ctl, live_rows, jac, first, acc, from_west, from_east, u, on_ext, state)
    panel = interpolated(1, ctl, offsets, off, off_ext, later)
    panel, state = lax.optimization_barrier((panel, state))
    window = cross_interface(panel, turn_1)
    out = second_off(ctl, live_rows, jac, state, off_ext, window)
    return out.reshape(flow_state.shape)


def solution(mesh):
    placed = (P("block", None, None, None, "azim"), P(), P(), P(), P("block"))
    return jax.shard_map(
        shards,
        mesh=mesh,
        in_specs=placed,
        out_specs=P("block", None, None, None, "azim"),
        check_vma=False,
    )
```

```python
import functools

import jax
import jax.numpy as jnp
import numpy as np
from jax import lax
from jax.experimental import pallas as pl
from jax.experimental.pallas import tpu as pltpu
from jax.sharding import PartitionSpec as P

STEP = 0.04
VARS = 5
TILE = (8, 128)
AXES = ("azim", "block")
VMEM = pl.BlockSpec(memory_space=pltpu.VMEM)
HBM = pl.BlockSpec(memory_space=pltpu.HBM)
SMEM = pl.BlockSpec(memory_space=pltpu.SMEM)


def derivative_matrix():
    points = np.array([-1.0, -1.0 / np.sqrt(5.0), 1.0 / np.sqrt(5.0), 1.0])
    differ = points[:, None] - points[None, :]
    filled = differ + np.eye(4)
    weights = 1.0 / np.prod(filled, axis=1)
    matrix = weights[None, :] / weights[:, None] / filled
    matrix = matrix * (1.0 - np.eye(4))
    return matrix - np.eye(4) * matrix.sum(axis=1)[:, None]


DM = derivative_matrix()


def lanes():
    return lax.broadcasted_iota(jnp.int32, TILE, 1)


def rows():
    return lax.broadcasted_iota(jnp.int32, TILE, 0)


def splat_matrix(jac_ref, side, k):
    return [[jnp.full(TILE, jac_ref[k, w, side, v], jnp.float32) for v in range(VARS)] for w in range(VARS)]


def bound_of(matrix):
    sums = [functools.reduce(jnp.add, [jnp.abs(e) for e in row]) for row in matrix]
    return functools.reduce(jnp.maximum, sums)


def face_matrix(jac_ref, side, k, orient, scale):
    matrix = splat_matrix(jac_ref, side, k)
    lam = bound_of(matrix)
    factor = jnp.full(TILE, orient, jnp.float32) * (3.0 * scale)
    return [
        [factor * matrix[w][v] + (3.0 * scale) * lam if w == v else factor * matrix[w][v] for v in range(VARS)]
        for w in range(VARS)
    ]


def mix(matrix, z):
    return [functools.reduce(jnp.add, [matrix[w][v] * z[v] for v in range(VARS)]) for w in range(VARS)]


def live_masks(live_ref):
    live = live_ref[0]
    return [(rows() + 8 * h < live).astype(jnp.float32) for h in range(2)]


def put_columns(lane, j, west_tile, east_tile, west, east):
    return (
        jnp.where(lane == j, pltpu.roll(west_tile, j, 1), west),
        jnp.where(lane == j, pltpu.roll(east_tile, j + 1, 1), east),
    )


def split_bf16(x):
    high = x.astype(jnp.bfloat16)
    return high, (x - high.astype(jnp.float32)).astype(jnp.bfloat16)


def extract_kernel(ctl_ref, state_ref, u_ref, off_ref, on_ref, west_ref, east_ref, sems):
    x_off = 3 * (ctl_ref[0] % 2)
    load = load_parts(state_ref, u_ref, sems, (0, 3, 1, 2))
    for a in (0, 3, 1, 2):
        load(a).wait()
        for p in range(4):
            ap = 4 * a + p
            for v in range(VARS):
                off_ref[v * 16 + ap] = u_ref[v, ap, x_off]
                on_ref[v * 16 + ap] = u_ref[v, ap, 3 - x_off]
        if a == 3:
            middle_columns(lambda v, e, p, x, h: u_ref[v, 12 * e + p, x, h], west_ref, east_ref)
            face_columns(off_ref, x_off, west_ref, east_ref)
            face_columns(on_ref, 3 - x_off, west_ref, east_ref)


def middle_columns(tile, west_ref, east_ref):
    lane = lanes()
    for h in range(2):
        west = jnp.zeros(TILE, jnp.float32)
        east = jnp.zeros(TILE, jnp.float32)
        for v in range(VARS):
            for p in range(4):
                for x in (1, 2):
                    west, east = put_columns(
                        lane, 16 * v + 4 * p + x, tile(v, 0, p, x, h), tile(v, 1, p, x, h), west, east
                    )
        west_ref[h] = west
        east_ref[h] = east


def face_columns(face_ref, x, west_ref, east_ref):
    lane = lanes()
    for h in range(2):
        west, east = west_ref[h], east_ref[h]
        for v in range(VARS):
            for p in range(4):
                west, east = put_columns(
                    lane, 16 * v + 4 * p + x, face_ref[v * 16 + p, h], face_ref[v * 16 + 12 + p, h], west, east
                )
        west_ref[h] = west
        east_ref[h] = east


def derivative_terms(u0, u1, u2, u3):
    even = (u0 + u3) - (u1 + u2)
    o, g = u0 - u3, u1 - u2
    a = float(0.5 * (DM[0, 0] + DM[3, 0]))
    b = float(0.5 * (DM[0, 1] + DM[3, 1]))
    c = float(0.5 * (DM[1, 0] + DM[2, 0]))
    d = float(0.5 * (DM[1, 1] + DM[2, 1]))
    outer = (-a) * o - b * g
    inner = (-c) * o - d * g
    outer_even = float(-0.5 * (DM[0, 0] - DM[3, 0])) * even
    inner_even = float(-0.5 * (DM[1, 0] - DM[2, 0])) * even
    return outer + outer_even, inner + inner_even, inner - inner_even, outer - outer_even


def terms(matrix, lam3, z, jumps):
    outs = []
    for node in range(4):
        mixed = mix(matrix, [z[v][node] for v in range(VARS)])
        if node in jumps:
            mixed = [mixed[v] - lam3 * jumps[node][v] for v in range(VARS)]
        outs.append(mixed)
    return outs


def coefficients(ctl_ref, jac_ref, k, scale):
    matrix = splat_matrix(jac_ref, jnp.where(ctl_ref[0] < 8, 0, 1), k)
    lam3 = bound_of(matrix) * (3.0 * scale)
    return [[scale * e for e in r] for r in matrix], lam3


def interior_axis_span(ctl_ref, jac_ref, u_ref, acc_ref, scale, before):
    row = rows()

    def along_x(matrix, lam3):
        def one_a(a, carry):
            before(a)

            def body(i, carry):
                h, ap = i % 2, 4 * a + i // 2
                z, first, last = [], [], []
                for v in range(VARS):
                    u = [u_ref[v, ap, x, h] for x in range(4)]
                    d = derivative_terms(*u)
                    z.append([d[0] - 3.0 * u[0], d[1], d[2], d[3] + 3.0 * u[3]])
                    first.append(u[0])
                    last.append(u[3])
                outs = terms(matrix, lam3, z, {0: first, 3: last})
                for x in range(4):
                    for v in range(VARS):
                        acc_ref[v, ap, x, h] = outs[x][v]
                return carry

            lax.fori_loop(0, 8, body, 0, unroll=2)
            return carry

        lax.fori_loop(0, 4, one_a, 0)

    def along_p(matrix, lam3):
        def body(i, carry):
            a, x = i // 4, i % 4
            for h in range(2):
                z, jump_l, jump_u = [], [], []
                for v in range(VARS):
                    u = [u_ref[v, 4 * a + p, x, h] for p in range(4)]
                    d = derivative_terms(*u)
                    if h == 0:
                        below = jnp.where(row == 0, u[0], pltpu.roll(u[3], 1, 0))
                        other = u_ref[v, 4 * a, x, 1]
                        above = pltpu.roll(jnp.where(row == 0, other, u[0]), 7, 0)
                    else:
                        other = u_ref[v, 4 * a + 3, x, 0]
                        below = pltpu.roll(jnp.where(row == 7, other, u[3]), 1, 0)
                        above = jnp.where(row == 7, u[3], pltpu.roll(u[0], 7, 0))
                    lower, upper = u[0] - below, u[3] - above
                    z.append([d[0] - 3.0 * lower, d[1], d[2], d[3] + 3.0 * upper])
                    jump_l.append(lower)
                    jump_u.append(upper)
                outs = terms(matrix, lam3, z, {0: jump_l, 3: jump_u})
                for p in range(4):
                    for v in range(VARS):
                        acc_ref[v, 4 * a + p, x, h] += outs[p][v]
            return carry

        lax.fori_loop(0, 16, body, 0, unroll=2)

    along_x(*coefficients(ctl_ref, jac_ref, 2, scale))
    along_p(*coefficients(ctl_ref, jac_ref, 1, scale))


def interior_azimuth(ctl_ref, live_ref, jac_ref, u_ref, acc_ref, west_ref, east_ref, out_ref, scale, base, before, done):
    lane = lanes()
    matrix, lam3 = coefficients(ctl_ref, jac_ref, 0, scale)
    live = live_ref[0]
    x_off = 3 * (ctl_ref[0] % 2)

    def one_x(step, carry):
        x = jnp.where(step == 0, x_off, jnp.where(step == 3, 3 - x_off, step))
        before(step, x)

        def body(i, carry):
            h, p = i % 2, i // 2
            n = 4 * p + x
            mask = (rows() + 8 * h < live).astype(jnp.float32)
            halo_w, halo_e = west_ref[h], east_ref[h]
            z, jump_w, jump_e = [], [], []
            for v in range(VARS):
                u = [u_ref[v, 4 * a + p, x, h] for a in range(4)]
                d = derivative_terms(*u)
                from_w = pltpu.roll(halo_w, (128 - 16 * v - n) % 128, 1)
                from_e = pltpu.roll(halo_e, 127 - 16 * v - n, 1)
                west = u[0] - jnp.where(lane == 0, from_w, pltpu.roll(u[3], 1, 1))
                east = u[3] - jnp.where(lane == 127, from_e, pltpu.roll(u[0], 127, 1))
                z.append([d[0] - 3.0 * west, d[1], d[2], d[3] + 3.0 * east])
                jump_w.append(west)
                jump_e.append(east)
            outs = terms(matrix, lam3, z, {0: jump_w, 3: jump_e})
            for a in range(4):
                for v in range(VARS):
                    ap = 4 * a + p
                    out_ref[v, ap, x, h] = base(v, ap, x, h) + mask * (acc_ref[v, ap, x, h] + outs[a][v])
            return carry

        lax.fori_loop(0, 8, body, 0, unroll=8)
        done(step, x)
        return carry

    lax.fori_loop(0, 4, one_x, 0)


def plane_copies(source, target, x, sems):
    return [pltpu.make_async_copy(source.at[v, :, x], target.at[v, :, x], sems.at[v]) for v in range(VARS)]


def azimuth_and_on_face(ctl_ref, live_ref, jac_ref, u_ref, acc_ref, west_ref, east_ref, on_ext_ref, state_ref,
                        out_ref, ext_ref, sems, ext_sem, scale, base, on_ref=None, before=lambda step, x: None):
    block = ctl_ref[0]
    x_on = 3 - 3 * (block % 2)
    load = pltpu.make_async_copy(on_ext_ref, ext_ref, ext_sem)
    load.start()

    def done(step, x):
        @pl.when(step == 3)
        def _():
            load.wait()
            masks = live_masks(live_ref)
            orient = jnp.where(block % 2 == 0, -1.0, 1.0)
            matrix = face_matrix(jac_ref, jnp.where(block < 8, 0, 1), 2, orient, scale)

            def body(ap, carry):
                for h in range(2):
                    mixed = mix(matrix, [ext_ref[v * 16 + ap, h] for v in range(VARS)])
                    for v in range(VARS):
                        total = out_ref[v, ap, x, h] + masks[h] * mixed[v]
                        out_ref[v, ap, x, h] = total
                        if on_ref is not None:
                            on_ref[v * 16 + ap, h] = total
                return carry

            lax.fori_loop(0, 16, body, 0, unroll=2)

        for copy in plane_copies(out_ref, state_ref, x, sems.at[step]):
            copy.start()

    interior_azimuth(
        ctl_ref, live_ref, jac_ref, u_ref, acc_ref, west_ref, east_ref, out_ref, scale, base, before, done
    )

    def finish():
        for step, x in enumerate((3 - x_on, 1, 2, x_on)):
            for copy in plane_copies(out_ref, state_ref, x, sems.at[step]):
                copy.wait()

    return finish


def load_parts(source, target, sems, order=(0, 1, 2, 3)):
    def load(a):
        part = pl.ds(4 * a, 4)
        return pltpu.make_async_copy(source.at[:, part], target.at[:, part], sems.at[a])

    for a in order:
        load(a).start()
    return load


def first_axis_span_kernel(ctl_ref, jac_ref, offset_ref, u_ref, acc_ref, turn_0_ref, turn_1_ref):
    turn_0_ref[0] = lax.shift_right_logical(offset_ref[0], 7)
    turn_1_ref[0] = lax.shift_right_logical(offset_ref[1], 7)
    interior_axis_span(ctl_ref, jac_ref, u_ref, acc_ref, STEP, lambda a: None)


def second_axis_span_kernel(ctl_ref, jac_ref, state_ref, off_ref, first_ref, acc_ref, sems):
    x_off = 3 * (ctl_ref[0] % 2)
    load = load_parts(state_ref, first_ref, sems)

    def before(a):
        load(a).wait()
        for v in range(VARS):
            for p in range(4):
                ap = 4 * a + p
                first_ref[v, ap, x_off] = off_ref[v * 16 + ap]

    interior_axis_span(ctl_ref, jac_ref, first_ref, acc_ref, 0.5 * STEP, before)


def expanded_weights(turn, weight_ref, out_refs):
    parts = []
    for section in range(2):
        for i in range(2):
            high, low = split_bf16(weight_ref[section, i])
            parts += [high.astype(jnp.float32), low.astype(jnp.float32)]
    spread = lax.broadcasted_iota(jnp.int32, (128, 16), 0) // 8 == lax.broadcasted_iota(jnp.int32, (128, 16), 1)
    spread = spread.astype(jnp.bfloat16)

    def dot(a, b, dims):
        return lax.dot_general(
            a.astype(jnp.bfloat16), b.astype(jnp.bfloat16), (dims, ((), ())), preferred_element_type=jnp.float32
        )

    plain = dot(spread, jnp.concatenate(parts, axis=1), ((1,), (0,)))
    turned = dot(spread, jnp.concatenate(parts, axis=0), ((1,), (1,)))
    picked = jnp.where(turn, turned, plain)
    row = lax.broadcasted_iota(jnp.int32, (128, 1024), 0)
    col = lax.broadcasted_iota(jnp.int32, (128, 1024), 1)
    widen = (row == 16 * (col // 128) + (col % 128) // 8).astype(jnp.bfloat16)
    wide = dot(picked, widen, ((1,), (0,)))
    wide = jnp.where(row % 8 == col % 8, wide, 0.0).astype(jnp.bfloat16)
    for section in range(2):
        near_high, near_low, far_high, far_low = [
            wide[:, 128 * (4 * section + k) : 128 * (4 * section + k + 1)] for k in range(4)
        ]
        high = jnp.concatenate([near_high, far_high], axis=1)
        low = jnp.concatenate([near_low, far_low], axis=1)
        out_refs[section][...] = jnp.concatenate([high, low], axis=0)


def first_azimuth_kernel(ctl_ref, live_ref, jac_ref, u_ref, acc_ref, west_ref, east_ref, weight_ref, on_ext_ref,
                         state_ref, on_ref, new_west_ref, new_east_ref, near_ref, later_ref,
                         out_ref, ext_ref, sems, ext_sems):
    block = ctl_ref[0]
    finish = azimuth_and_on_face(
        ctl_ref, live_ref, jac_ref, u_ref, acc_ref, west_ref, east_ref, on_ext_ref, state_ref,
        out_ref, ext_ref, sems, ext_sems.at[0], STEP, lambda v, ap, x, h: u_ref[v, ap, x, h], on_ref,
    )
    middle_columns(lambda v, e, p, x, h: out_ref[v, 12 * e + p, x, h], new_west_ref, new_east_ref)
    face_columns(on_ref, 3 - 3 * (block % 2), new_west_ref, new_east_ref)

    @pl.when((block == 7) | (block == 8))
    def _():
        expanded_weights(block >= 8, weight_ref, (near_ref, later_ref))

    finish()


def second_azimuth_kernel(ctl_ref, live_ref, jac_ref, first_ref, acc_ref, west_ref, east_ref, u_ref, on_ext_ref,
                          old_ref, state_ref, out_ref, ext_ref, near_ref, sems, ext_sems, near_sems):
    def loads(step, x):
        return plane_copies(u_ref, near_ref, x, near_sems.at[step])

    x_off = 3 * (ctl_ref[0] % 2)
    for step, x in enumerate((x_off, 1, 2, 3 - x_off)):
        for copy in loads(step, x):
            copy.start()

    def before(step, x):
        for copy in loads(step, x):
            copy.wait()

    finish = azimuth_and_on_face(
        ctl_ref, live_ref, jac_ref, first_ref, acc_ref, west_ref, east_ref, on_ext_ref, state_ref,
        out_ref, ext_ref, sems, ext_sems.at[0], 0.5 * STEP,
        lambda v, ap, x, h: 0.5 * near_ref[v, ap, x, h] + 0.5 * first_ref[v, ap, x, h], before=before,
    )
    finish()


def interface_kernel(section, ctl_ref, offset_ref, own_ref, next_ref, weight_ref, *rest):
    out_ref, near_ref = rest[-2:]
    block = ctl_ref[0]

    @pl.when((block == 7) | (block == 8))
    def _():
        rotor = block < 8
        within = lax.rem(offset_ref[section], 128)
        lane = lanes()

        def pick(own, other, amount):
            start = jnp.where(rotor, 128 - amount, 0)
            sent = (lane >= start) & (lane < start + amount)
            turn = lax.rem(jnp.where(rotor, amount, 128 - amount), 128)
            return pltpu.roll(jnp.where(sent, other, own), turn, 1)

        def body(ap, carry):
            place = pl.multiple_of(8 * ap, 8)
            for v in range(VARS):
                for h in range(2):
                    own, other = own_ref[v * 16 + ap, h], next_ref[v * 16 + ap, h]
                    near_ref[2 * v + h, pl.ds(place, 8), :] = pick(own, other, within)
                    near_ref[2 * v + h, pl.ds(place + 128, 8), :] = pick(own, other, within + 1)
            return carry

        lax.fori_loop(0, 16, body, 0, unroll=2)
        w_both = weight_ref[...]
        for v in range(VARS):
            both = jnp.concatenate([near_ref[2 * v], near_ref[2 * v + 1]], axis=1)
            high, low = split_bf16(both)
            first = jnp.dot(w_both, high, preferred_element_type=jnp.float32)
            total = first[:128] + first[128:] + jnp.dot(w_both[:128], low, preferred_element_type=jnp.float32)
            out_ref[2 * v] = total[:, :128]
            out_ref[2 * v + 1] = total[:, 128:]


def off_face(ctl_ref, live_ref, jac_ref, off_ext_ref, state_ref, window_ref, out_ref, cross_ref, sems, scale, done):
    block = ctl_ref[0]
    odd = block % 2
    masks = live_masks(live_ref)
    interface = (block == 7) | (block == 8)

    def loads(part):
        nodes = pl.ds(4 * part, 4)
        return [
            pltpu.make_async_copy(
                state_ref.at[v, nodes, 3 * odd], out_ref.at[pl.ds(16 * v + 4 * part, 4)], sems.at[part, v]
            )
            for v in range(VARS)
        ]

    def cross(part):
        place = pl.ds(32 * part, 32)
        return pltpu.make_async_copy(window_ref.at[:, place], cross_ref.at[:, place], sems.at[part, VARS])

    for part in range(4):
        for copy in loads(part):
            copy.start()

        @pl.when(interface)
        def _(part=part):
            cross(part).start()

    matrix = face_matrix(jac_ref, jnp.where(block < 8, 0, 1), 2, jnp.where(odd == 0, 1.0, -1.0), scale)

    def run(part, load):
        def body(i, carry):
            ap = 4 * part + i
            for h in range(2):
                mixed = mix(matrix, [load(v, ap, h) for v in range(VARS)])
                for v in range(VARS):
                    out_ref[v * 16 + ap, h] += masks[h] * mixed[v]
            return carry

        lax.fori_loop(0, 4, body, 0, unroll=2)

    for part in range(4):
        for copy in loads(part):
            copy.wait()

        @pl.when(interface)
        def _(part=part):
            cross(part).wait()
            run(part, lambda v, ap, h: cross_ref[2 * v + h, pl.ds(pl.multiple_of(8 * ap, 8), 8), :])

        @pl.when(jnp.logical_not(interface))
        def _(part=part):
            run(part, lambda v, ap, h: off_ext_ref[v * 16 + ap, h])

        done(part)


def first_off_kernel(ctl_ref, live_ref, jac_ref, west_ref, east_ref, off_ext_ref, state_ref, window_ref,
                     out_ref, new_west_ref, new_east_ref, cross_ref, sems):
    off_face(ctl_ref, live_ref, jac_ref, off_ext_ref, state_ref, window_ref, out_ref, cross_ref, sems, STEP, lambda part: None)
    new_west_ref[...] = west_ref[...]
    new_east_ref[...] = east_ref[...]
    face_columns(out_ref, 3 * (ctl_ref[0] % 2), new_west_ref, new_east_ref)


def second_off_kernel(ctl_ref, live_ref, jac_ref, off_ext_ref, state_ref, window_ref, out_ref,
                      face_ref, cross_ref, sems):
    x_off = 3 * (ctl_ref[0] % 2)

    def stores(part):
        return [
            pltpu.make_async_copy(
                face_ref.at[pl.ds(16 * v + 4 * part, 4)], out_ref.at[v, pl.ds(4 * part, 4), x_off], sems.at[part, v]
            )
            for v in range(VARS)
        ]

    def done(part):
        for copy in stores(part):
            copy.start()

    off_face(
        ctl_ref, live_ref, jac_ref, off_ext_ref, state_ref, window_ref, face_ref, cross_ref, sems, 0.5 * STEP, done
    )
    for part in range(4):
        for copy in stores(part):
            copy.wait()


def shape(*dims, dtype=jnp.float32):
    return jax.ShapeDtypeStruct(dims, dtype)


def vmem(like):
    return pltpu.VMEM(like.shape, like.dtype)


STATE = shape(VARS, 16, 4, 2, 8, 128)
FACE = shape(80, 2, 8, 128)
COLUMNS = shape(2, 8, 128)
EXPANDED = shape(256, 256, dtype=jnp.bfloat16)
WINDOW = shape(10, 128, 128)
TURN = shape(1, dtype=jnp.int32)
DMA = pltpu.SemaphoreType.DMA


def call(kernel, operands, outs, scratch=(), flops=10**7, aliases=None, moved=None, limit=20):
    if moved is None:
        moved = sum(a.size * a.dtype.itemsize for _, a in operands)
        moved += sum(int(np.prod(o.shape)) * o.dtype.itemsize for _, o in outs)
    return pl.pallas_call(
        kernel,
        in_specs=[m for m, _ in operands],
        out_specs=[m for m, _ in outs],
        out_shape=[o for _, o in outs],
        scratch_shapes=list(scratch),
        input_output_aliases=aliases or {},
        compiler_params=pltpu.CompilerParams(vmem_limit_bytes=limit * 2**20),
        cost_estimate=pl.CostEstimate(flops=flops, bytes_accessed=moved, transcendentals=0),
    )(*[a for _, a in operands])


def send(array, route):
    sectors, layers = lax.axis_size("azim"), lax.axis_size("block")
    pairs = []
    for s in range(sectors):
        for b in range(layers):
            to = route(s, b)
            if to is not None:
                pairs.append((s * layers + b, to[0] * layers + to[1]))
    return lax.ppermute(array, AXES, pairs)


def off_chip(s, b):
    if b in (0, 7, 8, 15):
        return None
    return (s, b + 1 if b % 2 else b - 1)


def off_chip_or_beside(s, b):
    return beside(s, b) or off_chip(s, b)


def on_chip(s, b):
    return (s, b ^ 1)


def eastward(s, b):
    return ((s + 1) % 16, b)


def westward(s, b):
    return ((s - 1) % 16, b)


def across(turns):
    def route(s, b):
        if b == 7:
            return ((s + turns) % 16, 8)
        if b == 8:
            return ((s - turns) % 16, 7)
        return None

    return route


def beside(s, b):
    return {7: ((s + 1) % 16, 7), 8: ((s - 1) % 16, 8)}.get(b)


def cross_interface(panel, turn):
    branches = [lambda panel, turns=turns: send(panel, across(turns)) for turns in range(16)]
    return lax.switch(turn[0], branches, panel)


def extract(ctl, u):
    return call(
        extract_kernel,
        [(SMEM, ctl), (HBM, u)],
        [(VMEM, STATE), (VMEM, FACE), (VMEM, FACE), (VMEM, COLUMNS), (VMEM, COLUMNS)],
        [DMA((4,))],
        limit=49,
    )


def first_axis_span(ctl, jac, offsets, u):
    return call(
        first_axis_span_kernel,
        [(SMEM, ctl), (SMEM, jac), (SMEM, offsets), (VMEM, u)],
        [(VMEM, STATE), (SMEM, TURN), (SMEM, TURN)],
        flops=10**8,
    )


def second_axis_span(ctl, jac, state, off):
    return call(
        second_axis_span_kernel,
        [(SMEM, ctl), (SMEM, jac), (HBM, state), (VMEM, off)],
        [(VMEM, STATE), (VMEM, STATE)],
        [DMA((4,))],
        flops=10**8,
    )


def first_azimuth(ctl, live, jac, u, acc, west, east, weights, on_ext):
    return call(
        first_azimuth_kernel,
        [(SMEM, ctl), (SMEM, live), (SMEM, jac)]
        + [(VMEM, a) for a in (u, acc, west, east, weights)]
        + [(HBM, on_ext)],
        [(HBM, STATE), (VMEM, FACE)]
        + [(VMEM, COLUMNS), (VMEM, COLUMNS), (VMEM, EXPANDED), (VMEM, EXPANDED)],
        [vmem(STATE), vmem(FACE), DMA((4, VARS)), DMA((1,))],
        flops=10**8,
    )


def second_azimuth(ctl, live, jac, first, acc, west, east, u, on_ext, state):
    return call(
        second_azimuth_kernel,
        [(SMEM, ctl), (SMEM, live), (SMEM, jac)]
        + [(VMEM, a) for a in (first, acc, west, east)]
        + [(HBM, u), (HBM, on_ext), (HBM, state)],
        [(HBM, STATE)],
        [vmem(STATE), vmem(FACE), vmem(STATE), DMA((4, VARS)), DMA((1,)), DMA((4, VARS))],
        flops=10**8,
        aliases={9: 0},
        limit=48,
    )[0]


def interpolated(section, ctl, offsets, own, other, expanded, later=()):
    return call(
        functools.partial(interface_kernel, section),
        [(SMEM, ctl), (SMEM, offsets), (VMEM, own), (VMEM, other), (VMEM, expanded)]
        + [(HBM, a) for a in later],
        [(VMEM, WINDOW)],
        [pltpu.VMEM((10, 256, 128), jnp.float32)],
    )[0]


def first_off(ctl, live, jac, west, east, off_ext, state, window):
    return call(
        first_off_kernel,
        [(SMEM, ctl), (SMEM, live), (SMEM, jac), (VMEM, west), (VMEM, east)]
        + [(VMEM, off_ext), (HBM, state), (HBM, window)],
        [(VMEM, FACE), (VMEM, COLUMNS), (VMEM, COLUMNS)],
        [vmem(WINDOW), DMA((4, VARS + 1))],
    )


def second_off(ctl, live, jac, state, off_ext, window):
    return call(
        second_off_kernel,
        [(SMEM, ctl), (SMEM, live), (SMEM, jac), (VMEM, off_ext), (HBM, state), (HBM, window)],
        [(HBM, STATE)],
        [vmem(FACE), vmem(WINDOW), DMA((4, VARS + 1))],
        aliases={4: 0},
    )[0]


def shards(flow_state, jacobians, interp_weights, offsets, live_rows):
    ctl = lax.axis_index("block").astype(jnp.int32).reshape(1)
    jac = jnp.transpose(jacobians, (1, 2, 0, 3))
    u = flow_state.reshape(VARS, 16, 4, 2, 8, 128)
    u_near, off, on, west, east = extract(ctl, u)
    off_ext = send(off, off_chip_or_beside)
    from_west, from_east = send(east, eastward), send(west, westward)
    on_ext = send(on, on_chip)
    acc, turn_0, turn_1 = first_axis_span(ctl, jac, offsets, u_near)
    state, on, west, east, near, later = first_azimuth(
        ctl, live_rows, jac, u_near, acc, from_west, from_east, interp_weights, on_ext
    )
    window = cross_interface(interpolated(0, ctl, offsets, off, off_ext, near, [on]), turn_0)
    off, west, east = first_off(ctl, live_rows, jac, west, east, off_ext, state, window)
    off_ext = send(off, off_chip_or_beside)
    on_ext = send(on, on_chip)
    from_west, from_east = send(east, eastward), send(west, westward)
    first, acc = second_axis_span(ctl, jac, state, off)
    state = second_azimuth(ctl, live_rows, jac, first, acc, from_west, from_east, u, on_ext, state)
    off_ext, state = lax.optimization_barrier((off_ext, state))
    window = cross_interface(interpolated(1, ctl, offsets, off, off_ext, later), turn_1)
    out = second_off(ctl, live_rows, jac, state, off_ext, window)
    return out.reshape(flow_state.shape)


def solution(mesh):
    placed = (P("block", None, None, None, "azim"), P(), P(), P(), P("block"))
    return jax.shard_map(
        shards,
        mesh=mesh,
        in_specs=placed,
        out_specs=P("block", None, None, None, "azim"),
        check_vma=False,
    )
```

```python
import functools

import jax
import jax.numpy as jnp
import numpy as np
from jax import lax
from jax.experimental import pallas as pl
from jax.experimental.pallas import tpu as pltpu
from jax.sharding import PartitionSpec as P

STEP = 0.04
VARS = 5
TILE = (8, 128)
AXES = ("azim", "block")
VMEM = pl.BlockSpec(memory_space=pltpu.VMEM)
HBM = pl.BlockSpec(memory_space=pltpu.HBM)
SMEM = pl.BlockSpec(memory_space=pltpu.SMEM)


def derivative_matrix():
    points = np.array([-1.0, -1.0 / np.sqrt(5.0), 1.0 / np.sqrt(5.0), 1.0])
    differ = points[:, None] - points[None, :]
    filled = differ + np.eye(4)
    weights = 1.0 / np.prod(filled, axis=1)
    matrix = weights[None, :] / weights[:, None] / filled
    matrix = matrix * (1.0 - np.eye(4))
    return matrix - np.eye(4) * matrix.sum(axis=1)[:, None]


DM = derivative_matrix()


def lanes():
    return lax.broadcasted_iota(jnp.int32, TILE, 1)


def rows():
    return lax.broadcasted_iota(jnp.int32, TILE, 0)


def splat_matrix(jac_ref, side, k):
    return [[jnp.full(TILE, jac_ref[k, w, side, v], jnp.float32) for v in range(VARS)] for w in range(VARS)]


def bound_of(matrix):
    sums = [functools.reduce(jnp.add, [jnp.abs(e) for e in row]) for row in matrix]
    return functools.reduce(jnp.maximum, sums)


def face_matrix(jac_ref, side, k, orient, scale):
    matrix = splat_matrix(jac_ref, side, k)
    lam = bound_of(matrix)
    factor = jnp.full(TILE, orient, jnp.float32) * (3.0 * scale)
    return [
        [factor * matrix[w][v] + (3.0 * scale) * lam if w == v else factor * matrix[w][v] for v in range(VARS)]
        for w in range(VARS)
    ]


def mix(matrix, z):
    return [functools.reduce(jnp.add, [matrix[w][v] * z[v] for v in range(VARS)]) for w in range(VARS)]


def live_masks(live_ref):
    live = live_ref[0]
    return [(rows() + 8 * h < live).astype(jnp.float32) for h in range(2)]


def put_columns(lane, j, west_tile, east_tile, west, east):
    return (
        jnp.where(lane == j, pltpu.roll(west_tile, j, 1), west),
        jnp.where(lane == j, pltpu.roll(east_tile, j + 1, 1), east),
    )


def split_bf16(x):
    high = x.astype(jnp.bfloat16)
    return high, (x - high.astype(jnp.float32)).astype(jnp.bfloat16)


def extract_kernel(ctl_ref, state_ref, u_ref, off_ref, on_ref, west_ref, east_ref, sems):
    x_off = 3 * (ctl_ref[0] % 2)
    load = load_parts(state_ref, u_ref, sems, (0, 3, 1, 2))
    for a in (0, 3, 1, 2):
        load(a).wait()
        for p in range(4):
            ap = 4 * a + p
            for v in range(VARS):
                off_ref[v * 16 + ap] = u_ref[v, ap, x_off]
                on_ref[v * 16 + ap] = u_ref[v, ap, 3 - x_off]
        if a == 3:
            middle_columns(lambda v, e, p, x, h: u_ref[v, 12 * e + p, x, h], west_ref, east_ref)
            face_columns(off_ref, x_off, west_ref, east_ref)
            face_columns(on_ref, 3 - x_off, west_ref, east_ref)


def rolled_columns(planes, west_ref, east_ref):
    lane = lanes()
    for h in range(2):

        def body(i, carry, h=h):
            west, east = carry
            v, p = i // 4, i % 4
            for x, tile in planes:
                j = 16 * v + 4 * p + x
                west = jnp.where(lane == j, pltpu.roll(tile(v, 0, p, h), j, 1), west)
                east = jnp.where(lane == j, pltpu.roll(tile(v, 1, p, h), (j + 1) % 128, 1), east)
            return west, east

        zero = jnp.zeros(TILE, jnp.float32)
        west_ref[h], east_ref[h] = lax.fori_loop(0, 20, body, (zero, zero))


def middle_columns(tile, west_ref, east_ref):
    lane = lanes()
    for h in range(2):
        west = jnp.zeros(TILE, jnp.float32)
        east = jnp.zeros(TILE, jnp.float32)
        for v in range(VARS):
            for p in range(4):
                for x in (1, 2):
                    west, east = put_columns(
                        lane, 16 * v + 4 * p + x, tile(v, 0, p, x, h), tile(v, 1, p, x, h), west, east
                    )
        west_ref[h] = west
        east_ref[h] = east


def face_columns(face_ref, x, west_ref, east_ref):
    lane = lanes()
    for h in range(2):
        west, east = west_ref[h], east_ref[h]
        for v in range(VARS):
            for p in range(4):
                west, east = put_columns(
                    lane, 16 * v + 4 * p + x, face_ref[v * 16 + p, h], face_ref[v * 16 + 12 + p, h], west, east
                )
        west_ref[h] = west
        east_ref[h] = east


def derivative_terms(u0, u1, u2, u3):
    even = (u0 + u3) - (u1 + u2)
    o, g = u0 - u3, u1 - u2
    a = float(0.5 * (DM[0, 0] + DM[3, 0]))
    b = float(0.5 * (DM[0, 1] + DM[3, 1]))
    c = float(0.5 * (DM[1, 0] + DM[2, 0]))
    d = float(0.5 * (DM[1, 1] + DM[2, 1]))
    outer = (-a) * o - b * g
    inner = (-c) * o - d * g
    outer_even = float(-0.5 * (DM[0, 0] - DM[3, 0])) * even
    inner_even = float(-0.5 * (DM[1, 0] - DM[2, 0])) * even
    return outer + outer_even, inner + inner_even, inner - inner_even, outer - outer_even


def terms(matrix, lam3, z, jumps):
    outs = []
    for node in range(4):
        mixed = mix(matrix, [z[v][node] for v in range(VARS)])
        if node in jumps:
            mixed = [mixed[v] - lam3 * jumps[node][v] for v in range(VARS)]
        outs.append(mixed)
    return outs


def coefficients(ctl_ref, jac_ref, k, scale):
    matrix = splat_matrix(jac_ref, jnp.where(ctl_ref[0] < 8, 0, 1), k)
    lam3 = bound_of(matrix) * (3.0 * scale)
    return [[scale * e for e in r] for r in matrix], lam3


def interior_axis_span(ctl_ref, jac_ref, u_ref, acc_ref, scale, before):
    row = rows()

    def along_x(matrix, lam3):
        def one_a(a, carry):
            before(a)

            def body(i, carry):
                h, ap = i % 2, 4 * a + i // 2
                z, first, last = [], [], []
                for v in range(VARS):
                    u = [u_ref[v, ap, x, h] for x in range(4)]
                    d = derivative_terms(*u)
                    z.append([d[0] - 3.0 * u[0], d[1], d[2], d[3] + 3.0 * u[3]])
                    first.append(u[0])
                    last.append(u[3])
                outs = terms(matrix, lam3, z, {0: first, 3: last})
                for x in range(4):
                    for v in range(VARS):
                        acc_ref[v, ap, x, h] = outs[x][v]
                return carry

            lax.fori_loop(0, 8, body, 0, unroll=2)
            return carry

        lax.fori_loop(0, 4, one_a, 0)

    def along_p(matrix, lam3):
        def body(i, carry):
            a, x = i // 4, i % 4
            for h in range(2):
                z, jump_l, jump_u = [], [], []
                for v in range(VARS):
                    u = [u_ref[v, 4 * a + p, x, h] for p in range(4)]
                    d = derivative_terms(*u)
                    if h == 0:
                        below = jnp.where(row == 0, u[0], pltpu.roll(u[3], 1, 0))
                        other = u_ref[v, 4 * a, x, 1]
                        above = pltpu.roll(jnp.where(row == 0, other, u[0]), 7, 0)
                    else:
                        other = u_ref[v, 4 * a + 3, x, 0]
                        below = pltpu.roll(jnp.where(row == 7, other, u[3]), 1, 0)
                        above = jnp.where(row == 7, u[3], pltpu.roll(u[0], 7, 0))
                    lower, upper = u[0] - below, u[3] - above
                    z.append([d[0] - 3.0 * lower, d[1], d[2], d[3] + 3.0 * upper])
                    jump_l.append(lower)
                    jump_u.append(upper)
                outs = terms(matrix, lam3, z, {0: jump_l, 3: jump_u})
                for p in range(4):
                    for v in range(VARS):
                        acc_ref[v, 4 * a + p, x, h] += outs[p][v]
            return carry

        lax.fori_loop(0, 16, body, 0, unroll=2)

    along_x(*coefficients(ctl_ref, jac_ref, 2, scale))
    along_p(*coefficients(ctl_ref, jac_ref, 1, scale))


def interior_azimuth(ctl_ref, live_ref, jac_ref, u_ref, acc_ref, west_ref, east_ref, out_ref, scale, base, before, done):
    lane = lanes()
    matrix, lam3 = coefficients(ctl_ref, jac_ref, 0, scale)
    live = live_ref[0]
    x_off = 3 * (ctl_ref[0] % 2)

    def one_x(step, carry):
        x = jnp.where(step == 0, x_off, jnp.where(step == 3, 3 - x_off, step))
        before(step, x)

        def body(i, carry):
            h, p = i % 2, i // 2
            n = 4 * p + x
            mask = (rows() + 8 * h < live).astype(jnp.float32)
            halo_w, halo_e = west_ref[h], east_ref[h]
            z, jump_w, jump_e = [], [], []
            for v in range(VARS):
                u = [u_ref[v, 4 * a + p, x, h] for a in range(4)]
                d = derivative_terms(*u)
                from_w = pltpu.roll(halo_w, (128 - 16 * v - n) % 128, 1)
                from_e = pltpu.roll(halo_e, 127 - 16 * v - n, 1)
                west = u[0] - jnp.where(lane == 0, from_w, pltpu.roll(u[3], 1, 1))
                east = u[3] - jnp.where(lane == 127, from_e, pltpu.roll(u[0], 127, 1))
                z.append([d[0] - 3.0 * west, d[1], d[2], d[3] + 3.0 * east])
                jump_w.append(west)
                jump_e.append(east)
            outs = terms(matrix, lam3, z, {0: jump_w, 3: jump_e})
            for a in range(4):
                for v in range(VARS):
                    ap = 4 * a + p
                    out_ref[v, ap, x, h] = base(v, ap, x, h) + mask * (acc_ref[v, ap, x, h] + outs[a][v])
            return carry

        lax.fori_loop(0, 8, body, 0)
        done(step, x)
        return carry

    lax.fori_loop(0, 4, one_x, 0)


def plane_copies(source, target, x, sems):
    return [pltpu.make_async_copy(source.at[v, :, x], target.at[v, :, x], sems.at[v]) for v in range(VARS)]


def azimuth_and_on_face(ctl_ref, live_ref, jac_ref, u_ref, acc_ref, west_ref, east_ref, on_ext_ref, state_ref,
                        out_ref, ext_ref, sems, ext_sem, scale, base, on_ref=None, before=lambda step, x: None):
    block = ctl_ref[0]
    x_on = 3 - 3 * (block % 2)
    load = pltpu.make_async_copy(on_ext_ref, ext_ref, ext_sem)
    load.start()

    def done(step, x):
        @pl.when(step == 3)
        def _():
            load.wait()
            masks = live_masks(live_ref)
            orient = jnp.where(block % 2 == 0, -1.0, 1.0)
            matrix = face_matrix(jac_ref, jnp.where(block < 8, 0, 1), 2, orient, scale)

            def body(ap, carry):
                for h in range(2):
                    mixed = mix(matrix, [ext_ref[v * 16 + ap, h] for v in range(VARS)])
                    for v in range(VARS):
                        total = out_ref[v, ap, x, h] + masks[h] * mixed[v]
                        out_ref[v, ap, x, h] = total
                        if on_ref is not None:
                            on_ref[v * 16 + ap, h] = total
                return carry

            lax.fori_loop(0, 16, body, 0)

        for copy in plane_copies(out_ref, state_ref, x, sems.at[step]):
            copy.start()

    interior_azimuth(
        ctl_ref, live_ref, jac_ref, u_ref, acc_ref, west_ref, east_ref, out_ref, scale, base, before, done
    )

    def finish():
        for step, x in enumerate((3 - x_on, 1, 2, x_on)):
            for copy in plane_copies(out_ref, state_ref, x, sems.at[step]):
                copy.wait()

    return finish


def load_parts(source, target, sems, order=(0, 1, 2, 3)):
    def load(a):
        part = pl.ds(4 * a, 4)
        return pltpu.make_async_copy(source.at[:, part], target.at[:, part], sems.at[a])

    for a in order:
        load(a).start()
    return load


def first_axis_span_kernel(ctl_ref, jac_ref, offset_ref, u_ref, weight_ref, acc_ref, turn_0_ref, turn_1_ref,
                           near_ref, later_ref):
    block = ctl_ref[0]

    @pl.when((block == 7) | (block == 8))
    def _():
        expanded_weights(block >= 8, weight_ref, (near_ref, later_ref))

    turn_0_ref[0] = lax.shift_right_logical(offset_ref[0], 7)
    turn_1_ref[0] = lax.shift_right_logical(offset_ref[1], 7)
    interior_axis_span(ctl_ref, jac_ref, u_ref, acc_ref, STEP, lambda a: None)


def second_axis_span_kernel(ctl_ref, jac_ref, state_ref, off_ref, first_ref, acc_ref, sems):
    x_off = 3 * (ctl_ref[0] % 2)
    load = load_parts(state_ref, first_ref, sems)

    def before(a):
        load(a).wait()
        for v in range(VARS):
            for p in range(4):
                ap = 4 * a + p
                first_ref[v, ap, x_off] = off_ref[v * 16 + ap]

    interior_axis_span(ctl_ref, jac_ref, first_ref, acc_ref, 0.5 * STEP, before)


def expanded_weights(turn, weight_ref, out_refs):
    parts = []
    for section in range(2):
        for i in range(2):
            high, low = split_bf16(weight_ref[section, i])
            parts += [high.astype(jnp.float32), low.astype(jnp.float32)]
    spread = lax.broadcasted_iota(jnp.int32, (128, 16), 0) // 8 == lax.broadcasted_iota(jnp.int32, (128, 16), 1)
    spread = spread.astype(jnp.bfloat16)

    def dot(a, b, dims):
        return lax.dot_general(
            a.astype(jnp.bfloat16), b.astype(jnp.bfloat16), (dims, ((), ())), preferred_element_type=jnp.float32
        )

    plain = dot(spread, jnp.concatenate(parts, axis=1), ((1,), (0,)))
    turned = dot(spread, jnp.concatenate(parts, axis=0), ((1,), (1,)))
    picked = jnp.where(turn, turned, plain)
    row = lax.broadcasted_iota(jnp.int32, (128, 1024), 0)
    col = lax.broadcasted_iota(jnp.int32, (128, 1024), 1)
    widen = (row == 16 * (col // 128) + (col % 128) // 8).astype(jnp.bfloat16)
    wide = dot(picked, widen, ((1,), (0,)))
    wide = jnp.where(row % 8 == col % 8, wide, 0.0).astype(jnp.bfloat16)
    for section in range(2):
        near_high, near_low, far_high, far_low = [
            wide[:, 128 * (4 * section + k) : 128 * (4 * section + k + 1)] for k in range(4)
        ]
        high = jnp.concatenate([near_high, far_high], axis=1)
        low = jnp.concatenate([near_low, far_low], axis=1)
        out_refs[section][...] = jnp.concatenate([high, low], axis=0)


def first_azimuth_kernel(ctl_ref, live_ref, jac_ref, u_ref, acc_ref, west_ref, east_ref, on_ext_ref,
                         state_ref, on_ref, new_west_ref, new_east_ref, out_ref, ext_ref, sems, ext_sems):
    x_on = 3 - 3 * (ctl_ref[0] % 2)
    finish = azimuth_and_on_face(
        ctl_ref, live_ref, jac_ref, u_ref, acc_ref, west_ref, east_ref, on_ext_ref, state_ref,
        out_ref, ext_ref, sems, ext_sems.at[0], STEP, lambda v, ap, x, h: u_ref[v, ap, x, h], on_ref,
    )
    planes = [(x, lambda v, e, p, h, x=x: out_ref[v, 12 * e + p, x, h]) for x in (1, 2, x_on)]
    rolled_columns(planes, new_west_ref, new_east_ref)
    finish()


def second_azimuth_kernel(ctl_ref, live_ref, jac_ref, first_ref, acc_ref, west_ref, east_ref, u_ref, on_ext_ref,
                          state_ref, out_ref, ext_ref, near_ref, sems, ext_sems, near_sems):
    def loads(step, x):
        return plane_copies(u_ref, near_ref, x, near_sems.at[step])

    x_off = 3 * (ctl_ref[0] % 2)
    for step, x in enumerate((x_off, 1, 2, 3 - x_off)):
        for copy in loads(step, x):
            copy.start()

    def before(step, x):
        for copy in loads(step, x):
            copy.wait()

    finish = azimuth_and_on_face(
        ctl_ref, live_ref, jac_ref, first_ref, acc_ref, west_ref, east_ref, on_ext_ref, state_ref,
        out_ref, ext_ref, sems, ext_sems.at[0], 0.5 * STEP,
        lambda v, ap, x, h: 0.5 * near_ref[v, ap, x, h] + 0.5 * first_ref[v, ap, x, h], before=before,
    )
    finish()


def interface_kernel(section, ctl_ref, offset_ref, own_ref, next_ref, weight_ref, *rest):
    out_ref, near_ref = rest[-2:]
    block = ctl_ref[0]

    @pl.when((block == 7) | (block == 8))
    def _():
        rotor = block < 8
        within = lax.rem(offset_ref[section], 128)
        lane = lanes()

        def pick(own, other, amount):
            start = jnp.where(rotor, 128 - amount, 0)
            sent = (lane >= start) & (lane < start + amount)
            turn = lax.rem(jnp.where(rotor, amount, 128 - amount), 128)
            return pltpu.roll(jnp.where(sent, other, own), turn, 1)

        def body(ap, carry):
            place = pl.multiple_of(8 * ap, 8)
            for v in range(VARS):
                for h in range(2):
                    own, other = own_ref[v * 16 + ap, h], next_ref[v * 16 + ap, h]
                    near_ref[2 * v + h, pl.ds(place, 8), :] = pick(own, other, within)
                    near_ref[2 * v + h, pl.ds(place + 128, 8), :] = pick(own, other, within + 1)
            return carry

        lax.fori_loop(0, 16, body, 0, unroll=2)
        w_both = weight_ref[...]
        for v in range(VARS):
            both = jnp.concatenate([near_ref[2 * v], near_ref[2 * v + 1]], axis=1)
            high, low = split_bf16(both)
            first = jnp.dot(w_both, high, preferred_element_type=jnp.float32)
            total = first[:128] + first[128:] + jnp.dot(w_both[:128], low, preferred_element_type=jnp.float32)
            out_ref[2 * v] = total[:, :128]
            out_ref[2 * v + 1] = total[:, 128:]


def off_face(ctl_ref, live_ref, jac_ref, off_ext_ref, state_ref, window_ref, out_ref, cross_ref, sems, scale, done):
    block = ctl_ref[0]
    odd = block % 2
    masks = live_masks(live_ref)
    interface = (block == 7) | (block == 8)

    def loads(part):
        nodes = pl.ds(4 * part, 4)
        return [
            pltpu.make_async_copy(
                state_ref.at[v, nodes, 3 * odd], out_ref.at[pl.ds(16 * v + 4 * part, 4)], sems.at[part, v]
            )
            for v in range(VARS)
        ]

    def cross(part):
        place = pl.ds(32 * part, 32)
        return pltpu.make_async_copy(window_ref.at[:, place], cross_ref.at[:, place], sems.at[part, VARS])

    for part in range(4):
        for copy in loads(part):
            copy.start()

        @pl.when(interface)
        def _(part=part):
            cross(part).start()

    matrix = face_matrix(jac_ref, jnp.where(block < 8, 0, 1), 2, jnp.where(odd == 0, 1.0, -1.0), scale)

    def run(part, load):
        def body(i, carry):
            ap = 4 * part + i
            for h in range(2):
                mixed = mix(matrix, [load(v, ap, h) for v in range(VARS)])
                for v in range(VARS):
                    out_ref[v * 16 + ap, h] += masks[h] * mixed[v]
            return carry

        lax.fori_loop(0, 4, body, 0, unroll=2)

    for part in range(4):
        for copy in loads(part):
            copy.wait()

        @pl.when(interface)
        def _(part=part):
            cross(part).wait()
            run(part, lambda v, ap, h: cross_ref[2 * v + h, pl.ds(pl.multiple_of(8 * ap, 8), 8), :])

        @pl.when(jnp.logical_not(interface))
        def _(part=part):
            run(part, lambda v, ap, h: off_ext_ref[v * 16 + ap, h])

        done(part)


def first_off_kernel(ctl_ref, live_ref, jac_ref, west_ref, east_ref, off_ext_ref, state_ref, window_ref,
                     out_ref, new_west_ref, new_east_ref, cross_ref, sems):
    off_face(ctl_ref, live_ref, jac_ref, off_ext_ref, state_ref, window_ref, out_ref, cross_ref, sems, STEP, lambda part: None)
    new_west_ref[...] = west_ref[...]
    new_east_ref[...] = east_ref[...]
    face_columns(out_ref, 3 * (ctl_ref[0] % 2), new_west_ref, new_east_ref)


def second_off_kernel(ctl_ref, live_ref, jac_ref, off_ext_ref, state_ref, window_ref, out_ref,
                      face_ref, cross_ref, sems):
    x_off = 3 * (ctl_ref[0] % 2)

    def stores(part):
        return [
            pltpu.make_async_copy(
                face_ref.at[pl.ds(16 * v + 4 * part, 4)], out_ref.at[v, pl.ds(4 * part, 4), x_off], sems.at[part, v]
            )
            for v in range(VARS)
        ]

    def done(part):
        for copy in stores(part):
            copy.start()

    off_face(
        ctl_ref, live_ref, jac_ref, off_ext_ref, state_ref, window_ref, face_ref, cross_ref, sems, 0.5 * STEP, done
    )
    for part in range(4):
        for copy in stores(part):
            copy.wait()


def shape(*dims, dtype=jnp.float32):
    return jax.ShapeDtypeStruct(dims, dtype)


def vmem(like):
    return pltpu.VMEM(like.shape, like.dtype)


STATE = shape(VARS, 16, 4, 2, 8, 128)
FACE = shape(80, 2, 8, 128)
COLUMNS = shape(2, 8, 128)
EXPANDED = shape(256, 256, dtype=jnp.bfloat16)
WINDOW = shape(10, 128, 128)
TURN = shape(1, dtype=jnp.int32)
DMA = pltpu.SemaphoreType.DMA


def call(kernel, operands, outs, scratch=(), flops=10**7, aliases=None, moved=None, limit=20):
    if moved is None:
        moved = sum(a.size * a.dtype.itemsize for _, a in operands)
        moved += sum(int(np.prod(o.shape)) * o.dtype.itemsize for _, o in outs)
    return pl.pallas_call(
        kernel,
        in_specs=[m for m, _ in operands],
        out_specs=[m for m, _ in outs],
        out_shape=[o for _, o in outs],
        scratch_shapes=list(scratch),
        input_output_aliases=aliases or {},
        compiler_params=pltpu.CompilerParams(vmem_limit_bytes=limit * 2**20),
        cost_estimate=pl.CostEstimate(flops=flops, bytes_accessed=moved, transcendentals=0),
    )(*[a for _, a in operands])


def send(array, route):
    sectors, layers = lax.axis_size("azim"), lax.axis_size("block")
    pairs = []
    for s in range(sectors):
        for b in range(layers):
            to = route(s, b)
            if to is not None:
                pairs.append((s * layers + b, to[0] * layers + to[1]))
    return lax.ppermute(array, AXES, pairs)


def off_chip(s, b):
    if b in (0, 7, 8, 15):
        return None
    return (s, b + 1 if b % 2 else b - 1)


def off_chip_or_beside(s, b):
    return beside(s, b) or off_chip(s, b)


def on_chip(s, b):
    return (s, b ^ 1)


def eastward(s, b):
    return ((s + 1) % 16, b)


def westward(s, b):
    return ((s - 1) % 16, b)


def across(turns):
    def route(s, b):
        if b == 7:
            return ((s + turns) % 16, 8)
        if b == 8:
            return ((s - turns) % 16, 7)
        return None

    return route


def beside(s, b):
    return {7: ((s + 1) % 16, 7), 8: ((s - 1) % 16, 8)}.get(b)


def cross_interface(panel, turn, compute, *operands):
    def branch(turns):
        return lambda panel, *operands: (send(panel, across(turns)), *compute(*operands))

    return lax.switch(turn[0], [branch(turns) for turns in range(16)], panel, *operands)


def extract(ctl, u):
    return call(
        extract_kernel,
        [(SMEM, ctl), (HBM, u)],
        [(VMEM, STATE), (VMEM, FACE), (VMEM, FACE), (VMEM, COLUMNS), (VMEM, COLUMNS)],
        [DMA((4,))],
        limit=49,
    )


def first_axis_span(ctl, jac, offsets, u, weights):
    return call(
        first_axis_span_kernel,
        [(SMEM, ctl), (SMEM, jac), (SMEM, offsets), (VMEM, u), (VMEM, weights)],
        [(VMEM, STATE), (SMEM, TURN), (SMEM, TURN), (VMEM, EXPANDED), (VMEM, EXPANDED)],
        flops=10**8,
    )


def second_axis_span(ctl, jac, state, off):
    return call(
        second_axis_span_kernel,
        [(SMEM, ctl), (SMEM, jac), (HBM, state), (VMEM, off)],
        [(VMEM, STATE), (VMEM, STATE)],
        [DMA((4,))],
        flops=10**8,
    )


def first_azimuth(ctl, live, jac, u, acc, west, east, on_ext):
    return call(
        first_azimuth_kernel,
        [(SMEM, ctl), (SMEM, live), (SMEM, jac)]
        + [(VMEM, a) for a in (u, acc, west, east)]
        + [(HBM, on_ext)],
        [(HBM, STATE), (VMEM, FACE), (VMEM, COLUMNS), (VMEM, COLUMNS)],
        [vmem(STATE), vmem(FACE), DMA((4, VARS)), DMA((1,))],
        flops=10**8,
    )


def second_azimuth(ctl, live, jac, first, acc, west, east, u, on_ext):
    return call(
        second_azimuth_kernel,
        [(SMEM, ctl), (SMEM, live), (SMEM, jac)]
        + [(VMEM, a) for a in (first, acc, west, east)]
        + [(HBM, u), (HBM, on_ext)],
        [(HBM, STATE)],
        [vmem(STATE), vmem(FACE), vmem(STATE), DMA((4, VARS)), DMA((1,)), DMA((4, VARS))],
        flops=10**8,
    )


def interpolated(section, ctl, offsets, own, other, expanded, later=()):
    return call(
        functools.partial(interface_kernel, section),
        [(SMEM, ctl), (SMEM, offsets), (VMEM, own), (VMEM, other), (VMEM, expanded)]
        + [(HBM, a) for a in later],
        [(VMEM, WINDOW)],
        [pltpu.VMEM((10, 256, 128), jnp.float32)],
    )[0]


def first_off(ctl, live, jac, west, east, off_ext, state, window):
    return call(
        first_off_kernel,
        [(SMEM, ctl), (SMEM, live), (SMEM, jac), (VMEM, west), (VMEM, east)]
        + [(VMEM, off_ext), (HBM, state), (HBM, window)],
        [(VMEM, FACE), (VMEM, COLUMNS), (VMEM, COLUMNS)],
        [vmem(WINDOW), DMA((4, VARS + 1))],
    )


def second_off(ctl, live, jac, state, off_ext, window):
    return call(
        second_off_kernel,
        [(SMEM, ctl), (SMEM, live), (SMEM, jac), (VMEM, off_ext), (HBM, state), (HBM, window)],
        [(HBM, STATE)],
        [vmem(FACE), vmem(WINDOW), DMA((4, VARS + 1))],
        aliases={4: 0},
        limit=56,
    )[0]


def shards(flow_state, jacobians, interp_weights, offsets, live_rows):
    ctl = lax.axis_index("block").astype(jnp.int32).reshape(1)
    jac = jnp.transpose(jacobians, (1, 2, 0, 3))
    u = flow_state.reshape(VARS, 16, 4, 2, 8, 128)
    u_near, off, on, west, east = extract(ctl, u)
    off_ext = send(off, off_chip_or_beside)
    from_west, from_east = send(east, eastward), send(west, westward)
    on_ext = send(on, on_chip)
    acc, turn_0, turn_1, near, later = first_axis_span(ctl, jac, offsets, u_near, interp_weights)
    panel = interpolated(0, ctl, offsets, off, off_ext, near)
    window, state, on, west, east = cross_interface(
        panel, turn_0, first_azimuth, ctl, live_rows, jac, u_near, acc, from_west, from_east, on_ext
    )
    off, west, east = first_off(ctl, live_rows, jac, west, east, off_ext, state, window)
    off_ext = send(off, off_chip_or_beside)
    from_west, from_east = send(east, eastward), send(west, westward)
    on_ext = send(on, on_chip)
    first, acc = second_axis_span(ctl, jac, state, off)
    panel = interpolated(1, ctl, offsets, off, off_ext, later)
    window, state = cross_interface(
        panel, turn_1, second_azimuth, ctl, live_rows, jac, first, acc, from_west, from_east, u, on_ext
    )
    out = second_off(ctl, live_rows, jac, state, off_ext, window)
    return out.reshape(flow_state.shape)


def solution(mesh):
    placed = (P("block", None, None, None, "azim"), P(), P(), P(), P("block"))
    return jax.shard_map(
        shards,
        mesh=mesh,
        in_specs=placed,
        out_specs=P("block", None, None, None, "azim"),
        check_vma=False,
    )
```

```python
import functools

import jax
import jax.numpy as jnp
import numpy as np
from jax import lax
from jax.experimental import pallas as pl
from jax.experimental.pallas import tpu as pltpu
from jax.sharding import PartitionSpec as P

STEP = 0.04
VARS = 5
TILE = (8, 128)
AXES = ("azim", "block")
VMEM = pl.BlockSpec(memory_space=pltpu.VMEM)
HBM = pl.BlockSpec(memory_space=pltpu.HBM)
SMEM = pl.BlockSpec(memory_space=pltpu.SMEM)


def derivative_matrix():
    points = np.array([-1.0, -1.0 / np.sqrt(5.0), 1.0 / np.sqrt(5.0), 1.0])
    differ = points[:, None] - points[None, :]
    filled = differ + np.eye(4)
    weights = 1.0 / np.prod(filled, axis=1)
    matrix = weights[None, :] / weights[:, None] / filled
    matrix = matrix * (1.0 - np.eye(4))
    return matrix - np.eye(4) * matrix.sum(axis=1)[:, None]


DM = derivative_matrix()


def lanes():
    return lax.broadcasted_iota(jnp.int32, TILE, 1)


def rows():
    return lax.broadcasted_iota(jnp.int32, TILE, 0)


def splat_matrix(jac_ref, side, k):
    return [[jnp.full(TILE, jac_ref[k, w, side, v], jnp.float32) for v in range(VARS)] for w in range(VARS)]


def bound_of(matrix):
    sums = [functools.reduce(jnp.add, [jnp.abs(e) for e in row]) for row in matrix]
    return functools.reduce(jnp.maximum, sums)


def face_matrix(jac_ref, side, k, orient, scale):
    matrix = splat_matrix(jac_ref, side, k)
    lam = bound_of(matrix)
    factor = jnp.full(TILE, orient, jnp.float32) * (3.0 * scale)
    return [
        [factor * matrix[w][v] + (3.0 * scale) * lam if w == v else factor * matrix[w][v] for v in range(VARS)]
        for w in range(VARS)
    ]


def mix(matrix, z):
    return [functools.reduce(jnp.add, [matrix[w][v] * z[v] for v in range(VARS)]) for w in range(VARS)]


def live_masks(live_ref):
    live = live_ref[0]
    return [(rows() + 8 * h < live).astype(jnp.float32) for h in range(2)]


def put_columns(lane, j, west_tile, east_tile, west, east):
    return (
        jnp.where(lane == j, pltpu.roll(west_tile, j, 1), west),
        jnp.where(lane == j, pltpu.roll(east_tile, j + 1, 1), east),
    )


def pack_halves(face_ref, upper_ref, lower_ref):
    low = lanes() < 64

    def body(i, carry):
        first, second = face_ref[i, 0], face_ref[i, 1]
        upper_ref[i] = jnp.where(low, pltpu.roll(first, 64, 1), second)
        lower_ref[i] = jnp.where(low, first, pltpu.roll(second, 64, 1))
        return carry

    lax.fori_loop(0, 80, body, 0, unroll=8)


def split_bf16(x):
    high = x.astype(jnp.bfloat16)
    return high, (x - high.astype(jnp.float32)).astype(jnp.bfloat16)


def extract_kernel(ctl_ref, state_ref, u_ref, off_ref, on_ref, west_ref, east_ref, upper_ref, lower_ref, sems):
    block = ctl_ref[0]
    x_off = 3 * (block % 2)
    load = load_parts(state_ref, u_ref, sems, (0, 3, 1, 2))
    for a in (0, 3, 1, 2):
        load(a).wait()
        for p in range(4):
            ap = 4 * a + p
            for v in range(VARS):
                off_ref[v * 16 + ap] = u_ref[v, ap, x_off]
                on_ref[v * 16 + ap] = u_ref[v, ap, 3 - x_off]
        if a == 3:
            middle_columns(lambda v, e, p, x, h: u_ref[v, 12 * e + p, x, h], west_ref, east_ref)
            face_columns(off_ref, x_off, west_ref, east_ref)
            face_columns(on_ref, 3 - x_off, west_ref, east_ref)

    @pl.when((block == 7) | (block == 8))
    def _():
        pack_halves(off_ref, upper_ref, lower_ref)


def rolled_columns(planes, west_ref, east_ref):
    lane = lanes()
    for h in range(2):

        def body(i, carry, h=h):
            west, east = carry
            v, p = i // 4, i % 4
            for x, tile in planes:
                j = 16 * v + 4 * p + x
                west = jnp.where(lane == j, pltpu.roll(tile(v, 0, p, h), j, 1), west)
                east = jnp.where(lane == j, pltpu.roll(tile(v, 1, p, h), (j + 1) % 128, 1), east)
            return west, east

        zero = jnp.zeros(TILE, jnp.float32)
        west_ref[h], east_ref[h] = lax.fori_loop(0, 20, body, (zero, zero))


def middle_columns(tile, west_ref, east_ref):
    lane = lanes()
    for h in range(2):
        west = jnp.zeros(TILE, jnp.float32)
        east = jnp.zeros(TILE, jnp.float32)
        for v in range(VARS):
            for p in range(4):
                for x in (1, 2):
                    west, east = put_columns(
                        lane, 16 * v + 4 * p + x, tile(v, 0, p, x, h), tile(v, 1, p, x, h), west, east
                    )
        west_ref[h] = west
        east_ref[h] = east


def face_columns(face_ref, x, west_ref, east_ref):
    lane = lanes()
    for h in range(2):
        west, east = west_ref[h], east_ref[h]
        for v in range(VARS):
            for p in range(4):
                west, east = put_columns(
                    lane, 16 * v + 4 * p + x, face_ref[v * 16 + p, h], face_ref[v * 16 + 12 + p, h], west, east
                )
        west_ref[h] = west
        east_ref[h] = east


def derivative_terms(u0, u1, u2, u3):
    even = (u0 + u3) - (u1 + u2)
    o, g = u0 - u3, u1 - u2
    a = float(0.5 * (DM[0, 0] + DM[3, 0]))
    b = float(0.5 * (DM[0, 1] + DM[3, 1]))
    c = float(0.5 * (DM[1, 0] + DM[2, 0]))
    d = float(0.5 * (DM[1, 1] + DM[2, 1]))
    outer = (-a) * o - b * g
    inner = (-c) * o - d * g
    outer_even = float(-0.5 * (DM[0, 0] - DM[3, 0])) * even
    inner_even = float(-0.5 * (DM[1, 0] - DM[2, 0])) * even
    return outer + outer_even, inner + inner_even, inner - inner_even, outer - outer_even


def terms(matrix, lam3, z, jumps):
    outs = []
    for node in range(4):
        mixed = mix(matrix, [z[v][node] for v in range(VARS)])
        if node in jumps:
            mixed = [mixed[v] - lam3 * jumps[node][v] for v in range(VARS)]
        outs.append(mixed)
    return outs


def coefficients(ctl_ref, jac_ref, k, scale):
    matrix = splat_matrix(jac_ref, jnp.where(ctl_ref[0] < 8, 0, 1), k)
    lam3 = bound_of(matrix) * (3.0 * scale)
    return [[scale * e for e in r] for r in matrix], lam3


def interior_axis_span(ctl_ref, jac_ref, u_ref, acc_ref, scale, before):
    row = rows()

    def along_x(matrix, lam3):
        def one_a(a, carry):
            before(a)

            def body(i, carry):
                h, ap = i % 2, 4 * a + i // 2
                z, first, last = [], [], []
                for v in range(VARS):
                    u = [u_ref[v, ap, x, h] for x in range(4)]
                    d = derivative_terms(*u)
                    z.append([d[0] - 3.0 * u[0], d[1], d[2], d[3] + 3.0 * u[3]])
                    first.append(u[0])
                    last.append(u[3])
                outs = terms(matrix, lam3, z, {0: first, 3: last})
                for x in range(4):
                    for v in range(VARS):
                        acc_ref[v, ap, x, h] = outs[x][v]
                return carry

            lax.fori_loop(0, 8, body, 0, unroll=2)
            return carry

        lax.fori_loop(0, 4, one_a, 0)

    def along_p(matrix, lam3):
        def body(i, carry):
            a, x = i // 4, i % 4
            for h in range(2):
                z, jump_l, jump_u = [], [], []
                for v in range(VARS):
                    u = [u_ref[v, 4 * a + p, x, h] for p in range(4)]
                    d = derivative_terms(*u)
                    if h == 0:
                        below = jnp.where(row == 0, u[0], pltpu.roll(u[3], 1, 0))
                        other = u_ref[v, 4 * a, x, 1]
                        above = pltpu.roll(jnp.where(row == 0, other, u[0]), 7, 0)
                    else:
                        other = u_ref[v, 4 * a + 3, x, 0]
                        below = pltpu.roll(jnp.where(row == 7, other, u[3]), 1, 0)
                        above = jnp.where(row == 7, u[3], pltpu.roll(u[0], 7, 0))
                    lower, upper = u[0] - below, u[3] - above
                    z.append([d[0] - 3.0 * lower, d[1], d[2], d[3] + 3.0 * upper])
                    jump_l.append(lower)
                    jump_u.append(upper)
                outs = terms(matrix, lam3, z, {0: jump_l, 3: jump_u})
                for p in range(4):
                    for v in range(VARS):
                        acc_ref[v, 4 * a + p, x, h] += outs[p][v]
            return carry

        lax.fori_loop(0, 16, body, 0, unroll=2)

    along_x(*coefficients(ctl_ref, jac_ref, 2, scale))
    along_p(*coefficients(ctl_ref, jac_ref, 1, scale))


def interior_azimuth(ctl_ref, live_ref, jac_ref, u_ref, acc_ref, west_ref, east_ref, out_ref, scale, base, before, done):
    lane = lanes()
    matrix, lam3 = coefficients(ctl_ref, jac_ref, 0, scale)
    live = live_ref[0]
    x_off = 3 * (ctl_ref[0] % 2)

    def one_x(step, carry):
        x = jnp.where(step == 0, x_off, jnp.where(step == 3, 3 - x_off, step))
        before(step, x)

        def body(i, carry):
            h, p = i % 2, i // 2
            n = 4 * p + x
            mask = (rows() + 8 * h < live).astype(jnp.float32)
            halo_w, halo_e = west_ref[h], east_ref[h]
            z, jump_w, jump_e = [], [], []
            for v in range(VARS):
                u = [u_ref[v, 4 * a + p, x, h] for a in range(4)]
                d = derivative_terms(*u)
                from_w = pltpu.roll(halo_w, (128 - 16 * v - n) % 128, 1)
                from_e = pltpu.roll(halo_e, 127 - 16 * v - n, 1)
                west = u[0] - jnp.where(lane == 0, from_w, pltpu.roll(u[3], 1, 1))
                east = u[3] - jnp.where(lane == 127, from_e, pltpu.roll(u[0], 127, 1))
                z.append([d[0] - 3.0 * west, d[1], d[2], d[3] + 3.0 * east])
                jump_w.append(west)
                jump_e.append(east)
            outs = terms(matrix, lam3, z, {0: jump_w, 3: jump_e})
            for a in range(4):
                for v in range(VARS):
                    ap = 4 * a + p
                    out_ref[v, ap, x, h] = base(v, ap, x, h) + mask * (acc_ref[v, ap, x, h] + outs[a][v])
            return carry

        lax.fori_loop(0, 8, body, 0, unroll=2)
        done(step, x)
        return carry

    lax.fori_loop(0, 4, one_x, 0)


def plane_copies(source, target, x, sems):
    return [pltpu.make_async_copy(source.at[v, :, x], target.at[v, :, x], sems.at[v]) for v in range(VARS)]


def azimuth_and_on_face(ctl_ref, live_ref, jac_ref, u_ref, acc_ref, west_ref, east_ref, on_ext_ref, state_ref,
                        out_ref, ext_ref, sems, ext_sem, scale, base, on_ref=None, before=lambda step, x: None):
    block = ctl_ref[0]
    x_on = 3 - 3 * (block % 2)
    load = pltpu.make_async_copy(on_ext_ref, ext_ref, ext_sem)
    load.start()

    def done(step, x):
        @pl.when(step == 3)
        def _():
            load.wait()
            masks = live_masks(live_ref)
            orient = jnp.where(block % 2 == 0, -1.0, 1.0)
            matrix = face_matrix(jac_ref, jnp.where(block < 8, 0, 1), 2, orient, scale)

            def body(ap, carry):
                for h in range(2):
                    mixed = mix(matrix, [ext_ref[v * 16 + ap, h] for v in range(VARS)])
                    for v in range(VARS):
                        total = out_ref[v, ap, x, h] + masks[h] * mixed[v]
                        out_ref[v, ap, x, h] = total
                        if on_ref is not None:
                            on_ref[v * 16 + ap, h] = total
                return carry

            lax.fori_loop(0, 16, body, 0)

        for copy in plane_copies(out_ref, state_ref, x, sems.at[step]):
            copy.start()

    interior_azimuth(
        ctl_ref, live_ref, jac_ref, u_ref, acc_ref, west_ref, east_ref, out_ref, scale, base, before, done
    )

    def finish():
        for step, x in enumerate((3 - x_on, 1, 2, x_on)):
            for copy in plane_copies(out_ref, state_ref, x, sems.at[step]):
                copy.wait()

    return finish


def load_parts(source, target, sems, order=(0, 1, 2, 3)):
    def load(a):
        part = pl.ds(4 * a, 4)
        return pltpu.make_async_copy(source.at[:, part], target.at[:, part], sems.at[a])

    for a in order:
        load(a).start()
    return load


def prepare_kernel(ctl_ref, offset_ref, weight_ref, turn_0_ref, turn_1_ref, near_ref, later_ref):
    block = ctl_ref[0]
    turn_0_ref[0] = lax.shift_right_logical(offset_ref[0] + 64, 7) & 15
    turn_1_ref[0] = lax.shift_right_logical(offset_ref[1] + 64, 7) & 15

    @pl.when((block == 7) | (block == 8))
    def _():
        expanded_weights(block >= 8, weight_ref, (near_ref, later_ref))


def first_axis_span_kernel(ctl_ref, jac_ref, u_ref, acc_ref):
    interior_axis_span(ctl_ref, jac_ref, u_ref, acc_ref, STEP, lambda a: None)


def second_axis_span_kernel(ctl_ref, jac_ref, state_ref, off_ref, first_ref, acc_ref, sems):
    x_off = 3 * (ctl_ref[0] % 2)
    load = load_parts(state_ref, first_ref, sems)

    def before(a):
        load(a).wait()
        for v in range(VARS):
            for p in range(4):
                ap = 4 * a + p
                first_ref[v, ap, x_off] = off_ref[v * 16 + ap]

    interior_axis_span(ctl_ref, jac_ref, first_ref, acc_ref, 0.5 * STEP, before)


def expanded_weights(turn, weight_ref, out_refs):
    parts = []
    for section in range(2):
        for i in range(2):
            high, low = split_bf16(weight_ref[section, i])
            parts += [high.astype(jnp.float32), low.astype(jnp.float32)]
    spread = lax.broadcasted_iota(jnp.int32, (128, 16), 0) // 8 == lax.broadcasted_iota(jnp.int32, (128, 16), 1)
    spread = spread.astype(jnp.bfloat16)

    def dot(a, b, dims):
        return lax.dot_general(
            a.astype(jnp.bfloat16), b.astype(jnp.bfloat16), (dims, ((), ())), preferred_element_type=jnp.float32
        )

    plain = dot(spread, jnp.concatenate(parts, axis=1), ((1,), (0,)))
    turned = dot(spread, jnp.concatenate(parts, axis=0), ((1,), (1,)))
    picked = jnp.where(turn, turned, plain)
    row = lax.broadcasted_iota(jnp.int32, (128, 1024), 0)
    col = lax.broadcasted_iota(jnp.int32, (128, 1024), 1)
    widen = (row == 16 * (col // 128) + (col % 128) // 8).astype(jnp.bfloat16)
    wide = dot(picked, widen, ((1,), (0,)))
    wide = jnp.where(row % 8 == col % 8, wide, 0.0).astype(jnp.bfloat16)
    for section in range(2):
        near_high, near_low, far_high, far_low = [
            wide[:, 128 * (4 * section + k) : 128 * (4 * section + k + 1)] for k in range(4)
        ]
        high = jnp.concatenate([near_high, far_high], axis=1)
        low = jnp.concatenate([near_low, far_low], axis=1)
        out_refs[section][...] = jnp.concatenate([high, low], axis=0)


def first_azimuth_kernel(ctl_ref, live_ref, jac_ref, u_ref, acc_ref, west_ref, east_ref, on_ext_ref,
                         state_ref, on_ref, new_west_ref, new_east_ref, out_ref, ext_ref, sems, ext_sems):
    x_on = 3 - 3 * (ctl_ref[0] % 2)
    finish = azimuth_and_on_face(
        ctl_ref, live_ref, jac_ref, u_ref, acc_ref, west_ref, east_ref, on_ext_ref, state_ref,
        out_ref, ext_ref, sems, ext_sems.at[0], STEP, lambda v, ap, x, h: u_ref[v, ap, x, h], on_ref,
    )
    planes = [(x, lambda v, e, p, h, x=x: out_ref[v, 12 * e + p, x, h]) for x in (1, 2, x_on)]
    rolled_columns(planes, new_west_ref, new_east_ref)
    finish()


def second_azimuth_kernel(ctl_ref, live_ref, jac_ref, first_ref, acc_ref, west_ref, east_ref, u_ref, on_ext_ref,
                          state_ref, out_ref, ext_ref, near_ref, sems, ext_sems, near_sems):
    def loads(step, x):
        return plane_copies(u_ref, near_ref, x, near_sems.at[step])

    x_off = 3 * (ctl_ref[0] % 2)
    for step, x in enumerate((x_off, 1, 2, 3 - x_off)):
        for copy in loads(step, x):
            copy.start()

    def before(step, x):
        for copy in loads(step, x):
            copy.wait()

    finish = azimuth_and_on_face(
        ctl_ref, live_ref, jac_ref, first_ref, acc_ref, west_ref, east_ref, on_ext_ref, state_ref,
        out_ref, ext_ref, sems, ext_sems.at[0], 0.5 * STEP,
        lambda v, ap, x, h: 0.5 * near_ref[v, ap, x, h] + 0.5 * first_ref[v, ap, x, h], before=before,
    )
    finish()


def interface_kernel(section, ctl_ref, offset_ref, own_ref, upper_ref, lower_ref, weight_ref, out_ref, near_ref):
    block = ctl_ref[0]

    @pl.when((block == 7) | (block == 8))
    def _():
        lane = lanes()
        sign = jnp.where(block == 7, 1, -1)
        within = ((offset_ref[section] + 64) & 127) - 64
        amounts = (sign * within, sign * (within + 1))

        def pick(own, west, east, amount):
            low = jnp.where(amount > 0, 128 - amount, 0)
            high = jnp.where(amount > 0, 128, -amount)
            other = jnp.where(amount > 0, west, east)
            return pltpu.roll(jnp.where((lane >= low) & (lane < high), other, own), amount & 127, 1)

        def body(ap, carry):
            place = pl.multiple_of(8 * ap, 8)
            for v in range(VARS):
                upper, lower = upper_ref[v * 16 + ap], lower_ref[v * 16 + ap]
                wests = (pltpu.roll(upper, 64, 1), upper)
                easts = (lower, pltpu.roll(lower, 64, 1))
                for h in range(2):
                    own = own_ref[v * 16 + ap, h]
                    near_ref[2 * v + h, pl.ds(place, 8), :] = pick(own, wests[h], easts[h], amounts[0])
                    near_ref[2 * v + h, pl.ds(place + 128, 8), :] = pick(own, wests[h], easts[h], amounts[1])
            return carry

        lax.fori_loop(0, 16, body, 0, unroll=2)
        w_both = weight_ref[...]
        for v in range(VARS):
            both = jnp.concatenate([near_ref[2 * v], near_ref[2 * v + 1]], axis=1)
            high, low = split_bf16(both)
            first = jnp.dot(w_both, high, preferred_element_type=jnp.float32)
            total = first[:128] + first[128:] + jnp.dot(w_both[:128], low, preferred_element_type=jnp.float32)
            out_ref[2 * v] = total[:, :128]
            out_ref[2 * v + 1] = total[:, 128:]


def off_face(ctl_ref, live_ref, jac_ref, off_ext_ref, state_ref, window_ref, out_ref, cross_ref, sems, scale, done):
    block = ctl_ref[0]
    odd = block % 2
    masks = live_masks(live_ref)
    interface = (block == 7) | (block == 8)

    def loads(part):
        nodes = pl.ds(4 * part, 4)
        return [
            pltpu.make_async_copy(
                state_ref.at[v, nodes, 3 * odd], out_ref.at[pl.ds(16 * v + 4 * part, 4)], sems.at[part, v]
            )
            for v in range(VARS)
        ]

    def cross(part):
        place = pl.ds(32 * part, 32)
        return pltpu.make_async_copy(window_ref.at[:, place], cross_ref.at[:, place], sems.at[part, VARS])

    for part in range(4):
        for copy in loads(part):
            copy.start()

        @pl.when(interface)
        def _(part=part):
            cross(part).start()

    matrix = face_matrix(jac_ref, jnp.where(block < 8, 0, 1), 2, jnp.where(odd == 0, 1.0, -1.0), scale)

    def run(part, load):
        def body(i, carry):
            ap = 4 * part + i
            for h in range(2):
                mixed = mix(matrix, [load(v, ap, h) for v in range(VARS)])
                for v in range(VARS):
                    out_ref[v * 16 + ap, h] += masks[h] * mixed[v]
            return carry

        lax.fori_loop(0, 4, body, 0, unroll=2)

    for part in range(4):
        for copy in loads(part):
            copy.wait()

        @pl.when(interface)
        def _(part=part):
            cross(part).wait()
            run(part, lambda v, ap, h: cross_ref[2 * v + h, pl.ds(pl.multiple_of(8 * ap, 8), 8), :])

        @pl.when(jnp.logical_not(interface))
        def _(part=part):
            run(part, lambda v, ap, h: off_ext_ref[v * 16 + ap, h])

        done(part)


def first_off_kernel(ctl_ref, live_ref, jac_ref, west_ref, east_ref, off_ext_ref, state_ref, window_ref,
                     out_ref, new_west_ref, new_east_ref, upper_ref, lower_ref, cross_ref, sems):
    off_face(ctl_ref, live_ref, jac_ref, off_ext_ref, state_ref, window_ref, out_ref, cross_ref, sems, STEP, lambda part: None)
    new_west_ref[...] = west_ref[...]
    new_east_ref[...] = east_ref[...]
    face_columns(out_ref, 3 * (ctl_ref[0] % 2), new_west_ref, new_east_ref)

    @pl.when((ctl_ref[0] == 7) | (ctl_ref[0] == 8))
    def _():
        pack_halves(out_ref, upper_ref, lower_ref)


def second_off_kernel(ctl_ref, live_ref, jac_ref, off_ext_ref, state_ref, window_ref, out_ref,
                      face_ref, cross_ref, sems):
    x_off = 3 * (ctl_ref[0] % 2)

    def stores(part):
        return [
            pltpu.make_async_copy(
                face_ref.at[pl.ds(16 * v + 4 * part, 4)], out_ref.at[v, pl.ds(4 * part, 4), x_off], sems.at[part, v]
            )
            for v in range(VARS)
        ]

    def done(part):
        for copy in stores(part):
            copy.start()

    off_face(
        ctl_ref, live_ref, jac_ref, off_ext_ref, state_ref, window_ref, face_ref, cross_ref, sems, 0.5 * STEP, done
    )
    for part in range(4):
        for copy in stores(part):
            copy.wait()


def shape(*dims, dtype=jnp.float32):
    return jax.ShapeDtypeStruct(dims, dtype)


def vmem(like):
    return pltpu.VMEM(like.shape, like.dtype)


STATE = shape(VARS, 16, 4, 2, 8, 128)
FACE = shape(80, 2, 8, 128)
HALF = shape(80, 8, 128)
COLUMNS = shape(2, 8, 128)
EXPANDED = shape(256, 256, dtype=jnp.bfloat16)
WINDOW = shape(10, 128, 128)
TURN = shape(1, dtype=jnp.int32)
DMA = pltpu.SemaphoreType.DMA


def call(kernel, operands, outs, scratch=(), flops=10**7, aliases=None, moved=None, limit=20):
    if moved is None:
        moved = sum(a.size * a.dtype.itemsize for _, a in operands)
        moved += sum(int(np.prod(o.shape)) * o.dtype.itemsize for _, o in outs)
    return pl.pallas_call(
        kernel,
        in_specs=[m for m, _ in operands],
        out_specs=[m for m, _ in outs],
        out_shape=[o for _, o in outs],
        scratch_shapes=list(scratch),
        input_output_aliases=aliases or {},
        compiler_params=pltpu.CompilerParams(vmem_limit_bytes=limit * 2**20),
        cost_estimate=pl.CostEstimate(flops=flops, bytes_accessed=moved, transcendentals=0),
    )(*[a for _, a in operands])


def send(array, route):
    sectors, layers = lax.axis_size("azim"), lax.axis_size("block")
    pairs = []
    for s in range(sectors):
        for b in range(layers):
            to = route(s, b)
            if to is not None:
                pairs.append((s * layers + b, to[0] * layers + to[1]))
    return lax.ppermute(array, AXES, pairs)


def off_chip(s, b):
    if b in (0, 7, 8, 15):
        return None
    return (s, b + 1 if b % 2 else b - 1)


def on_chip(s, b):
    return (s, b ^ 1)


def eastward(s, b):
    return ((s + 1) % 16, b)


def westward(s, b):
    return ((s - 1) % 16, b)


def across(turns):
    def route(s, b):
        if b == 7:
            return ((s + turns) % 16, 8)
        if b == 8:
            return ((s - turns) % 16, 7)
        return None

    return route


def beside_east(s, b):
    return ((s + 1) % 16, b) if b in (7, 8) else None


def beside_west(s, b):
    return ((s - 1) % 16, b) if b in (7, 8) else None


def cross_interface(panel, turn, compute, *operands):
    def branch(turns):
        return lambda panel, *operands: (send(panel, across(turns)), *compute(*operands))

    return lax.switch(turn[0], [branch(turns) for turns in range(16)], panel, *operands)


def extract(ctl, u):
    return call(
        extract_kernel,
        [(SMEM, ctl), (HBM, u)],
        [(VMEM, STATE), (VMEM, FACE), (VMEM, FACE), (VMEM, COLUMNS), (VMEM, COLUMNS), (VMEM, HALF), (VMEM, HALF)],
        [DMA((4,))],
        limit=49,
    )


def prepare(ctl, offsets, weights):
    return call(
        prepare_kernel,
        [(SMEM, ctl), (SMEM, offsets), (VMEM, weights)],
        [(SMEM, TURN), (SMEM, TURN), (VMEM, EXPANDED), (VMEM, EXPANDED)],
    )


def first_axis_span(ctl, jac, u):
    return call(
        first_axis_span_kernel, [(SMEM, ctl), (SMEM, jac), (VMEM, u)], [(VMEM, STATE)], flops=10**8
    )[0]


def second_axis_span(ctl, jac, state, off):
    return call(
        second_axis_span_kernel,
        [(SMEM, ctl), (SMEM, jac), (HBM, state), (VMEM, off)],
        [(VMEM, STATE), (VMEM, STATE)],
        [DMA((4,))],
        flops=10**8,
    )


def first_azimuth(ctl, live, jac, u, acc, west, east, on_ext):
    return call(
        first_azimuth_kernel,
        [(SMEM, ctl), (SMEM, live), (SMEM, jac)]
        + [(VMEM, a) for a in (u, acc, west, east)]
        + [(HBM, on_ext)],
        [(HBM, STATE), (VMEM, FACE), (VMEM, COLUMNS), (VMEM, COLUMNS)],
        [vmem(STATE), vmem(FACE), DMA((4, VARS)), DMA((1,))],
        flops=10**8,
    )


def second_azimuth(ctl, live, jac, first, acc, west, east, u, on_ext):
    return call(
        second_azimuth_kernel,
        [(SMEM, ctl), (SMEM, live), (SMEM, jac)]
        + [(VMEM, a) for a in (first, acc, west, east)]
        + [(HBM, u), (HBM, on_ext)],
        [(HBM, STATE)],
        [vmem(STATE), vmem(FACE), vmem(STATE), DMA((4, VARS)), DMA((1,)), DMA((4, VARS))],
        flops=10**8,
    )


def interpolated(section, ctl, offsets, own, upper, lower, expanded):
    return call(
        functools.partial(interface_kernel, section),
        [(SMEM, ctl), (SMEM, offsets)] + [(VMEM, a) for a in (own, upper, lower, expanded)],
        [(VMEM, WINDOW)],
        [pltpu.VMEM((10, 256, 128), jnp.float32)],
    )[0]


def first_off(ctl, live, jac, west, east, off_ext, state, window):
    return call(
        first_off_kernel,
        [(SMEM, ctl), (SMEM, live), (SMEM, jac), (VMEM, west), (VMEM, east)]
        + [(VMEM, off_ext), (HBM, state), (HBM, window)],
        [(VMEM, FACE), (VMEM, COLUMNS), (VMEM, COLUMNS), (VMEM, HALF), (VMEM, HALF)],
        [vmem(WINDOW), DMA((4, VARS + 1))],
    )


def second_off(ctl, live, jac, state, off_ext, window):
    return call(
        second_off_kernel,
        [(SMEM, ctl), (SMEM, live), (SMEM, jac), (VMEM, off_ext), (HBM, state), (HBM, window)],
        [(HBM, STATE)],
        [vmem(FACE), vmem(WINDOW), DMA((4, VARS + 1))],
        aliases={4: 0},
        limit=54,
    )[0]


def shards(flow_state, jacobians, interp_weights, offsets, live_rows):
    ctl = lax.axis_index("block").astype(jnp.int32).reshape(1)
    jac = jnp.transpose(jacobians, (1, 2, 0, 3))
    u = flow_state.reshape(VARS, 16, 4, 2, 8, 128)
    u_near, off, on, west, east, upper, lower = extract(ctl, u)
    upper, lower = send(upper, beside_east), send(lower, beside_west)
    off_ext = send(off, off_chip)
    from_west, from_east = send(east, eastward), send(west, westward)
    turn_0, turn_1, near, later = prepare(ctl, offsets, interp_weights)
    panel = interpolated(0, ctl, offsets, off, upper, lower, near)

    def first_interior(ctl, live, jac, u, from_west, from_east, on):
        on_ext = send(on, on_chip)
        acc = first_axis_span(ctl, jac, u)
        return first_azimuth(ctl, live, jac, u, acc, from_west, from_east, on_ext)

    window, state, on, west, east = cross_interface(
        panel, turn_0, first_interior, ctl, live_rows, jac, u_near, from_west, from_east, on
    )
    off, west, east, upper, lower = first_off(ctl, live_rows, jac, west, east, off_ext, state, window)
    upper, lower = send(upper, beside_east), send(lower, beside_west)
    off_ext = send(off, off_chip)
    from_west, from_east = send(east, eastward), send(west, westward)
    first, acc = second_axis_span(ctl, jac, state, off)
    panel = interpolated(1, ctl, offsets, off, upper, lower, later)

    def second_interior(ctl, live, jac, first, acc, from_west, from_east, u, on):
        return second_azimuth(ctl, live, jac, first, acc, from_west, from_east, u, send(on, on_chip))

    window, state = cross_interface(
        panel, turn_1, second_interior, ctl, live_rows, jac, first, acc, from_west, from_east, u, on
    )
    out = second_off(ctl, live_rows, jac, state, off_ext, window)
    return out.reshape(flow_state.shape)


def solution(mesh):
    placed = (P("block", None, None, None, "azim"), P(), P(), P(), P("block"))
    return jax.shard_map(
        shards,
        mesh=mesh,
        in_specs=placed,
        out_specs=P("block", None, None, None, "azim"),
        check_vma=False,
    )
```

```python
import functools

import jax
import jax.numpy as jnp
import numpy as np
from jax import lax
from jax.experimental import pallas as pl
from jax.experimental.pallas import tpu as pltpu
from jax.sharding import PartitionSpec as P

STEP = 0.04
VARS = 5
TILE = (8, 128)
AXES = ("azim", "block")
VMEM = pl.BlockSpec(memory_space=pltpu.VMEM)
HBM = pl.BlockSpec(memory_space=pltpu.HBM)
SMEM = pl.BlockSpec(memory_space=pltpu.SMEM)


def derivative_matrix():
    points = np.array([-1.0, -1.0 / np.sqrt(5.0), 1.0 / np.sqrt(5.0), 1.0])
    differ = points[:, None] - points[None, :]
    filled = differ + np.eye(4)
    weights = 1.0 / np.prod(filled, axis=1)
    matrix = weights[None, :] / weights[:, None] / filled
    matrix = matrix * (1.0 - np.eye(4))
    return matrix - np.eye(4) * matrix.sum(axis=1)[:, None]


DM = derivative_matrix()


def lanes():
    return lax.broadcasted_iota(jnp.int32, TILE, 1)


def rows():
    return lax.broadcasted_iota(jnp.int32, TILE, 0)


def splat_matrix(jac_ref, side, k):
    return [[jnp.full(TILE, jac_ref[k, w, side, v], jnp.float32) for v in range(VARS)] for w in range(VARS)]


def bound_of(matrix):
    sums = [functools.reduce(jnp.add, [jnp.abs(e) for e in row]) for row in matrix]
    return functools.reduce(jnp.maximum, sums)


def face_matrix(jac_ref, side, k, orient, scale):
    matrix = splat_matrix(jac_ref, side, k)
    lam = bound_of(matrix)
    factor = jnp.full(TILE, orient, jnp.float32) * (3.0 * scale)
    return [
        [factor * matrix[w][v] + (3.0 * scale) * lam if w == v else factor * matrix[w][v] for v in range(VARS)]
        for w in range(VARS)
    ]


def mix(matrix, z):
    return [functools.reduce(jnp.add, [matrix[w][v] * z[v] for v in range(VARS)]) for w in range(VARS)]


def live_masks(live_ref):
    live = live_ref[0]
    return [(rows() + 8 * h < live).astype(jnp.float32) for h in range(2)]


def put_columns(lane, j, west_tile, east_tile, west, east):
    return (
        jnp.where(lane == j, pltpu.roll(west_tile, j, 1), west),
        jnp.where(lane == j, pltpu.roll(east_tile, j + 1, 1), east),
    )


def split_bf16(x):
    high = x.astype(jnp.bfloat16)
    return high, (x - high.astype(jnp.float32)).astype(jnp.bfloat16)


def extract_kernel(ctl_ref, state_ref, u_ref, off_ref, on_ref, west_ref, east_ref, sems):
    x_off = 3 * (ctl_ref[0] % 2)
    load = load_parts(state_ref, u_ref, sems, (0, 3, 1, 2))
    for a in (0, 3, 1, 2):
        load(a).wait()
        for p in range(4):
            ap = 4 * a + p
            for v in range(VARS):
                off_ref[v * 16 + ap] = u_ref[v, ap, x_off]
                on_ref[v * 16 + ap] = u_ref[v, ap, 3 - x_off]
        if a == 3:
            middle_columns(lambda v, e, p, x, h: u_ref[v, 12 * e + p, x, h], west_ref, east_ref)
            face_columns(off_ref, x_off, west_ref, east_ref)
            face_columns(on_ref, 3 - x_off, west_ref, east_ref)


def rolled_columns(planes, west_ref, east_ref):
    lane = lanes()
    for h in range(2):

        def body(i, carry, h=h):
            west, east = carry
            v, p = i // 4, i % 4
            for x, tile in planes:
                j = 16 * v + 4 * p + x
                west = jnp.where(lane == j, pltpu.roll(tile(v, 0, p, h), j, 1), west)
                east = jnp.where(lane == j, pltpu.roll(tile(v, 1, p, h), (j + 1) % 128, 1), east)
            return west, east

        zero = jnp.zeros(TILE, jnp.float32)
        west_ref[h], east_ref[h] = lax.fori_loop(0, 20, body, (zero, zero))


def middle_columns(tile, west_ref, east_ref):
    lane = lanes()
    for h in range(2):
        west = jnp.zeros(TILE, jnp.float32)
        east = jnp.zeros(TILE, jnp.float32)
        for v in range(VARS):
            for p in range(4):
                for x in (1, 2):
                    west, east = put_columns(
                        lane, 16 * v + 4 * p + x, tile(v, 0, p, x, h), tile(v, 1, p, x, h), west, east
                    )
        west_ref[h] = west
        east_ref[h] = east


def face_columns(face_ref, x, west_ref, east_ref):
    lane = lanes()
    for h in range(2):
        west, east = west_ref[h], east_ref[h]
        for v in range(VARS):
            for p in range(4):
                west, east = put_columns(
                    lane, 16 * v + 4 * p + x, face_ref[v * 16 + p, h], face_ref[v * 16 + 12 + p, h], west, east
                )
        west_ref[h] = west
        east_ref[h] = east


def derivative_terms(u0, u1, u2, u3):
    even = (u0 + u3) - (u1 + u2)
    o, g = u0 - u3, u1 - u2
    a = float(0.5 * (DM[0, 0] + DM[3, 0]))
    b = float(0.5 * (DM[0, 1] + DM[3, 1]))
    c = float(0.5 * (DM[1, 0] + DM[2, 0]))
    d = float(0.5 * (DM[1, 1] + DM[2, 1]))
    outer = (-a) * o - b * g
    inner = (-c) * o - d * g
    outer_even = float(-0.5 * (DM[0, 0] - DM[3, 0])) * even
    inner_even = float(-0.5 * (DM[1, 0] - DM[2, 0])) * even
    return outer + outer_even, inner + inner_even, inner - inner_even, outer - outer_even


def terms(matrix, lam3, z, jumps):
    outs = []
    for node in range(4):
        mixed = mix(matrix, [z[v][node] for v in range(VARS)])
        if node in jumps:
            mixed = [mixed[v] - lam3 * jumps[node][v] for v in range(VARS)]
        outs.append(mixed)
    return outs


def coefficients(ctl_ref, jac_ref, k, scale):
    matrix = splat_matrix(jac_ref, jnp.where(ctl_ref[0] < 8, 0, 1), k)
    lam3 = bound_of(matrix) * (3.0 * scale)
    return [[scale * e for e in r] for r in matrix], lam3


def interior_axis_span(ctl_ref, jac_ref, u_ref, acc_ref, scale, before):
    row = rows()

    def along_x(matrix, lam3):
        def one_a(a, carry):
            before(a)

            def body(i, carry):
                h, ap = i % 2, 4 * a + i // 2
                z, first, last = [], [], []
                for v in range(VARS):
                    u = [u_ref[v, ap, x, h] for x in range(4)]
                    d = derivative_terms(*u)
                    z.append([d[0] - 3.0 * u[0], d[1], d[2], d[3] + 3.0 * u[3]])
                    first.append(u[0])
                    last.append(u[3])
                outs = terms(matrix, lam3, z, {0: first, 3: last})
                for x in range(4):
                    for v in range(VARS):
                        acc_ref[v, ap, x, h] = outs[x][v]
                return carry

            lax.fori_loop(0, 8, body, 0, unroll=2)
            return carry

        lax.fori_loop(0, 4, one_a, 0)

    def along_p(matrix, lam3):
        def body(i, carry):
            a, x = i // 4, i % 4
            for h in range(2):
                z, jump_l, jump_u = [], [], []
                for v in range(VARS):
                    u = [u_ref[v, 4 * a + p, x, h] for p in range(4)]
                    d = derivative_terms(*u)
                    if h == 0:
                        below = jnp.where(row == 0, u[0], pltpu.roll(u[3], 1, 0))
                        other = u_ref[v, 4 * a, x, 1]
                        above = pltpu.roll(jnp.where(row == 0, other, u[0]), 7, 0)
                    else:
                        other = u_ref[v, 4 * a + 3, x, 0]
                        below = pltpu.roll(jnp.where(row == 7, other, u[3]), 1, 0)
                        above = jnp.where(row == 7, u[3], pltpu.roll(u[0], 7, 0))
                    lower, upper = u[0] - below, u[3] - above
                    z.append([d[0] - 3.0 * lower, d[1], d[2], d[3] + 3.0 * upper])
                    jump_l.append(lower)
                    jump_u.append(upper)
                outs = terms(matrix, lam3, z, {0: jump_l, 3: jump_u})
                for p in range(4):
                    for v in range(VARS):
                        acc_ref[v, 4 * a + p, x, h] += outs[p][v]
            return carry

        lax.fori_loop(0, 16, body, 0, unroll=2)

    along_x(*coefficients(ctl_ref, jac_ref, 2, scale))
    along_p(*coefficients(ctl_ref, jac_ref, 1, scale))


def interior_azimuth(ctl_ref, live_ref, jac_ref, u_ref, acc_ref, west_ref, east_ref, out_ref, scale, base, before, done):
    lane = lanes()
    matrix, lam3 = coefficients(ctl_ref, jac_ref, 0, scale)
    live = live_ref[0]
    x_off = 3 * (ctl_ref[0] % 2)

    def one_x(step, carry):
        x = jnp.where(step == 0, x_off, jnp.where(step == 3, 3 - x_off, step))
        before(step, x)

        def body(i, carry):
            h, p = i % 2, i // 2
            n = 4 * p + x
            mask = (rows() + 8 * h < live).astype(jnp.float32)
            halo_w, halo_e = west_ref[h], east_ref[h]
            z, jump_w, jump_e = [], [], []
            for v in range(VARS):
                u = [u_ref[v, 4 * a + p, x, h] for a in range(4)]
                d = derivative_terms(*u)
                from_w = pltpu.roll(halo_w, (128 - 16 * v - n) % 128, 1)
                from_e = pltpu.roll(halo_e, 127 - 16 * v - n, 1)
                west = u[0] - jnp.where(lane == 0, from_w, pltpu.roll(u[3], 1, 1))
                east = u[3] - jnp.where(lane == 127, from_e, pltpu.roll(u[0], 127, 1))
                z.append([d[0] - 3.0 * west, d[1], d[2], d[3] + 3.0 * east])
                jump_w.append(west)
                jump_e.append(east)
            outs = terms(matrix, lam3, z, {0: jump_w, 3: jump_e})
            for a in range(4):
                for v in range(VARS):
                    ap = 4 * a + p
                    out_ref[v, ap, x, h] = base(v, ap, x, h) + mask * (acc_ref[v, ap, x, h] + outs[a][v])
            return carry

        lax.fori_loop(0, 8, body, 0)
        done(step, x)
        return carry

    lax.fori_loop(0, 4, one_x, 0)


def plane_copies(source, target, x, sems):
    return [pltpu.make_async_copy(source.at[v, :, x], target.at[v, :, x], sems.at[v]) for v in range(VARS)]


def azimuth_and_on_face(ctl_ref, live_ref, jac_ref, u_ref, acc_ref, west_ref, east_ref, on_ext_ref, state_ref,
                        out_ref, ext_ref, sems, ext_sem, scale, base, on_ref=None, before=lambda step, x: None):
    block = ctl_ref[0]
    x_on = 3 - 3 * (block % 2)
    load = pltpu.make_async_copy(on_ext_ref, ext_ref, ext_sem)
    load.start()

    def done(step, x):
        @pl.when(step == 3)
        def _():
            load.wait()
            masks = live_masks(live_ref)
            orient = jnp.where(block % 2 == 0, -1.0, 1.0)
            matrix = face_matrix(jac_ref, jnp.where(block < 8, 0, 1), 2, orient, scale)

            def body(ap, carry):
                for h in range(2):
                    mixed = mix(matrix, [ext_ref[v * 16 + ap, h] for v in range(VARS)])
                    for v in range(VARS):
                        total = out_ref[v, ap, x, h] + masks[h] * mixed[v]
                        out_ref[v, ap, x, h] = total
                        if on_ref is not None:
                            on_ref[v * 16 + ap, h] = total
                return carry

            lax.fori_loop(0, 16, body, 0)

        for copy in plane_copies(out_ref, state_ref, x, sems.at[step]):
            copy.start()

    interior_azimuth(
        ctl_ref, live_ref, jac_ref, u_ref, acc_ref, west_ref, east_ref, out_ref, scale, base, before, done
    )

    def finish():
        for step, x in enumerate((3 - x_on, 1, 2, x_on)):
            for copy in plane_copies(out_ref, state_ref, x, sems.at[step]):
                copy.wait()

    return finish


def load_parts(source, target, sems, order=(0, 1, 2, 3)):
    def load(a):
        part = pl.ds(4 * a, 4)
        return pltpu.make_async_copy(source.at[:, part], target.at[:, part], sems.at[a])

    for a in order:
        load(a).start()
    return load


def first_axis_span_kernel(ctl_ref, jac_ref, offset_ref, u_ref, weight_ref, acc_ref, turn_0_ref, turn_1_ref,
                           near_ref, later_ref):
    block = ctl_ref[0]

    @pl.when((block == 7) | (block == 8))
    def _():
        expanded_weights(block >= 8, weight_ref, (near_ref, later_ref))

    turn_0_ref[0] = lax.shift_right_logical(offset_ref[0], 7)
    turn_1_ref[0] = lax.shift_right_logical(offset_ref[1], 7)
    interior_axis_span(ctl_ref, jac_ref, u_ref, acc_ref, STEP, lambda a: None)


def second_axis_span_kernel(ctl_ref, jac_ref, state_ref, off_ref, first_ref, acc_ref, sems):
    x_off = 3 * (ctl_ref[0] % 2)
    load = load_parts(state_ref, first_ref, sems)

    def before(a):
        load(a).wait()
        for v in range(VARS):
            for p in range(4):
                ap = 4 * a + p
                first_ref[v, ap, x_off] = off_ref[v * 16 + ap]

    interior_axis_span(ctl_ref, jac_ref, first_ref, acc_ref, 0.5 * STEP, before)


def expanded_weights(turn, weight_ref, out_refs):
    parts = []
    for section in range(2):
        for i in range(2):
            high, low = split_bf16(weight_ref[section, i])
            parts += [high.astype(jnp.float32), low.astype(jnp.float32)]
    spread = lax.broadcasted_iota(jnp.int32, (128, 16), 0) // 8 == lax.broadcasted_iota(jnp.int32, (128, 16), 1)
    spread = spread.astype(jnp.bfloat16)

    def dot(a, b, dims):
        return lax.dot_general(
            a.astype(jnp.bfloat16), b.astype(jnp.bfloat16), (dims, ((), ())), preferred_element_type=jnp.float32
        )

    plain = dot(spread, jnp.concatenate(parts, axis=1), ((1,), (0,)))
    turned = dot(spread, jnp.concatenate(parts, axis=0), ((1,), (1,)))
    picked = jnp.where(turn, turned, plain)
    row = lax.broadcasted_iota(jnp.int32, (128, 1024), 0)
    col = lax.broadcasted_iota(jnp.int32, (128, 1024), 1)
    widen = (row == 16 * (col // 128) + (col % 128) // 8).astype(jnp.bfloat16)
    wide = dot(picked, widen, ((1,), (0,)))
    wide = jnp.where(row % 8 == col % 8, wide, 0.0).astype(jnp.bfloat16)
    for section in range(2):
        near_high, near_low, far_high, far_low = [
            wide[:, 128 * (4 * section + k) : 128 * (4 * section + k + 1)] for k in range(4)
        ]
        high = jnp.concatenate([near_high, far_high], axis=1)
        low = jnp.concatenate([near_low, far_low], axis=1)
        out_refs[section][...] = jnp.concatenate([high, low], axis=0)


def first_azimuth_kernel(ctl_ref, live_ref, jac_ref, u_ref, acc_ref, west_ref, east_ref, on_ext_ref,
                         state_ref, on_ref, new_west_ref, new_east_ref, out_ref, ext_ref, sems, ext_sems):
    x_on = 3 - 3 * (ctl_ref[0] % 2)
    finish = azimuth_and_on_face(
        ctl_ref, live_ref, jac_ref, u_ref, acc_ref, west_ref, east_ref, on_ext_ref, state_ref,
        out_ref, ext_ref, sems, ext_sems.at[0], STEP, lambda v, ap, x, h: u_ref[v, ap, x, h], on_ref,
    )
    planes = [(x, lambda v, e, p, h, x=x: out_ref[v, 12 * e + p, x, h]) for x in (1, 2, x_on)]
    rolled_columns(planes, new_west_ref, new_east_ref)
    finish()


def second_azimuth_kernel(ctl_ref, live_ref, jac_ref, first_ref, acc_ref, west_ref, east_ref, u_ref, on_ext_ref,
                          state_ref, out_ref, ext_ref, near_ref, sems, ext_sems, near_sems):
    def loads(step, x):
        return plane_copies(u_ref, near_ref, x, near_sems.at[step])

    x_off = 3 * (ctl_ref[0] % 2)
    for step, x in enumerate((x_off, 1, 2, 3 - x_off)):
        for copy in loads(step, x):
            copy.start()

    def before(step, x):
        for copy in loads(step, x):
            copy.wait()

    finish = azimuth_and_on_face(
        ctl_ref, live_ref, jac_ref, first_ref, acc_ref, west_ref, east_ref, on_ext_ref, state_ref,
        out_ref, ext_ref, sems, ext_sems.at[0], 0.5 * STEP,
        lambda v, ap, x, h: 0.5 * near_ref[v, ap, x, h] + 0.5 * first_ref[v, ap, x, h], before=before,
    )
    finish()


def interface_kernel(section, ctl_ref, offset_ref, own_ref, next_ref, weight_ref, *rest):
    out_ref, near_ref = rest[-2:]
    block = ctl_ref[0]

    @pl.when((block == 7) | (block == 8))
    def _():
        rotor = block < 8
        within = lax.rem(offset_ref[section], 128)
        lane = lanes()

        def pick(own, other, amount):
            start = jnp.where(rotor, 128 - amount, 0)
            sent = (lane >= start) & (lane < start + amount)
            turn = lax.rem(jnp.where(rotor, amount, 128 - amount), 128)
            return pltpu.roll(jnp.where(sent, other, own), turn, 1)

        def body(ap, carry):
            place = pl.multiple_of(8 * ap, 8)
            for v in range(VARS):
                for h in range(2):
                    own, other = own_ref[v * 16 + ap, h], next_ref[v * 16 + ap, h]
                    near_ref[2 * v + h, pl.ds(place, 8), :] = pick(own, other, within)
                    near_ref[2 * v + h, pl.ds(place + 128, 8), :] = pick(own, other, within + 1)
            return carry

        lax.fori_loop(0, 16, body, 0, unroll=2)
        w_both = weight_ref[...]
        for v in range(VARS):
            both = jnp.concatenate([near_ref[2 * v], near_ref[2 * v + 1]], axis=1)
            high, low = split_bf16(both)
            first = jnp.dot(w_both, high, preferred_element_type=jnp.float32)
            total = first[:128] + first[128:] + jnp.dot(w_both[:128], low, preferred_element_type=jnp.float32)
            out_ref[2 * v] = total[:, :128]
            out_ref[2 * v + 1] = total[:, 128:]


def off_face(ctl_ref, live_ref, jac_ref, off_ext_ref, state_ref, window_ref, out_ref, cross_ref, sems, scale, done):
    block = ctl_ref[0]
    odd = block % 2
    masks = live_masks(live_ref)
    interface = (block == 7) | (block == 8)

    def loads(part):
        nodes = pl.ds(4 * part, 4)
        return [
            pltpu.make_async_copy(
                state_ref.at[v, nodes, 3 * odd], out_ref.at[pl.ds(16 * v + 4 * part, 4)], sems.at[part, v]
            )
            for v in range(VARS)
        ]

    def cross(part):
        place = pl.ds(32 * part, 32)
        return pltpu.make_async_copy(window_ref.at[:, place], cross_ref.at[:, place], sems.at[part, VARS])

    for part in range(4):
        for copy in loads(part):
            copy.start()

        @pl.when(interface)
        def _(part=part):
            cross(part).start()

    matrix = face_matrix(jac_ref, jnp.where(block < 8, 0, 1), 2, jnp.where(odd == 0, 1.0, -1.0), scale)

    def run(part, load):
        def body(i, carry):
            ap = 4 * part + i
            for h in range(2):
                mixed = mix(matrix, [load(v, ap, h) for v in range(VARS)])
                for v in range(VARS):
                    out_ref[v * 16 + ap, h] += masks[h] * mixed[v]
            return carry

        lax.fori_loop(0, 4, body, 0, unroll=2)

    for part in range(4):
        for copy in loads(part):
            copy.wait()

        @pl.when(interface)
        def _(part=part):
            cross(part).wait()
            run(part, lambda v, ap, h: cross_ref[2 * v + h, pl.ds(pl.multiple_of(8 * ap, 8), 8), :])

        @pl.when(jnp.logical_not(interface))
        def _(part=part):
            run(part, lambda v, ap, h: off_ext_ref[v * 16 + ap, h])

        done(part)


def first_off_kernel(ctl_ref, live_ref, jac_ref, west_ref, east_ref, off_ext_ref, state_ref, window_ref,
                     out_ref, new_west_ref, new_east_ref, cross_ref, sems):
    off_face(ctl_ref, live_ref, jac_ref, off_ext_ref, state_ref, window_ref, out_ref, cross_ref, sems, STEP, lambda part: None)
    new_west_ref[...] = west_ref[...]
    new_east_ref[...] = east_ref[...]
    face_columns(out_ref, 3 * (ctl_ref[0] % 2), new_west_ref, new_east_ref)


def second_off_kernel(ctl_ref, live_ref, jac_ref, off_ext_ref, state_ref, window_ref, out_ref,
                      face_ref, cross_ref, sems):
    x_off = 3 * (ctl_ref[0] % 2)

    def stores(part):
        return [
            pltpu.make_async_copy(
                face_ref.at[pl.ds(16 * v + 4 * part, 4)], out_ref.at[v, pl.ds(4 * part, 4), x_off], sems.at[part, v]
            )
            for v in range(VARS)
        ]

    def done(part):
        for copy in stores(part):
            copy.start()

    off_face(
        ctl_ref, live_ref, jac_ref, off_ext_ref, state_ref, window_ref, face_ref, cross_ref, sems, 0.5 * STEP, done
    )
    for part in range(4):
        for copy in stores(part):
            copy.wait()


def shape(*dims, dtype=jnp.float32):
    return jax.ShapeDtypeStruct(dims, dtype)


def vmem(like):
    return pltpu.VMEM(like.shape, like.dtype)


STATE = shape(VARS, 16, 4, 2, 8, 128)
FACE = shape(80, 2, 8, 128)
COLUMNS = shape(2, 8, 128)
EXPANDED = shape(256, 256, dtype=jnp.bfloat16)
WINDOW = shape(10, 128, 128)
TURN = shape(1, dtype=jnp.int32)
DMA = pltpu.SemaphoreType.DMA


def call(kernel, operands, outs, scratch=(), flops=10**7, aliases=None, moved=None, limit=20):
    if moved is None:
        moved = sum(a.size * a.dtype.itemsize for _, a in operands)
        moved += sum(int(np.prod(o.shape)) * o.dtype.itemsize for _, o in outs)
    return pl.pallas_call(
        kernel,
        in_specs=[m for m, _ in operands],
        out_specs=[m for m, _ in outs],
        out_shape=[o for _, o in outs],
        scratch_shapes=list(scratch),
        input_output_aliases=aliases or {},
        compiler_params=pltpu.CompilerParams(vmem_limit_bytes=limit * 2**20),
        cost_estimate=pl.CostEstimate(flops=flops, bytes_accessed=moved, transcendentals=0),
    )(*[a for _, a in operands])


def send(array, route):
    sectors, layers = lax.axis_size("azim"), lax.axis_size("block")
    pairs = []
    for s in range(sectors):
        for b in range(layers):
            to = route(s, b)
            if to is not None:
                pairs.append((s * layers + b, to[0] * layers + to[1]))
    return lax.ppermute(array, AXES, pairs)


def off_chip(s, b):
    if b in (0, 7, 8, 15):
        return None
    return (s, b + 1 if b % 2 else b - 1)


def off_chip_or_beside(s, b):
    return beside(s, b) or off_chip(s, b)


def on_chip(s, b):
    return (s, b ^ 1)


def eastward(s, b):
    return ((s + 1) % 16, b)


def westward(s, b):
    return ((s - 1) % 16, b)


def across(turns):
    def route(s, b):
        if b == 7:
            return ((s + turns) % 16, 8)
        if b == 8:
            return ((s - turns) % 16, 7)
        return None

    return route


def beside(s, b):
    return {7: ((s + 1) % 16, 7), 8: ((s - 1) % 16, 8)}.get(b)


def cross_interface(panel, turn, compute, *operands):
    def branch(turns):
        return lambda panel, *operands: (send(panel, across(turns)), *compute(*operands))

    return lax.switch(turn[0], [branch(turns) for turns in range(16)], panel, *operands)


def extract(ctl, u):
    return call(
        extract_kernel,
        [(SMEM, ctl), (HBM, u)],
        [(VMEM, STATE), (VMEM, FACE), (VMEM, FACE), (VMEM, COLUMNS), (VMEM, COLUMNS)],
        [DMA((4,))],
        limit=49,
    )


def first_axis_span(ctl, jac, offsets, u, weights):
    return call(
        first_axis_span_kernel,
        [(SMEM, ctl), (SMEM, jac), (SMEM, offsets), (VMEM, u), (VMEM, weights)],
        [(VMEM, STATE), (SMEM, TURN), (SMEM, TURN), (VMEM, EXPANDED), (VMEM, EXPANDED)],
        flops=10**8,
    )


def second_axis_span(ctl, jac, state, off):
    return call(
        second_axis_span_kernel,
        [(SMEM, ctl), (SMEM, jac), (HBM, state), (VMEM, off)],
        [(VMEM, STATE), (VMEM, STATE)],
        [DMA((4,))],
        flops=10**8,
    )


def first_azimuth(ctl, live, jac, u, acc, west, east, on_ext):
    return call(
        first_azimuth_kernel,
        [(SMEM, ctl), (SMEM, live), (SMEM, jac)]
        + [(VMEM, a) for a in (u, acc, west, east)]
        + [(HBM, on_ext)],
        [(HBM, STATE), (VMEM, FACE), (VMEM, COLUMNS), (VMEM, COLUMNS)],
        [vmem(STATE), vmem(FACE), DMA((4, VARS)), DMA((1,))],
        flops=10**8,
    )


def second_azimuth(ctl, live, jac, first, acc, west, east, u, on_ext):
    return call(
        second_azimuth_kernel,
        [(SMEM, ctl), (SMEM, live), (SMEM, jac)]
        + [(VMEM, a) for a in (first, acc, west, east)]
        + [(HBM, u), (HBM, on_ext)],
        [(HBM, STATE)],
        [vmem(STATE), vmem(FACE), vmem(STATE), DMA((4, VARS)), DMA((1,)), DMA((4, VARS))],
        flops=10**8,
    )


def interpolated(section, ctl, offsets, own, other, expanded, later=()):
    return call(
        functools.partial(interface_kernel, section),
        [(SMEM, ctl), (SMEM, offsets), (VMEM, own), (VMEM, other), (VMEM, expanded)]
        + [(HBM, a) for a in later],
        [(VMEM, WINDOW)],
        [pltpu.VMEM((10, 256, 128), jnp.float32)],
    )[0]


def first_off(ctl, live, jac, west, east, off_ext, state, window):
    return call(
        first_off_kernel,
        [(SMEM, ctl), (SMEM, live), (SMEM, jac), (VMEM, west), (VMEM, east)]
        + [(VMEM, off_ext), (HBM, state), (HBM, window)],
        [(VMEM, FACE), (VMEM, COLUMNS), (VMEM, COLUMNS)],
        [vmem(WINDOW), DMA((4, VARS + 1))],
    )


def second_off(ctl, live, jac, state, off_ext, window):
    return call(
        second_off_kernel,
        [(SMEM, ctl), (SMEM, live), (SMEM, jac), (VMEM, off_ext), (HBM, state), (HBM, window)],
        [(HBM, STATE)],
        [vmem(FACE), vmem(WINDOW), DMA((4, VARS + 1))],
        aliases={4: 0},
        limit=56,
    )[0]


def with_on_chip(compute):
    return lambda *operands: compute(*operands[:-1], send(operands[-1], on_chip))


def shards(flow_state, jacobians, interp_weights, offsets, live_rows):
    ctl = lax.axis_index("block").astype(jnp.int32).reshape(1)
    jac = jnp.transpose(jacobians, (1, 2, 0, 3))
    u = flow_state.reshape(VARS, 16, 4, 2, 8, 128)
    u_near, off, on, west, east = extract(ctl, u)
    off_ext = send(off, off_chip_or_beside)
    from_west, from_east = send(east, eastward), send(west, westward)
    acc, turn_0, turn_1, near, later = first_axis_span(ctl, jac, offsets, u_near, interp_weights)
    panel = interpolated(0, ctl, offsets, off, off_ext, near)
    window, state, on, west, east = cross_interface(
        panel, turn_0, with_on_chip(first_azimuth), ctl, live_rows, jac, u_near, acc, from_west, from_east, on
    )
    off, west, east = first_off(ctl, live_rows, jac, west, east, off_ext, state, window)
    off_ext = send(off, off_chip_or_beside)
    from_west, from_east = send(east, eastward), send(west, westward)
    first, acc = second_axis_span(ctl, jac, state, off)
    panel = interpolated(1, ctl, offsets, off, off_ext, later)
    window, state = cross_interface(
        panel, turn_1, with_on_chip(second_azimuth), ctl, live_rows, jac, first, acc, from_west, from_east, u, on
    )
    out = second_off(ctl, live_rows, jac, state, off_ext, window)
    return out.reshape(flow_state.shape)


def solution(mesh):
    placed = (P("block", None, None, None, "azim"), P(), P(), P(), P("block"))
    return jax.shard_map(
        shards,
        mesh=mesh,
        in_specs=placed,
        out_specs=P("block", None, None, None, "azim"),
        check_vma=False,
    )
```
